32 devices in a mesh: gy: 8 (over y, x, core), gz: 4 (over z).
Axes of the slice: x: 2, y: 2, z: 4, core: 2. Of those that a mesh axis runs over, the one named last changes fastest.
Arguments:
- volume: float32 [160, 8, 4096], P('gz', 'gy'), may hold values from -6 to 6
- x_offsets: int32 [160], replicated, may hold values from -64 to 64, as said below
- x_fracs: float32 [160], replicated, may hold values from 0 to 1
- z_offsets: int32 [8], P('gy'), may hold values from -4 to 4, as said below
- z_fracs: float32 [8], P('gy'), may hold values from 0 to 1
- y_offsets: int32 [4096], P('gy'), may hold values from -2 to 2, as said below
- y_fracs: float32 [4096], P('gy'), may hold values from 0 to 1
- slopes: int32 [8], replicated, may hold values from -4 to 4, as said below
Outputs:
- rotated: float32 [160, 8, 4096], P('gz', 'gy')
- projections: float32 [8, 4096, 8], P('gz', 'gy')
The draws below stay inside these ranges and needn't reach their ends.
Inputs may be any that keep to these rules, and one draw needn't show every extreme that they name: `x_offsets`: each value between -64 and 64, both ends taken by some plane. `z_offsets`: each value between -4 and 4, both ends taken by some row. `y_offsets`: each value between -2 and 2, both ends taken by some column. `slopes`: each value between -4 and 4, both ends taken by some tilt.
All inputs are finite; a program needn't handle non-finite values.
Results may differ from the reference program's by a relative error of at most 0.0003.
Values sent between devices are 32-bit elements; how exact they have to be, the bound alone decides.
No kernel may reach another device: no remote copies, remote signals or barrier semaphores. Data moves between devices by JAX's collectives and lax.ppermute only.
A program may use at most 64 MiB of HBM per device.

```python
import jax
import jax.numpy as jnp
from jax import lax

X = 4096
TAPS = 64
OFFX = 64
OFFZ = 4
TILTS = 8
SLOPE = 4
NY = 8
NZ = 160
OFFY = 2


def bounded_offsets(key, count_total, reach):
    values = jax.random.randint(key, (count_total,), -reach, reach + 1)
    places = jax.random.permutation(jax.random.fold_in(key, 7), count_total)
    values = values.at[places[0]].set(-reach)
    values = values.at[places[1]].set(reach)
    return values.astype(jnp.int32)


def draw_x_offsets(key, part):
    return bounded_offsets(jax.random.fold_in(key, 11), NZ, OFFX)


def draw_z_offsets(key, part):
    return bounded_offsets(jax.random.fold_in(key, 13), NY, OFFZ)


def draw_y_offsets(key, part):
    return bounded_offsets(jax.random.fold_in(key, 17), X, OFFY)


def draw_slopes(key, part):
    return bounded_offsets(jax.random.fold_in(key, 19), TILTS, SLOPE)


def level_of(own_key, extent, shards, smallest, top_value):
    level, own = 1.0, jax.random.fold_in(own_key, 6)
    for position, blocks in shards:
        draws = jnp.exp(jax.random.uniform(jax.random.fold_in(own, position), (blocks,), jnp.float32, smallest / len(shards), top_value / len(shards)))
        level = level * jnp.repeat(draws, extent[position] // blocks).reshape([-1 if axis == position else 1 for axis in range(len(extent))])
    return level


def normal_values(key, dims, scale, most, pieces=(), held_as=jnp.bfloat16):
    entries = scale * jax.random.normal(key, dims, jnp.float32)
    if pieces:
        entries = entries * level_of(key, dims, pieces, -0.22, 0.18)
    return jnp.clip(entries, -most, most).astype(held_as)


def setup_inputs(seed: int = 0) -> dict:
    arg_keys = jax.random.split(jax.random.key(seed), 9)
    return {
        "volume": normal_values(arg_keys[0], (NZ, NY, X), 1.0, 6.0, ((0, 4), (1, 8)), jnp.float32),
        "x_offsets": draw_x_offsets(jax.random.fold_in(arg_keys[8], 71), 0),
        "x_fracs": jnp.clip(jax.random.uniform(arg_keys[2], (NZ,), jnp.float32, 0.0, 1.0), 0.0, 1.0),
        "z_offsets": draw_z_offsets(jax.random.fold_in(arg_keys[8], 71), 0),
        "z_fracs": jnp.clip(1.0 * jax.random.uniform(arg_keys[4], (NY,), jnp.float32) ** level_of(arg_keys[4], (NY,), ((0, 8),), -0.2, 0.2), 0.0, 1.0),
        "y_offsets": draw_y_offsets(jax.random.fold_in(arg_keys[8], 71), 0),
        "y_fracs": jnp.clip(1.0 * jax.random.uniform(arg_keys[6], (X,), jnp.float32) ** level_of(arg_keys[6], (X,), ((0, 8),), -0.2, 0.2), 0.0, 1.0),
        "slopes": draw_slopes(jax.random.fold_in(arg_keys[8], 71), 0),
    }


def tap_weight(offset, fraction):
    moved = offset.astype(jnp.float32) - fraction
    inside = (offset >= 1 - TAPS // 2) & (offset <= TAPS // 2)
    value = jnp.sinc(moved) * (0.5 + 0.5 * jnp.cos(jnp.pi * moved / (TAPS // 2 + 1)))
    return jnp.where(inside, value, jnp.zeros_like(value))


def shift_lines(lines, shifts, fractions, margin):
    length = lines.shape[1]
    padded = jnp.pad(lines, ((0, 0), (margin, margin)))
    starts = (margin + shifts - (TAPS // 2 - 1)).astype(jnp.int32)
    spans = jax.vmap(lambda one_row, first_index: lax.dynamic_slice_in_dim(one_row, first_index, length + TAPS - 1))(padded, starts)
    offsets = (jnp.arange(TAPS) - (TAPS // 2 - 1)).astype(jnp.int32)
    weights = tap_weight(offsets[None, :], fractions[:, None])
    result = jnp.zeros(lines.shape, jnp.float32)
    for tap_index in range(TAPS):
        result = result + weights[:, tap_index:tap_index + 1] * spans[:, tap_index:tap_index + length]
    return result


def reference(volume, x_offsets, x_fracs, z_offsets, z_fracs, y_offsets, y_fracs, slopes):
    def shear_plane(items):
        plane, shift_value, frac_value = items
        return shift_lines(plane, jnp.full((NY,), shift_value), jnp.full((NY,), frac_value), OFFX + TAPS)

    sheared_x = lax.map(shear_plane, (volume, x_offsets, x_fracs))

    def shear_row(row_index):
        slab = lax.dynamic_index_in_dim(sheared_x, row_index, 1, keepdims=False)
        shift_value = lax.dynamic_index_in_dim(z_offsets, row_index, 0, keepdims=False)
        frac_value = lax.dynamic_index_in_dim(z_fracs, row_index, 0, keepdims=False)
        moved = shift_lines(slab.T, jnp.full((X,), shift_value), jnp.full((X,), frac_value), OFFZ + TAPS)
        return moved.T

    sheared_z = lax.map(shear_row, jnp.arange(NY, dtype=jnp.int32))
    span_pad = NY // 4

    def step_plane(totals, plane_index):
        plane = lax.dynamic_index_in_dim(sheared_z, plane_index, 1, keepdims=False)
        turned = shift_lines(plane.T, y_offsets, y_fracs, OFFY + TAPS)
        lifts = (slopes * (2 * plane_index - NZ) * NY) // (16 * NZ)
        padded = jnp.pad(turned, ((0, 0), (span_pad, span_pad)))
        moved = jax.vmap(lambda lift_one: lax.dynamic_slice_in_dim(padded, (span_pad + lift_one).astype(jnp.int32), NY, 1))(lifts)
        return totals + moved, turned.T

    start_totals = jnp.zeros((TILTS, X, NY), jnp.float32)
    totals, rotated = lax.scan(step_plane, start_totals, jnp.arange(NZ, dtype=jnp.int32))
    projections = totals * (NZ ** -0.5)
    return rotated, projections
```

```python
import functools

import jax
import jax.numpy as jnp
from jax import lax
from jax.experimental import pallas as pl
from jax.experimental.pallas import tpu as pltpu
from jax.sharding import PartitionSpec as P

TAPS = 64
OFFX = 64
OFFZ = 4
LANES = 128
BELOW = TAPS // 2 - 1
VMEM_LIMIT = 48 * 1024 * 1024

SMEM_SPEC = pl.BlockSpec(memory_space=pltpu.SMEM)
VMEM_SPEC = pl.BlockSpec(memory_space=pltpu.VMEM)


def tap_weight(offset, fraction):
    moved = offset.astype(jnp.float32) - fraction
    inside = (offset >= 1 - TAPS // 2) & (offset <= TAPS // 2)
    value = jnp.sinc(moved) * (0.5 + 0.5 * jnp.cos(jnp.pi * moved / (TAPS // 2 + 1)))
    return jnp.where(inside, value, jnp.zeros_like(value))


def tap_weight_in_kernel(offset, fraction):
    moved = offset.astype(jnp.float32) - fraction
    inside = (offset >= 1 - TAPS // 2) & (offset <= TAPS // 2)
    angle = jnp.pi * moved
    at_zero = moved == 0.0
    sinc = jnp.where(at_zero, 1.0, jnp.sin(angle) / jnp.where(at_zero, 1.0, angle))
    window = 0.5 + 0.5 * jnp.cos(angle / (TAPS // 2 + 1))
    return jnp.where(inside, sinc * window, 0.0)


def split_high_low(value):
    high = value.astype(jnp.bfloat16)
    low = (value - high.astype(jnp.float32)).astype(jnp.bfloat16)
    return high, low


def shear_x_kernel(first_ref, shifts_ref, fracs_ref, planes_ref, out_ref, margin_ref):
    plane_count, rows, lanes = planes_ref.shape
    before, after = 8, 8
    line = lax.broadcasted_iota(jnp.int32, (lanes, lanes), 0)
    lane = lax.broadcasted_iota(jnp.int32, (lanes, lanes), 1)
    own_side = lane <= line
    tap = (lanes - lax.broadcasted_iota(jnp.int32, (8, lanes), 1)) % lanes
    lane_of_row = lax.broadcasted_iota(jnp.int32, (rows, lanes), 1)
    zeros = jnp.zeros((8, lanes), jnp.float32)
    first = first_ref[0]

    def one_plane(z, carry):
        shift = shifts_ref[first + z]
        frac = fracs_ref[first + z]
        margin_ref[z, 0:before, :] = zeros
        margin_ref[z, before:before + rows, :] = planes_ref[z]
        margin_ref[z, before + rows:before + rows + after, :] = zeros
        base = tap_weight_in_kernel(tap - BELOW, frac)
        spread = pltpu.roll(
            jnp.broadcast_to(base[0:1], (lanes, lanes)), 0, 1, stride=1, stride_axis=0
        )
        own = jnp.where(own_side, spread, 0.0)
        band = jnp.concatenate([own, spread - own], axis=0)
        band = jnp.concatenate(split_high_low(band), axis=1)
        start = shift - BELOW + before * lanes
        top = start // lanes
        turn = start - top * lanes
        back = lanes - turn
        parts = [
            pltpu.roll(margin_ref[z, pl.ds(top + i, rows), :], back, 1) for i in range(3)
        ]
        keep = lane_of_row < back
        window = jnp.concatenate(
            [jnp.where(keep, parts[0], parts[1]), jnp.where(keep, parts[1], parts[2])], axis=1
        )
        window = jnp.concatenate(split_high_low(window), axis=0)
        product = jnp.dot(window, band, preferred_element_type=jnp.float32)
        product = product[:rows] + product[rows:]
        out_ref[z] = product[:, :lanes] + product[:, lanes:]
        return carry

    lax.fori_loop(0, plane_count, one_plane, 0, unroll=2)


def shear_x(volume, x_offsets, x_fracs, first_plane):
    plane_count, rows, lanes = volume.shape
    return pl.pallas_call(
        shear_x_kernel,
        out_shape=jax.ShapeDtypeStruct(volume.shape, jnp.float32),
        in_specs=[SMEM_SPEC, SMEM_SPEC, SMEM_SPEC, VMEM_SPEC],
        out_specs=VMEM_SPEC,
        scratch_shapes=[pltpu.VMEM((plane_count, rows + 16, lanes), jnp.float32)],
        compiler_params=pltpu.CompilerParams(vmem_limit_bytes=VMEM_LIMIT),
        name="shear_x",
    )(first_plane.reshape(1), x_offsets, x_fracs, volume)


def shear_z_kernel(plane_count, depth, shift_ref, frac_ref, left_ref, own_ref, right_ref, out_ref):
    lanes = own_ref.shape[1]
    rows = own_ref.shape[0] // plane_count
    reach = plane_count + 2 * depth
    target = lax.broadcasted_iota(jnp.int32, (plane_count, reach), 0)
    source = lax.broadcasted_iota(jnp.int32, (plane_count, reach), 1)
    mixing = tap_weight_in_kernel(source - depth - target - shift_ref[0], frac_ref[0])
    mixing_high, mixing_low = split_high_low(mixing)
    mixing = jnp.concatenate(
        [
            jnp.concatenate([mixing_high, mixing_high], axis=1),
            jnp.concatenate([mixing_low, mixing_low], axis=1),
        ],
        axis=0,
    )

    def stack_of(row):
        return jnp.concatenate(
            [
                left_ref[pl.ds(row, depth, stride=rows), :],
                own_ref[pl.ds(row, plane_count, stride=rows), :],
                right_ref[pl.ds(row, depth, stride=rows), :],
            ],
            axis=0,
        )

    chunks, _, width = out_ref.shape
    per_chunk = width // lanes
    pair = 2 if per_chunk % 2 == 0 else 1

    for chunk in range(chunks):
        for piece in range(per_chunk // pair):
            row = chunk * per_chunk + piece * pair
            stack = jnp.concatenate([stack_of(row + i) for i in range(pair)], axis=1)
            stack = jnp.concatenate(split_high_low(stack), axis=0)
            product = jnp.dot(mixing, stack, preferred_element_type=jnp.float32)
            out_ref[chunk, :, piece * pair * lanes:(piece + 1) * pair * lanes] = (
                product[:plane_count] + product[plane_count:]
            )


def shear_z(own, left, right, z_offsets, z_fracs, chunks):
    plane_count, rows, lanes = own.shape
    depth = left.shape[0]
    return pl.pallas_call(
        functools.partial(shear_z_kernel, plane_count, depth),
        out_shape=jax.ShapeDtypeStruct((chunks, plane_count, rows * lanes // chunks), jnp.float32),
        in_specs=[SMEM_SPEC, SMEM_SPEC, VMEM_SPEC, VMEM_SPEC, VMEM_SPEC],
        out_specs=VMEM_SPEC,
        compiler_params=pltpu.CompilerParams(vmem_limit_bytes=VMEM_LIMIT),
        name="shear_z",
    )(
        z_offsets,
        z_fracs,
        left.reshape(depth * rows, lanes),
        own.reshape(plane_count * rows, lanes),
        right.reshape(depth * rows, lanes),
    )


def shear_y_kernel(
    total_planes, first_ref, slopes_ref, shifts_ref, fracs_ref, in_ref, out_ref, tilted_ref,
    taps_ref, totals_ref,
):
    ny, plane_count, width = in_ref.shape
    tilts = slopes_ref.shape[0]
    span = ny // 4
    shares = tilted_ref.shape[0]
    tap_rows = taps_ref.shape[0]
    distance = lax.broadcasted_iota(jnp.int32, (tap_rows, width), 0) - (ny - 1)
    taps_ref[...] = tap_weight_in_kernel(distance - shifts_ref[...], fracs_ref[...])

    for tile in range(width // LANES):
        lanes = slice(tile * LANES, (tile + 1) * LANES)
        weights = [
            jnp.broadcast_to(taps_ref[d:d + 1, lanes], (8, LANES)) for d in range(2 * ny - 1)
        ]
        for block in range(plane_count // 8):
            planes = slice(block * 8, (block + 1) * 8)
            source = [in_ref[j, planes, lanes] for j in range(ny)]
            for i in range(ny):
                value = weights[ny - 1 - i] * source[0]
                for j in range(1, ny):
                    value = value + weights[j - i + ny - 1] * source[j]
                out_ref[i, planes, lanes] = value

    lifts = 2 * span + 1
    entry = lax.broadcasted_iota(jnp.int32, (lifts * tilts, plane_count), 0)
    plane = lax.broadcasted_iota(jnp.int32, (lifts * tilts, plane_count), 1) + first_ref[0]
    lift = entry // tilts - span
    tilt = entry - (lift + span) * tilts
    slope = jnp.zeros_like(tilt)
    for t in range(tilts):
        slope = jnp.where(tilt == t, slopes_ref[t], slope)
    numerator = slope * (2 * plane - total_planes) * ny
    floor_at = lift * (16 * total_planes)
    chosen = (numerator >= floor_at) & (numerator < floor_at + 16 * total_planes)
    chosen = jnp.where(chosen, 1.0, 0.0).astype(jnp.bfloat16)
    chosen = jnp.concatenate([chosen, chosen], axis=1)

    totals_ref[...] = jnp.zeros(totals_ref.shape, jnp.float32)
    for j in range(ny):
        sums = jnp.dot(
            chosen,
            jnp.concatenate(split_high_low(out_ref[j]), axis=0),
            preferred_element_type=jnp.float32,
        )
        for l in range(lifts):
            i = j - (l - span)
            if 0 <= i < ny:
                for tile in range(width // LANES):
                    place = (tile * ny + i) * tilts
                    totals_ref[place:place + tilts, :] += sums[
                        l * tilts:(l + 1) * tilts, tile * LANES:(tile + 1) * LANES
                    ]
    per_share = tilts // shares
    for t in range(tilts):
        for tile in range(width // LANES):
            lanes = slice(tile * LANES, (tile + 1) * LANES)
            tilted_ref[t // per_share, t % per_share, :, lanes] = (
                totals_ref[pl.ds(tile * ny * tilts + t, ny, stride=tilts), :] * total_planes ** (-0.5)
            )


def shear_y(columns, y_offsets, y_fracs, slopes, first_plane, total_planes, shares):
    ny, plane_count, width = columns.shape
    tilts = slopes.shape[0]
    return pl.pallas_call(
        functools.partial(shear_y_kernel, total_planes),
        out_shape=(
            jax.ShapeDtypeStruct(columns.shape, jnp.float32),
            jax.ShapeDtypeStruct((shares, tilts // shares, ny, width), jnp.float32),
        ),
        in_specs=[SMEM_SPEC, SMEM_SPEC, VMEM_SPEC, VMEM_SPEC, VMEM_SPEC],
        out_specs=(VMEM_SPEC, VMEM_SPEC),
        scratch_shapes=[
            pltpu.VMEM((2 * ny, width), jnp.float32),
            pltpu.VMEM((width // LANES * ny * tilts, LANES), jnp.float32),
        ],
        compiler_params=pltpu.CompilerParams(vmem_limit_bytes=VMEM_LIMIT),
        name="shear_y",
    )(first_plane.reshape(1), slopes, y_offsets.reshape(1, width), y_fracs.reshape(1, width), columns)


def finish_kernel(landed_ref, shares_ref, rotated_ref, projections_ref):
    groups, plane_count, width = landed_ref.shape
    per_group = width // LANES
    rows = groups * per_group
    for group in range(groups):
        for tile in range(per_group):
            rotated_ref[pl.ds(group * per_group + tile, plane_count, stride=rows), :] = landed_ref[
                group, :, tile * LANES:(tile + 1) * LANES
            ]
    total = shares_ref[0]
    for share in range(1, shares_ref.shape[0]):
        total = total + shares_ref[share]
    projections_ref[...] = total


def finish(landed, shares):
    groups, plane_count, width = landed.shape
    return pl.pallas_call(
        finish_kernel,
        out_shape=(
            jax.ShapeDtypeStruct((plane_count * groups * width // LANES, LANES), jnp.float32),
            jax.ShapeDtypeStruct(shares.shape[1:], jnp.float32),
        ),
        in_specs=[VMEM_SPEC, VMEM_SPEC],
        out_specs=(VMEM_SPEC, VMEM_SPEC),
        compiler_params=pltpu.CompilerParams(vmem_limit_bytes=VMEM_LIMIT),
        name="finish",
    )(landed, shares)


def narrow_columns(columns, y_offsets, y_fracs, slopes, first_plane, total_planes):
    row_total, plane_count, col_local = columns.shape
    target_row = jnp.arange(row_total, dtype=jnp.int32)[:, None]
    source_row = jnp.arange(row_total, dtype=jnp.int32)[None, :]
    operator = tap_weight(
        (source_row - target_row)[None] - y_offsets[:, None, None], y_fracs[:, None, None]
    )
    rotated = jnp.einsum("cij,jzc->izc", operator, columns, precision=lax.Precision.HIGHEST)
    span = row_total // 4
    planes = first_plane + jnp.arange(plane_count, dtype=jnp.int32)
    padded = jnp.pad(rotated, ((span, span), (0, 0), (0, 0)))
    per_tilt = []
    for tilt in range(slopes.shape[0]):
        lifts = slopes[tilt] * (2 * planes - total_planes) * row_total // (16 * total_planes)
        moved = jax.vmap(
            lambda one_plane, lift: lax.dynamic_slice_in_dim(one_plane, span + lift, row_total, 0),
            in_axes=(1, 0),
        )(padded, lifts)
        per_tilt.append(jnp.sum(moved, axis=0))
    return rotated, jnp.stack(per_tilt) * total_planes ** (-0.5)


def local(volume, x_offsets, x_fracs, z_offsets, z_fracs, y_offsets, y_fracs, slopes):
    depth = TAPS // 2 + OFFZ
    plane_count, row_local, width_all = volume.shape
    groups, shares = lax.axis_size("gy"), lax.axis_size("gz")
    assert row_local == 1 and width_all % LANES == 0
    rows = width_all // LANES
    col_local = width_all // groups
    total_planes = plane_count * shares
    first_plane = (lax.axis_index("gz") * plane_count).astype(jnp.int32)
    sheared = shear_x(volume.reshape(plane_count, rows, LANES), x_offsets, x_fracs, first_plane)
    up = [(i, i + 1) for i in range(shares - 1)]
    down = [(j, i) for i, j in up]
    left = lax.ppermute(sheared[plane_count - depth:], "gz", up)
    right = lax.ppermute(sheared[:depth], "gz", down)
    if col_local % LANES:
        mixed = shear_z(sheared, left, right, z_offsets, z_fracs, rows)
        mixed = jnp.moveaxis(mixed, 0, 1).reshape(plane_count, groups, col_local)
        outgoing = jnp.moveaxis(mixed, 1, 0)
        columns = lax.all_to_all(outgoing, "gy", split_axis=0, concat_axis=0, tiled=True)
        rotated, tilted = narrow_columns(
            columns, y_offsets, y_fracs, slopes, first_plane, total_planes
        )
        projections = lax.psum_scatter(tilted, "gz", scatter_dimension=0, tiled=True)
        landed = lax.all_to_all(rotated, "gy", split_axis=0, concat_axis=0, tiled=True)
        rotated = jnp.moveaxis(landed, 0, 1).reshape(plane_count, row_local, width_all)
        return rotated, jnp.swapaxes(projections, 1, 2)
    outgoing = shear_z(sheared, left, right, z_offsets, z_fracs, groups)
    columns = lax.all_to_all(outgoing, "gy", split_axis=0, concat_axis=0, tiled=True)
    rotated, tilted = shear_y(
        columns, y_offsets, y_fracs, slopes, first_plane, total_planes, shares
    )
    tilted = lax.all_to_all(tilted, "gz", split_axis=0, concat_axis=0, tiled=True)
    landed = lax.all_to_all(rotated, "gy", split_axis=0, concat_axis=0, tiled=True)
    rotated, projections = finish(landed, tilted)
    return (
        rotated.reshape(plane_count, row_local, width_all),
        jnp.swapaxes(projections, 1, 2),
    )


def solution(mesh):
    return jax.shard_map(
        local,
        mesh=mesh,
        in_specs=(P("gz", "gy", None), P(), P(), P("gy"), P("gy"), P("gy"), P("gy"), P()),
        out_specs=(P("gz", "gy", None), P("gz", "gy", None)),
        check_vma=False,
    )
```

```python
import functools

import jax
import jax.numpy as jnp
from jax import lax
from jax.experimental import pallas as pl
from jax.experimental.pallas import tpu as pltpu
from jax.sharding import PartitionSpec as P

TAPS = 64
OFFX = 64
OFFZ = 4
LANES = 128
PARTS = 1
BELOW = TAPS // 2 - 1
VMEM_LIMIT = 48 * 1024 * 1024

SMEM_SPEC = pl.BlockSpec(memory_space=pltpu.SMEM)
VMEM_SPEC = pl.BlockSpec(memory_space=pltpu.VMEM)


def tap_weight(offset, fraction):
    moved = offset.astype(jnp.float32) - fraction
    inside = (offset >= 1 - TAPS // 2) & (offset <= TAPS // 2)
    value = jnp.sinc(moved) * (0.5 + 0.5 * jnp.cos(jnp.pi * moved / (TAPS // 2 + 1)))
    return jnp.where(inside, value, jnp.zeros_like(value))


def tap_weight_in_kernel(offset, fraction):
    moved = offset.astype(jnp.float32) - fraction
    inside = (offset >= 1 - TAPS // 2) & (offset <= TAPS // 2)
    angle = jnp.pi * moved
    at_zero = moved == 0.0
    sinc = jnp.where(at_zero, 1.0, jnp.sin(angle) / jnp.where(at_zero, 1.0, angle))
    window = 0.5 + 0.5 * jnp.cos(angle / (TAPS // 2 + 1))
    return jnp.where(inside, sinc * window, 0.0)


def split_high_low(value):
    high = value.astype(jnp.bfloat16)
    low = (value - high.astype(jnp.float32)).astype(jnp.bfloat16)
    return high, low


def shear_x_kernel(
    classes, first_ref, shifts_hbm, fracs_hbm, planes_hbm, *rest
):
    parts = len(rest) - 7
    out_refs = rest[:parts]
    planes_ref, margin_ref, base_ref, shifts_ref, fracs_ref, small_sem, plane_sem = rest[parts:]
    plane_count, rows, lanes = planes_ref.shape
    per_class = rows // classes
    before, after = 8, margin_ref.shape[1] - rows - 8
    blocks = plane_sem.shape[0]
    per_block = plane_count // blocks
    small = [
        pltpu.make_async_copy(shifts_hbm, shifts_ref, small_sem.at[0]),
        pltpu.make_async_copy(fracs_hbm, fracs_ref, small_sem.at[1]),
    ]
    large = [
        pltpu.make_async_copy(
            planes_hbm.at[b * per_block:(b + 1) * per_block],
            planes_ref.at[b * per_block:(b + 1) * per_block],
            plane_sem.at[b],
        )
        for b in range(blocks)
    ]
    for copy in small + large:
        copy.start()
    line = lax.broadcasted_iota(jnp.int32, (lanes, lanes), 0)
    lane = lax.broadcasted_iota(jnp.int32, (lanes, lanes), 1)
    own_side = lane <= line
    tap = (lanes - lax.broadcasted_iota(jnp.int32, (plane_count, lanes), 1)) % lanes
    lane_of_row = lax.broadcasted_iota(jnp.int32, (per_class, lanes), 1)
    zeros = jnp.zeros((8, lanes), jnp.float32)
    first = first_ref[0]
    for copy in small:
        copy.wait()
    for z in range(plane_count):
        base_ref[z:z + 1, :] = jnp.full((1, lanes), fracs_ref[first + z], jnp.float32)
    base_ref[...] = tap_weight_in_kernel(tap - BELOW, base_ref[...])

    def one_plane(z, carry):
        margin_ref[z, 0:before, :] = zeros
        margin_ref[z, before:before + rows, :] = planes_ref[z]
        margin_ref[z, before + rows:before + rows + after, :] = zeros
        spread = pltpu.roll(
            jnp.broadcast_to(base_ref[pl.ds(z, 1), :], (lanes, lanes)),
            0, 1, stride=1, stride_axis=0,
        )
        own = jnp.where(own_side, spread, 0.0)
        band = jnp.concatenate([own, spread - own], axis=0)
        band = jnp.concatenate(split_high_low(band), axis=1)
        start = shifts_ref[first + z] - BELOW + before * lanes
        top = start // lanes
        back = lanes - (start - top * lanes)
        keep = lane_of_row < back
        turned = [
            pltpu.roll(margin_ref[z, pl.ds(top + i, per_class, stride=classes), :], back, 1)
            for i in range(classes + 2)
        ]
        lines = [jnp.where(keep, turned[i], turned[i + 1]) for i in range(classes + 1)]
        window = jnp.concatenate(
            [jnp.concatenate(lines[:-1], axis=0), jnp.concatenate(lines[1:], axis=0)], axis=1
        )
        window = jnp.concatenate(split_high_low(window), axis=0)
        product = jnp.dot(window, band, preferred_element_type=jnp.float32)
        product = product[:rows] + product[rows:]
        product = product[:, :lanes] + product[:, lanes:]
        for part in range(parts):
            out_refs[part][z] = product[part * rows // parts:(part + 1) * rows // parts]
        return carry

    for b in range(blocks):
        large[b].wait()
        lax.fori_loop(b * per_block, (b + 1) * per_block, one_plane, 0, unroll=True)


def shear_x(volume, x_offsets, x_fracs, first_plane, classes, parts):
    plane_count, rows, lanes = volume.shape
    blocks = 2 if plane_count % 2 == 0 else 1
    return pl.pallas_call(
        functools.partial(shear_x_kernel, classes),
        out_shape=[
            jax.ShapeDtypeStruct((plane_count, rows // parts, lanes), jnp.float32)
        ] * parts,
        in_specs=[SMEM_SPEC] + [pl.BlockSpec(memory_space=pl.ANY)] * 3,
        out_specs=[VMEM_SPEC] * parts,
        scratch_shapes=[
            pltpu.VMEM(volume.shape, jnp.float32),
            pltpu.VMEM((plane_count, rows + 16, lanes), jnp.float32),
            pltpu.VMEM((plane_count, lanes), jnp.float32),
            pltpu.SMEM(x_offsets.shape, jnp.int32),
            pltpu.SMEM(x_fracs.shape, jnp.float32),
            pltpu.SemaphoreType.DMA((2,)),
            pltpu.SemaphoreType.DMA((blocks,)),
        ],
        compiler_params=pltpu.CompilerParams(vmem_limit_bytes=VMEM_LIMIT),
        name="shear_x",
    )(first_plane.reshape(1), x_offsets, x_fracs, volume)


def shear_z_kernel(
    plane_count, depth, place_ref, shift_ref, frac_ref, pair_ref, own_ref, other_ref, out_ref
):
    lanes = own_ref.shape[1]
    rows = own_ref.shape[0] // plane_count
    reach = plane_count + 2 * depth
    even = place_ref[0] % 2 == 0
    target = lax.broadcasted_iota(jnp.int32, (plane_count, reach), 0)
    column = lax.broadcasted_iota(jnp.int32, (plane_count, reach), 1)
    pair_start = jnp.where(even, plane_count, -depth)
    other_start = jnp.where(even, -depth, plane_count)
    source = jnp.where(
        column < depth,
        column + pair_start,
        jnp.where(
            column < depth + plane_count,
            column - depth,
            column - (depth + plane_count) + other_start,
        ),
    )
    mixing = tap_weight_in_kernel(source - target - shift_ref[0], frac_ref[0])
    mixing_high, mixing_low = split_high_low(mixing)
    mixing = jnp.concatenate(
        [
            jnp.concatenate([mixing_high, mixing_high], axis=1),
            jnp.concatenate([mixing_low, mixing_low], axis=1),
        ],
        axis=0,
    )

    def stack_of(row):
        return jnp.concatenate(
            [
                pair_ref[pl.ds(row, depth, stride=rows), :],
                own_ref[pl.ds(row, plane_count, stride=rows), :],
                other_ref[pl.ds(row, depth, stride=rows), :],
            ],
            axis=0,
        )

    chunks, _, width = out_ref.shape
    per_chunk = width // lanes
    pair = 2 if per_chunk % 2 == 0 else 1
    for chunk in range(chunks):
        for piece in range(per_chunk // pair):
            stack = jnp.concatenate(
                [stack_of((piece * pair + i) * chunks + chunk) for i in range(pair)], axis=1
            )
            stack = jnp.concatenate(split_high_low(stack), axis=0)
            product = jnp.dot(mixing, stack, preferred_element_type=jnp.float32)
            out_ref[chunk, :, piece * pair * lanes:(piece + 1) * pair * lanes] = (
                product[:plane_count] + product[plane_count:]
            )


def shear_z(own, pair, other, z_offsets, z_fracs, place, chunks):
    plane_count, rows, lanes = own.shape
    depth = pair.shape[0]
    return pl.pallas_call(
        functools.partial(shear_z_kernel, plane_count, depth),
        out_shape=jax.ShapeDtypeStruct((chunks, plane_count, rows * lanes // chunks), jnp.float32),
        in_specs=[SMEM_SPEC, SMEM_SPEC, SMEM_SPEC, VMEM_SPEC, VMEM_SPEC, VMEM_SPEC],
        out_specs=VMEM_SPEC,
        compiler_params=pltpu.CompilerParams(vmem_limit_bytes=VMEM_LIMIT),
        name="shear_z",
    )(
        place.reshape(1),
        z_offsets,
        z_fracs,
        pair.reshape(depth * rows, lanes),
        own.reshape(plane_count * rows, lanes),
        other.reshape(depth * rows, lanes),
    )


def shear_y_kernel(part, parts, shares, place_ref, slopes_ref, shifts_ref, fracs_ref, in_ref, *rest):
    last = part == parts - 1
    earlier = rest[:part] if last else ()
    rest = rest[len(earlier):]
    out_ref = rest[0]
    share_refs = rest[1:1 + shares] if last else ()
    totals_ref, taps_ref = rest[-2:]
    ny, plane_count, width = in_ref.shape
    total_planes = plane_count * shares
    tilts = slopes_ref.shape[0]
    span = ny // 4
    tiles = width // LANES
    tap_rows = taps_ref.shape[0]
    own = slice(part * width, (part + 1) * width)
    distance = lax.broadcasted_iota(jnp.int32, (tap_rows, width), 0) - (ny - 1)
    taps_ref[...] = tap_weight_in_kernel(distance - shifts_ref[:, own], fracs_ref[:, own])

    for tile in range(tiles):
        lanes = slice(tile * LANES, (tile + 1) * LANES)
        weights = [
            jnp.broadcast_to(taps_ref[d:d + 1, lanes], (8, LANES)) for d in range(2 * ny - 1)
        ]
        for block in range(plane_count // 8):
            planes = slice(block * 8, (block + 1) * 8)
            source = [in_ref[j, planes, lanes] for j in range(ny)]
            for i in range(ny):
                value = weights[ny - 1 - i] * source[0]
                for j in range(1, ny):
                    value = value + weights[j - i + ny - 1] * source[j]
                out_ref[i, planes, lanes] = value

    lifts = 2 * span + 1
    entry = lax.broadcasted_iota(jnp.int32, (lifts * tilts, plane_count), 0)
    plane = lax.broadcasted_iota(jnp.int32, (lifts * tilts, plane_count), 1)
    plane = plane + place_ref[0] * plane_count
    lift = entry // tilts - span
    tilt = entry - (lift + span) * tilts
    slope = jnp.zeros_like(tilt)
    for t in range(tilts):
        slope = jnp.where(tilt == t, slopes_ref[t], slope)
    numerator = slope * (2 * plane - total_planes) * ny
    floor_at = lift * (16 * total_planes)
    chosen = (numerator >= floor_at) & (numerator < floor_at + 16 * total_planes)
    chosen = jnp.where(chosen, 1.0, 0.0).astype(jnp.bfloat16)
    chosen = jnp.concatenate([chosen, chosen], axis=1)

    totals_ref[...] = jnp.zeros(totals_ref.shape, jnp.float32)
    for j in range(ny):
        sums = jnp.dot(
            chosen,
            jnp.concatenate(split_high_low(out_ref[j]), axis=0),
            preferred_element_type=jnp.float32,
        )
        for l in range(lifts):
            i = j - (l - span)
            if 0 <= i < ny:
                for tile in range(tiles):
                    row = (tile * ny + i) * tilts
                    totals_ref[row:row + tilts, :] += sums[
                        l * tilts:(l + 1) * tilts, tile * LANES:(tile + 1) * LANES
                    ]
    if not last:
        return
    per_share = tilts // shares
    for step, share_ref in enumerate(share_refs):
        tilt = (place_ref[0] ^ step) * per_share
        for u in range(per_share):
            for source, ref in enumerate((*earlier, totals_ref)):
                for tile in range(tiles):
                    column = source * width + tile * LANES
                    share_ref[u, :, column:column + LANES] = (
                        ref[pl.ds(tile * ny * tilts + tilt + u, ny, stride=tilts), :]
                        * total_planes ** (-0.5)
                    )


def shear_y(columns, y_offsets, y_fracs, slopes, place, part, parts, shares, earlier):
    ny, plane_count, width = columns.shape
    tilts = slopes.shape[0]
    last = part == parts - 1
    totals = (width // LANES * ny * tilts, LANES)
    out_shape = [jax.ShapeDtypeStruct(columns.shape, jnp.float32)]
    scratch = [pltpu.VMEM((2 * ny, width), jnp.float32)]
    if last:
        share = (tilts // shares, ny, width * parts)
        out_shape += [jax.ShapeDtypeStruct(share, jnp.float32)] * shares
        scratch = [pltpu.VMEM(totals, jnp.float32)] + scratch
    else:
        out_shape += [jax.ShapeDtypeStruct(totals, jnp.float32)]
    return pl.pallas_call(
        functools.partial(shear_y_kernel, part, parts, shares),
        out_shape=out_shape,
        in_specs=[SMEM_SPEC, SMEM_SPEC] + [VMEM_SPEC] * (3 + len(earlier)),
        out_specs=[VMEM_SPEC] * len(out_shape),
        scratch_shapes=scratch,
        compiler_params=pltpu.CompilerParams(vmem_limit_bytes=VMEM_LIMIT),
        name="shear_y",
    )(
        place.reshape(1),
        slopes,
        y_offsets.reshape(1, width * parts),
        y_fracs.reshape(1, width * parts),
        columns,
        *earlier,
    )


def finish_kernel(parts, *refs):
    landed_refs, share_refs = refs[:parts], refs[parts:-2]
    rotated_ref, projections_ref = refs[-2:]
    groups, plane_count, width = landed_refs[0].shape
    per_part = width // LANES
    per_group = per_part * parts
    rows = groups * per_group
    for part, landed_ref in enumerate(landed_refs):
        for group in range(groups):
            for tile in range(per_part):
                row = group * per_group + part * per_part + tile
                rotated_ref[pl.ds(row, plane_count, stride=rows), :] = landed_ref[
                    group, :, tile * LANES:(tile + 1) * LANES
                ]
    total = share_refs[0][...]
    for share_ref in share_refs[1:]:
        total = total + share_ref[...]
    projections_ref[...] = total


def finish(landed, shares):
    groups, plane_count, width = landed[0].shape
    rows = plane_count * groups * len(landed) * width // LANES
    return pl.pallas_call(
        functools.partial(finish_kernel, len(landed)),
        out_shape=(
            jax.ShapeDtypeStruct((rows, LANES), jnp.float32),
            jax.ShapeDtypeStruct(shares[0].shape, jnp.float32),
        ),
        in_specs=[VMEM_SPEC] * (len(landed) + len(shares)),
        out_specs=(VMEM_SPEC, VMEM_SPEC),
        compiler_params=pltpu.CompilerParams(vmem_limit_bytes=VMEM_LIMIT),
        name="finish",
    )(*landed, *shares)


def narrow_columns(columns, y_offsets, y_fracs, slopes, first_plane, total_planes):
    row_total, plane_count, col_local = columns.shape
    target_row = jnp.arange(row_total, dtype=jnp.int32)[:, None]
    source_row = jnp.arange(row_total, dtype=jnp.int32)[None, :]
    operator = tap_weight(
        (source_row - target_row)[None] - y_offsets[:, None, None], y_fracs[:, None, None]
    )
    rotated = jnp.einsum("cij,jzc->izc", operator, columns, precision=lax.Precision.HIGHEST)
    span = row_total // 4
    planes = first_plane + jnp.arange(plane_count, dtype=jnp.int32)
    padded = jnp.pad(rotated, ((span, span), (0, 0), (0, 0)))
    per_tilt = []
    for tilt in range(slopes.shape[0]):
        lifts = slopes[tilt] * (2 * planes - total_planes) * row_total // (16 * total_planes)
        moved = jax.vmap(
            lambda one_plane, lift: lax.dynamic_slice_in_dim(one_plane, span + lift, row_total, 0),
            in_axes=(1, 0),
        )(padded, lifts)
        per_tilt.append(jnp.sum(moved, axis=0))
    return rotated, jnp.stack(per_tilt) * total_planes ** (-0.5)


def exchange(value, axis):
    return lax.all_to_all(value, axis, split_axis=0, concat_axis=0, tiled=True)


def local(volume, x_offsets, x_fracs, z_offsets, z_fracs, y_offsets, y_fracs, slopes):
    depth = TAPS // 2 + OFFZ
    plane_count, row_local, width_all = volume.shape
    groups, shares = lax.axis_size("gy"), lax.axis_size("gz")
    assert row_local == 1 and width_all % LANES == 0
    rows = width_all // LANES
    col_local = width_all // groups
    total_planes = plane_count * shares
    place = lax.axis_index("gz").astype(jnp.int32)
    first_plane = place * plane_count
    wide = col_local % LANES == 0
    classes = col_local // LANES if wide else 1
    parts = PARTS if classes % PARTS == 0 else 1
    sheared = shear_x(
        volume.reshape(plane_count, rows, LANES), x_offsets, x_fracs, first_plane, classes, parts
    )
    spare = plane_count - depth
    pair_first = jnp.where(place % 2 == 0, spare, 0)
    swaps = [[], []]
    for i in range(shares - 1):
        swaps[i % 2] += [(i, i + 1), (i + 1, i)]
    mixed = []
    for value in sheared:
        pair = lax.ppermute(
            lax.dynamic_slice_in_dim(value, pair_first, depth, 0), "gz", swaps[0]
        )
        other = lax.ppermute(
            lax.dynamic_slice_in_dim(value, spare - pair_first, depth, 0), "gz", swaps[1]
        )
        mixed.append(
            shear_z(value, pair, other, z_offsets, z_fracs, place, groups if wide else rows)
        )
    if not wide:
        outgoing = jnp.moveaxis(mixed[0], 0, 1).reshape(plane_count, groups, col_local)
        columns = exchange(jnp.moveaxis(outgoing, 1, 0), "gy")
        rotated, tilted = narrow_columns(
            columns, y_offsets, y_fracs, slopes, first_plane, total_planes
        )
        projections = lax.psum_scatter(tilted, "gz", scatter_dimension=0, tiled=True)
        landed = exchange(rotated, "gy")
        rotated = jnp.moveaxis(landed, 0, 1).reshape(plane_count, row_local, width_all)
        return rotated, jnp.swapaxes(projections, 1, 2)
    columns = [exchange(value, "gy") for value in mixed]
    landed, totals = [], []
    for part in range(parts):
        rotated, *tilted = shear_y(
            columns[part], y_offsets, y_fracs, slopes, place, part, parts, shares,
            totals if part == parts - 1 else [],
        )
        landed.append(exchange(rotated, "gy"))
        totals += tilted
    shares_own = [tilted[0]] + [
        lax.ppermute(tilted[step], "gz", [(i, i ^ step) for i in range(shares)])
        for step in range(1, shares)
    ]
    rotated, projections = finish(landed, shares_own)
    return (
        rotated.reshape(plane_count, row_local, width_all),
        jnp.swapaxes(projections, 1, 2),
    )


def solution(mesh):
    return jax.shard_map(
        local,
        mesh=mesh,
        in_specs=(P("gz", "gy", None), P(), P(), P("gy"), P("gy"), P("gy"), P("gy"), P()),
        out_specs=(P("gz", "gy", None), P("gz", "gy", None)),
        check_vma=False,
    )
```

```python
import functools

import jax
import jax.numpy as jnp
from jax import lax
from jax.experimental import pallas as pl
from jax.experimental.pallas import tpu as pltpu
from jax.sharding import PartitionSpec as P

TAPS = 64
OFFX = 64
OFFZ = 4
LANES = 128
BELOW = TAPS // 2 - 1
VMEM_LIMIT = 32 * 1024 * 1024

SMEM_SPEC = pl.BlockSpec(memory_space=pltpu.SMEM)
VMEM_SPEC = pl.BlockSpec(memory_space=pltpu.VMEM)


def tap_weight(offset, fraction):
    moved = offset.astype(jnp.float32) - fraction
    inside = (offset >= 1 - TAPS // 2) & (offset <= TAPS // 2)
    value = jnp.sinc(moved) * (0.5 + 0.5 * jnp.cos(jnp.pi * moved / (TAPS // 2 + 1)))
    return jnp.where(inside, value, jnp.zeros_like(value))


def tap_weight_in_kernel(offset, fraction):
    moved = offset.astype(jnp.float32) - fraction
    inside = (offset >= 1 - TAPS // 2) & (offset <= TAPS // 2)
    angle = jnp.pi * moved
    at_zero = moved == 0.0
    sinc = jnp.where(at_zero, 1.0, jnp.sin(angle) / jnp.where(at_zero, 1.0, angle))
    window = 0.5 + 0.5 * jnp.cos(angle / (TAPS // 2 + 1))
    return jnp.where(inside, sinc * window, 0.0)


def split_high_low(value):
    high = value.astype(jnp.bfloat16)
    low = (value - high.astype(jnp.float32)).astype(jnp.bfloat16)
    return high, low


def shear_x_kernel(
    classes, first_ref, side_ref, shifts_hbm, fracs_hbm, planes_hbm, *rest
):
    out_refs = rest[:-8]
    planes_ref, margin_ref, base_ref, lines_ref, shifts_ref, fracs_ref, small_sem, plane_sem = (
        rest[-8:]
    )
    plane_count, rows, lanes = planes_ref.shape
    per_class = rows // classes
    before, after = 8, margin_ref.shape[1] - rows - 8
    blocks = plane_sem.shape[0]
    per_block = plane_count // blocks
    small = [
        pltpu.make_async_copy(shifts_hbm, shifts_ref, small_sem.at[0]),
        pltpu.make_async_copy(fracs_hbm, fracs_ref, small_sem.at[1]),
    ]
    large = [
        pltpu.make_async_copy(
            planes_hbm.at[b * per_block:(b + 1) * per_block],
            planes_ref.at[b * per_block:(b + 1) * per_block],
            plane_sem.at[b],
        )
        for b in range(blocks)
    ]
    for copy in small + large:
        copy.start()
    line = lax.broadcasted_iota(jnp.int32, (lanes, lanes), 0)
    lane = lax.broadcasted_iota(jnp.int32, (lanes, lanes), 1)
    own_side = lane <= line
    tap = (lanes - lax.broadcasted_iota(jnp.int32, (plane_count, lanes), 1)) % lanes
    lane_of_row = lax.broadcasted_iota(jnp.int32, (per_class, lanes), 1)
    zeros = jnp.zeros((8, lanes), jnp.float32)
    first = first_ref[0]
    first_lines = (2 - 2 * side_ref[0], 2 * side_ref[0])
    for copy in small:
        copy.wait()
    for z in range(plane_count):
        base_ref[z:z + 1, :] = jnp.full((1, lanes), fracs_ref[first + z], jnp.float32)
    base_ref[...] = tap_weight_in_kernel(tap - BELOW, base_ref[...])

    def one_plane(z, carry):
        margin_ref[z, 0:before, :] = zeros
        margin_ref[z, before:before + rows, :] = planes_ref[z]
        margin_ref[z, before + rows:before + rows + after, :] = zeros
        spread = pltpu.roll(
            jnp.broadcast_to(base_ref[pl.ds(z, 1), :], (lanes, lanes)),
            0, 1, stride=1, stride_axis=0,
        )
        own = jnp.where(own_side, spread, 0.0)
        band = jnp.concatenate([own, spread - own], axis=0)
        band = jnp.concatenate(split_high_low(band), axis=1)
        start = shifts_ref[first + z] - BELOW + before * lanes
        top = start // lanes
        back = lanes - (start - top * lanes)
        keep = lane_of_row < back
        turned = [
            pltpu.roll(margin_ref[z, pl.ds(top + i, per_class, stride=classes), :], back, 1)
            for i in range(classes + 2)
        ]
        lines = [jnp.where(keep, turned[i], turned[i + 1]) for i in range(classes + 1)]
        window = jnp.concatenate(
            [jnp.concatenate(lines[:-1], axis=0), jnp.concatenate(lines[1:], axis=0)], axis=1
        )
        window = jnp.concatenate(split_high_low(window), axis=0)
        product = jnp.dot(window, band, preferred_element_type=jnp.float32)
        product = product[:rows] + product[rows:]
        product = product[:, :lanes] + product[:, lanes:]
        if len(out_refs) == 1:
            out_refs[0][z] = product
            return carry
        lines_ref[z] = product
        quarter = rows // 4
        for out_ref, first_line in zip(out_refs, first_lines):
            for core in range(2):
                out_ref[z, core * quarter:(core + 1) * quarter, :] = lines_ref[
                    z, pl.ds(first_line + core, quarter, stride=4), :
                ]
        return carry

    for b in range(blocks):
        large[b].wait()
        lax.fori_loop(b * per_block, (b + 1) * per_block, one_plane, 0, unroll=True)


def shear_x(volume, x_offsets, x_fracs, first_plane, side, classes, parts):
    plane_count, rows, lanes = volume.shape
    blocks = 2 if plane_count % 2 == 0 else 1
    return pl.pallas_call(
        functools.partial(shear_x_kernel, classes),
        out_shape=[
            jax.ShapeDtypeStruct((plane_count, rows // parts, lanes), jnp.float32)
        ] * parts,
        in_specs=[SMEM_SPEC] * 2 + [pl.BlockSpec(memory_space=pltpu.HBM)] * 3,
        out_specs=[VMEM_SPEC] * parts,
        scratch_shapes=[
            pltpu.VMEM(volume.shape, jnp.float32),
            pltpu.VMEM((plane_count, rows + 16, lanes), jnp.float32),
            pltpu.VMEM((plane_count, lanes), jnp.float32),
            pltpu.VMEM(volume.shape, jnp.float32),
            pltpu.SMEM(x_offsets.shape, jnp.int32),
            pltpu.SMEM(x_fracs.shape, jnp.float32),
            pltpu.SemaphoreType.DMA((2,)),
            pltpu.SemaphoreType.DMA((blocks,)),
        ],
        compiler_params=pltpu.CompilerParams(vmem_limit_bytes=VMEM_LIMIT),
        name="shear_x",
    )(
        first_plane.reshape(1),
        side.reshape(1),
        *(pltpu.with_memory_space_constraint(v, pltpu.HBM) for v in (x_offsets, x_fracs, volume)),
    )


def weights_kernel(
    plane_count, depth, ny, shares, place_ref, shift_ref, frac_ref, slopes_ref, shifts_ref,
    fracs_ref, mixing_ref, taps_ref, chosen_ref,
):
    reach = plane_count + 2 * depth
    even = place_ref[0] % 2 == 0
    target = lax.broadcasted_iota(jnp.int32, (plane_count, reach), 0)
    column = lax.broadcasted_iota(jnp.int32, (plane_count, reach), 1)
    pair_start = jnp.where(even, plane_count, -depth)
    other_start = jnp.where(even, -depth, plane_count)
    source = jnp.where(
        column < depth,
        column + pair_start,
        jnp.where(
            column < depth + plane_count,
            column - depth,
            column - (depth + plane_count) + other_start,
        ),
    )
    mixing_ref[...] = tap_weight_in_kernel(source - target - shift_ref[0], frac_ref[0])
    lanes = taps_ref.shape[1]
    distance = lax.broadcasted_iota(jnp.int32, (2 * ny, lanes), 0) - (ny - 1)
    for tile in range(shifts_ref.shape[1] // lanes):
        part = slice(tile * lanes, (tile + 1) * lanes)
        taps_ref[tile * 2 * ny:(tile + 1) * 2 * ny, :] = tap_weight_in_kernel(
            distance - shifts_ref[:, part], fracs_ref[:, part]
        )
    total_planes = plane_count * shares
    tilts = slopes_ref.shape[0]
    span = ny // 4
    entry = lax.broadcasted_iota(jnp.int32, chosen_ref.shape, 0)
    plane = lax.broadcasted_iota(jnp.int32, chosen_ref.shape, 1) + place_ref[0] * plane_count
    lift = entry // tilts - span
    tilt = entry - (lift + span) * tilts
    slope = jnp.zeros_like(tilt)
    for t in range(tilts):
        slope = jnp.where(tilt == t, slopes_ref[t], slope)
    numerator = slope * (2 * plane - total_planes) * ny
    floor_at = lift * (16 * total_planes)
    chosen = (numerator >= floor_at) & (numerator < floor_at + 16 * total_planes)
    chosen_ref[...] = jnp.where(chosen, 1.0, 0.0)


def weights(
    place, z_offsets, z_fracs, slopes, y_offsets, y_fracs, plane_count, depth, ny, shares
):
    width = y_offsets.shape[0]
    lifts = 2 * (ny // 4) + 1
    return pl.pallas_call(
        functools.partial(weights_kernel, plane_count, depth, ny, shares),
        out_shape=(
            jax.ShapeDtypeStruct((plane_count, plane_count + 2 * depth), jnp.float32),
            jax.ShapeDtypeStruct((width // LANES * 2 * ny, LANES), jnp.float32),
            jax.ShapeDtypeStruct((lifts * slopes.shape[0], plane_count), jnp.float32),
        ),
        in_specs=[SMEM_SPEC] * 4 + [VMEM_SPEC] * 2,
        out_specs=(VMEM_SPEC, VMEM_SPEC, VMEM_SPEC),
        compiler_params=pltpu.CompilerParams(vmem_limit_bytes=VMEM_LIMIT),
        name="weights",
    )(
        place.reshape(1), z_offsets, z_fracs, slopes,
        y_offsets.reshape(1, width), y_fracs.reshape(1, width),
    )


def shear_z_kernel(
    plane_count, depth, chips, row_ref, mixing_ref, pair_ref, own_ref, other_ref, *outs
):
    lanes = own_ref.shape[1]
    rows = own_ref.shape[0] // plane_count
    half = chips // 2
    tiles = rows // chips
    pair = 2 if tiles % 2 == 0 else 1
    high, low = split_high_low(mixing_ref[...])
    mixing = jnp.concatenate(
        [jnp.concatenate([high, high], axis=1), jnp.concatenate([low, low], axis=1)], axis=0
    )
    core, chip_pair = row_ref[0] % 2, row_ref[0] // 4
    for index, out_ref in enumerate(outs):
        first = (core ^ (index % 2)) * (rows // 2) + (chip_pair ^ (index // 2))
        for tile in range(0, tiles, pair):
            columns = []
            for i in range(tile, tile + pair):
                row = first + i * half
                columns.append(
                    jnp.concatenate(
                        [
                            pair_ref[pl.ds(row, depth, stride=rows), :],
                            own_ref[pl.ds(row, plane_count, stride=rows), :],
                            other_ref[pl.ds(row, depth, stride=rows), :],
                        ],
                        axis=0,
                    )
                )
            stack = jnp.concatenate(columns, axis=1)
            stack = jnp.concatenate(split_high_low(stack), axis=0)
            product = jnp.dot(mixing, stack, preferred_element_type=jnp.float32)
            out_ref[:, tile * lanes:(tile + pair) * lanes] = (
                product[:plane_count] + product[plane_count:]
            )


def shear_z(row, mixing, pair, own, other, chips):
    plane_count, rows, lanes = own.shape
    depth = pair.shape[0]
    width = rows * lanes // chips
    return pl.pallas_call(
        functools.partial(shear_z_kernel, plane_count, depth, chips),
        out_shape=[jax.ShapeDtypeStruct((plane_count, width), jnp.float32)] * chips,
        in_specs=[SMEM_SPEC] + [VMEM_SPEC] * 4,
        out_specs=[VMEM_SPEC] * chips,
        compiler_params=pltpu.CompilerParams(vmem_limit_bytes=VMEM_LIMIT),
        name="shear_z",
    )(row.reshape(1), mixing, *(value.reshape(-1, lanes) for value in (pair, own, other)))


def shear_y_kernel(ny, row_ref, taps_ref, *refs):
    in_refs, own_refs, out_refs = refs[:ny][::-1], refs[ny:ny + 2], refs[ny + 2:]
    plane_count, width = in_refs[0].shape
    row = row_ref[0]
    for tile in range(width // LANES):
        lanes = slice(tile * LANES, (tile + 1) * LANES)
        first = tile * 2 * ny + ny - 1
        for target in range(ny):
            weight = [
                jnp.broadcast_to(
                    taps_ref[pl.ds(first + (row ^ source) - (row ^ target), 1), :], (8, LANES)
                )
                for source in range(ny)
            ]
            for block in range(plane_count // 8):
                planes = slice(block * 8, (block + 1) * 8)
                value = weight[0] * in_refs[0][planes, lanes]
                for source in range(1, ny):
                    value = value + weight[source] * in_refs[source][planes, lanes]
                if target < 2:
                    own_refs[target][planes, lanes] = value
                else:
                    out_refs[target // 2 - 1][target % 2, planes, lanes] = value


def shear_y(row, taps, columns):
    ny = len(columns)
    shape = columns[0].shape
    out_shape = [jax.ShapeDtypeStruct(shape, jnp.float32)] * 2
    out_shape += [jax.ShapeDtypeStruct((2, *shape), jnp.float32)] * (ny // 2 - 1)
    return pl.pallas_call(
        functools.partial(shear_y_kernel, ny),
        out_shape=out_shape,
        in_specs=[SMEM_SPEC] + [VMEM_SPEC] * (1 + ny),
        out_specs=[VMEM_SPEC] * len(out_shape),
        compiler_params=pltpu.CompilerParams(vmem_limit_bytes=VMEM_LIMIT),
        name="shear_y",
    )(row.reshape(1), taps, *columns[::-1])


def collect_kernel(*refs):
    out_ref = refs[-1]
    for index, ref in enumerate(refs[:-1]):
        out_ref[index] = ref[1]


def collect(landed):
    return pl.pallas_call(
        collect_kernel,
        out_shape=jax.ShapeDtypeStruct((len(landed), *landed[0].shape[1:]), jnp.float32),
        in_specs=[VMEM_SPEC] * len(landed),
        out_specs=VMEM_SPEC,
        compiler_params=pltpu.CompilerParams(vmem_limit_bytes=VMEM_LIMIT),
        name="collect",
    )(*landed)


def project_kernel(chips, tilts, place_ref, row_ref, chosen_ref, *refs):
    in_refs, share_refs, totals_ref = refs[:chips + 1], refs[chips + 1:-1], refs[-1]
    ny, shares = 2 * chips, len(share_refs)
    plane_count, width = in_refs[0].shape
    total_planes = plane_count * shares
    span = ny // 4
    tiles = width // LANES
    lifts = 2 * span + 1
    chosen = chosen_ref[...].astype(jnp.bfloat16)
    chosen = jnp.concatenate([chosen, chosen], axis=1)

    per_tile = (ny + 2 * span) * tilts
    totals_ref[...] = jnp.zeros(totals_ref.shape, jnp.float32)
    for source in range(ny):
        if source < 2:
            value = in_refs[source][...]
        else:
            value = in_refs[source // 2 + 1][source % 2]
        sums = jnp.dot(
            chosen,
            jnp.concatenate(split_high_low(value), axis=0),
            preferred_element_type=jnp.float32,
        )
        row = row_ref[0] ^ source
        for l in range(lifts):
            for tile in range(tiles):
                start = pl.multiple_of(tile * per_tile + (row + 2 * span - l) * tilts, tilts)
                totals_ref[pl.ds(start, tilts), :] += sums[
                    l * tilts:(l + 1) * tilts, tile * LANES:(tile + 1) * LANES
                ]
    per_share = tilts // shares
    for step, share_ref in enumerate(share_refs):
        tilt = (place_ref[0] ^ step) * per_share
        for u in range(per_share):
            for tile in range(tiles):
                share_ref[u, :, tile * LANES:(tile + 1) * LANES] = (
                    totals_ref[
                        pl.ds(tile * per_tile + span * tilts + tilt + u, ny, stride=tilts), :
                    ]
                    * total_planes ** (-0.5)
                )


def project(place, row, chosen, rotated, shares):
    chips = len(rotated) - 1
    ny = 2 * chips
    tilts = chosen.shape[0] // (2 * (ny // 4) + 1)
    width = rotated[0].shape[1]
    share = jax.ShapeDtypeStruct((tilts // shares, ny, width), jnp.float32)
    totals = (width // LANES * (ny + 2 * (ny // 4)) * tilts, LANES)
    return pl.pallas_call(
        functools.partial(project_kernel, chips, tilts),
        out_shape=[share] * shares,
        in_specs=[SMEM_SPEC] * 2 + [VMEM_SPEC] * (1 + len(rotated)),
        out_specs=[VMEM_SPEC] * shares,
        scratch_shapes=[pltpu.VMEM(totals, jnp.float32)],
        compiler_params=pltpu.CompilerParams(vmem_limit_bytes=VMEM_LIMIT),
        name="project",
    )(place.reshape(1), row.reshape(1), chosen, *rotated)


def finish_kernel(slots, row_ref, *refs):
    rotated_ref, sources = refs[-1], refs[:len(slots)]
    rows = rotated_ref.shape[0] // sources[0].shape[-2]
    for ref, (slot, index) in zip(sources, slots):
        plane_count, width = ref.shape[-2:]
        per_group = width // LANES
        start = (row_ref[0] ^ slot) * per_group
        source = ref if index is None else ref.at[index]
        for tile in range(per_group):
            rotated_ref[pl.ds(start + tile, plane_count, stride=rows), :] = source[
                :, tile * LANES:(tile + 1) * LANES
            ]


def finish(row, own, early, late, landed):
    chips = len(landed) + 1
    plane_count, width = own.shape
    slots = [(0, None), (1, None)]
    slots += [(2 * step, 0) for step in range(1, chips)]
    slots += [(2 * step + 1, step - 1) for step in range(1, chips)]
    return pl.pallas_call(
        functools.partial(finish_kernel, slots),
        out_shape=jax.ShapeDtypeStruct(
            (plane_count * 2 * chips * width // LANES, LANES), jnp.float32
        ),
        in_specs=[SMEM_SPEC] + [VMEM_SPEC] * len(slots),
        out_specs=VMEM_SPEC,
        compiler_params=pltpu.CompilerParams(vmem_limit_bytes=VMEM_LIMIT),
        name="finish",
    )(row.reshape(1), own, early, *landed, *([late] * (chips - 1)))


def add_kernel(*refs):
    total = refs[0][...]
    for ref in refs[1:-1]:
        total = total + ref[...]
    refs[-1][...] = total


def add(shares):
    return pl.pallas_call(
        add_kernel,
        out_shape=jax.ShapeDtypeStruct(shares[0].shape, jnp.float32),
        in_specs=[VMEM_SPEC] * len(shares),
        out_specs=VMEM_SPEC,
        compiler_params=pltpu.CompilerParams(vmem_limit_bytes=VMEM_LIMIT),
        name="add_shares",
    )(*shares)


def with_halo(value, sides, width):
    for axis, dim in sides:
        peers, length = (lax.axis_size(axis), value.shape[dim])
        up = [(i, (i + 1) % peers) for i in range(peers - 1)]
        down = [(j, i) for i, j in up]
        last = lax.slice_in_dim(value, length - width, length, axis=dim)
        first = lax.slice_in_dim(value, 0, width, axis=dim)
        before = lax.ppermute(last, axis, up)
        after = lax.ppermute(first, axis, down)
        value = jnp.concatenate([before, value, after], axis=dim)
    return value


def narrow_local(sheared_x, first_plane, z_offsets, z_fracs, y_offsets, y_fracs, slopes):
    depth = TAPS // 2 + OFFZ
    plane_count, row_local, width_all = sheared_x.shape
    groups = lax.axis_size("gy")
    col_local = width_all // groups
    extended = with_halo(sheared_x, (("gz", 0),), depth)
    plane_index = jnp.arange(plane_count, dtype=jnp.int32)[:, None]
    source_index = jnp.arange(plane_count + 2 * depth, dtype=jnp.int32)[None, :]
    mixing = tap_weight(
        (source_index - depth - plane_index)[None] - z_offsets[:, None, None],
        z_fracs[:, None, None],
    )
    blocked = extended.reshape(plane_count + 2 * depth, row_local, groups, col_local)
    outgoing = jnp.einsum("rzj,jrgc->grcz", mixing, blocked, precision=lax.Precision.HIGHEST)
    outgoing = outgoing.reshape(groups, 1, row_local * col_local * plane_count)
    arrived = lax.all_to_all(outgoing, "gy", split_axis=0, concat_axis=1, tiled=True)
    row_total = groups * row_local
    columns = arrived.reshape(row_total, col_local, plane_count)
    target_row = jnp.arange(row_total, dtype=jnp.int32)[:, None]
    source_row = jnp.arange(row_total, dtype=jnp.int32)[None, :]
    operator = tap_weight(
        (source_row - target_row)[None] - y_offsets[:, None, None], y_fracs[:, None, None]
    )
    rotated_cols = jnp.einsum("cij,jcz->zci", operator, columns, precision=lax.Precision.HIGHEST)
    span_pad = row_total // 4
    total_planes = plane_count * lax.axis_size("gz")
    global_planes = first_plane + jnp.arange(plane_count, dtype=jnp.int32)
    padded_cols = jnp.pad(rotated_cols, ((0, 0), (0, 0), (span_pad, span_pad)))
    per_tilt = []
    for tilt_index in range(slopes.shape[0]):
        lifts = (
            slopes[tilt_index]
            * (2 * global_planes - total_planes)
            * row_total
            // (16 * total_planes)
        )
        moved = jax.vmap(
            lambda one_plane, lift_one: lax.dynamic_slice_in_dim(
                one_plane, span_pad + lift_one, row_total, 1
            )
        )(padded_cols, lifts)
        per_tilt.append(jnp.sum(moved, axis=0))
    partial_terms = jnp.stack(per_tilt) * total_planes ** (-0.5)
    projections = lax.psum_scatter(partial_terms, "gz", scatter_dimension=0, tiled=True)
    returning = rotated_cols.reshape(plane_count, col_local, groups, row_local)
    returning = jnp.transpose(returning, (2, 3, 1, 0)).reshape(
        groups, 1, row_local * col_local * plane_count
    )
    landed = lax.all_to_all(returning, "gy", split_axis=0, concat_axis=1, tiled=True)
    landed = landed.reshape(groups, row_local, col_local, plane_count)
    rotated = jnp.transpose(landed, (3, 1, 0, 2)).reshape(
        plane_count, row_local, groups * col_local
    )
    return (rotated, projections)


def swap(value, axis, step):
    return lax.ppermute(value, axis, [(i, i ^ step) for i in range(lax.axis_size(axis))])


def local(volume, x_offsets, x_fracs, z_offsets, z_fracs, y_offsets, y_fracs, slopes):
    depth = TAPS // 2 + OFFZ
    plane_count, row_local, width_all = volume.shape
    groups, shares = lax.axis_size("gy"), lax.axis_size("gz")
    assert row_local == 1 and width_all % LANES == 0
    rows = width_all // LANES
    col_local = width_all // groups
    place = lax.axis_index("gz").astype(jnp.int32)
    row = lax.axis_index("gy").astype(jnp.int32)
    first_plane = place * plane_count
    chips = groups // 2
    wide = col_local % LANES == 0 and col_local > LANES and chips % 2 == 0
    sheared = shear_x(
        volume.reshape(plane_count, rows, LANES), x_offsets, x_fracs, first_plane, row // 2 % 2,
        col_local // LANES if wide else 1, 2 if wide else 1,
    )
    if not wide:
        return narrow_local(
            sheared[0].reshape(volume.shape), first_plane, z_offsets, z_fracs, y_offsets, y_fracs,
            slopes,
        )
    mixing, taps, chosen = weights(
        place, z_offsets, z_fracs, slopes, y_offsets, y_fracs, plane_count, depth, groups, shares
    )
    spare = plane_count - depth
    pair_first = jnp.where(place % 2 == 0, spare, 0)
    ends = [[], []]
    for i in range(shares - 1):
        ends[i % 2] += [(i, i + 1), (i + 1, i)]
    columns = [None] * groups
    for half, value in zip((1, 0), sheared):
        pair, other = (
            lax.ppermute(lax.dynamic_slice_in_dim(value, first, depth, 0), "gz", ends[parity])
            for parity, first in ((0, pair_first), (1, spare - pair_first))
        )
        mixed = shear_z(row, mixing, pair, value, other, chips)
        mixing, *mixed = lax.optimization_barrier((mixing, *mixed))
        for index in reversed(range(chips)):
            step = 2 * (2 * (index // 2) + half) + index % 2
            columns[step] = swap(mixed[index], "gy", step) if step else mixed[index]
    own, cross, *rotated = shear_y(row, taps, columns)
    landed = [swap(value, "gy", 2 * step + 2) for step, value in enumerate(rotated)]
    early = swap(cross, "gy", 1)
    tilted = project(place, row, chosen, (own, cross, *rotated), shares)
    tilted = [tilted[0]] + [swap(tilted[step], "gz", step) for step in range(1, shares)]
    tilted, landed = lax.optimization_barrier((tilted, landed[::-1]))
    landed = landed[::-1]
    late = swap(collect(landed), "gy", 1)
    rotated = finish(row, own, early, late, landed)
    return (
        rotated.reshape(plane_count, row_local, width_all),
        jnp.swapaxes(add(tilted), 1, 2),
    )


def solution(mesh):
    return jax.shard_map(
        local,
        mesh=mesh,
        in_specs=(P("gz", "gy", None), P(), P(), P("gy"), P("gy"), P("gy"), P("gy"), P()),
        out_specs=(P("gz", "gy", None), P("gz", "gy", None)),
        check_vma=False,
    )
```

```python
import functools

import jax
import jax.numpy as jnp
from jax import lax
from jax.experimental import pallas as pl
from jax.experimental.pallas import tpu as pltpu
from jax.sharding import PartitionSpec as P

TAPS = 64
OFFX = 64
OFFZ = 4
LANES = 128
BELOW = TAPS // 2 - 1
VMEM_LIMIT = 32 * 1024 * 1024

SMEM_SPEC = pl.BlockSpec(memory_space=pltpu.SMEM)
VMEM_SPEC = pl.BlockSpec(memory_space=pltpu.VMEM)


def tap_weight(offset, fraction):
    moved = offset.astype(jnp.float32) - fraction
    inside = (offset >= 1 - TAPS // 2) & (offset <= TAPS // 2)
    value = jnp.sinc(moved) * (0.5 + 0.5 * jnp.cos(jnp.pi * moved / (TAPS // 2 + 1)))
    return jnp.where(inside, value, jnp.zeros_like(value))


def tap_weight_in_kernel(offset, fraction):
    moved = offset.astype(jnp.float32) - fraction
    inside = (offset >= 1 - TAPS // 2) & (offset <= TAPS // 2)
    angle = jnp.pi * moved
    at_zero = moved == 0.0
    sinc = jnp.where(at_zero, 1.0, jnp.sin(angle) / jnp.where(at_zero, 1.0, angle))
    window = 0.5 + 0.5 * jnp.cos(angle / (TAPS // 2 + 1))
    return jnp.where(inside, sinc * window, 0.0)


def split_high_low(value):
    high = value.astype(jnp.bfloat16)
    low = (value - high.astype(jnp.float32)).astype(jnp.bfloat16)
    return high, low


def shear_x_kernel(
    classes, shifts_hbm, fracs_hbm, planes_hbm, *rest
):
    out_refs = rest[:-8]
    planes_ref, margin_ref, base_ref, lines_ref, shifts_ref, fracs_ref, small_sem, plane_sem = (
        rest[-8:]
    )
    plane_count, rows, lanes = planes_ref.shape
    per_class = rows // classes
    before, after = 8, margin_ref.shape[1] - rows - 8
    blocks = plane_sem.shape[0]
    per_block = plane_count // blocks
    small = [
        pltpu.make_async_copy(shifts_hbm, shifts_ref, small_sem.at[0]),
        pltpu.make_async_copy(fracs_hbm, fracs_ref, small_sem.at[1]),
    ]
    large = [
        pltpu.make_async_copy(
            planes_hbm.at[b * per_block:(b + 1) * per_block],
            planes_ref.at[b * per_block:(b + 1) * per_block],
            plane_sem.at[b],
        )
        for b in range(blocks)
    ]
    for copy in small + large:
        copy.start()
    line = lax.broadcasted_iota(jnp.int32, (lanes, lanes), 0)
    lane = lax.broadcasted_iota(jnp.int32, (lanes, lanes), 1)
    own_side = lane <= line
    tap = (lanes - lax.broadcasted_iota(jnp.int32, (plane_count, lanes), 1)) % lanes
    lane_of_row = lax.broadcasted_iota(jnp.int32, (per_class, lanes), 1)
    zeros = jnp.zeros((8, lanes), jnp.float32)
    first = lax.axis_index("gz") * plane_count
    side = lax.axis_index("gy") // 2 % 2
    first_lines = (2 - 2 * side, 2 * side)
    for copy in small:
        copy.wait()
    for z in range(plane_count):
        base_ref[z:z + 1, :] = jnp.full((1, lanes), fracs_ref[first + z], jnp.float32)
    base_ref[...] = tap_weight_in_kernel(tap - BELOW, base_ref[...])

    def one_plane(z, carry):
        margin_ref[z, 0:before, :] = zeros
        margin_ref[z, before:before + rows, :] = planes_ref[z]
        margin_ref[z, before + rows:before + rows + after, :] = zeros
        spread = pltpu.roll(
            jnp.broadcast_to(base_ref[pl.ds(z, 1), :], (lanes, lanes)),
            0, 1, stride=1, stride_axis=0,
        )
        own = jnp.where(own_side, spread, 0.0)
        band = jnp.concatenate([own, spread - own], axis=0)
        band = jnp.concatenate(split_high_low(band), axis=1)
        start = shifts_ref[first + z] - BELOW + before * lanes
        top = start // lanes
        back = lanes - (start - top * lanes)
        keep = lane_of_row < back
        turned = [
            pltpu.roll(margin_ref[z, pl.ds(top + i, per_class, stride=classes), :], back, 1)
            for i in range(classes + 2)
        ]
        lines = [jnp.where(keep, turned[i], turned[i + 1]) for i in range(classes + 1)]
        window = jnp.concatenate(
            [jnp.concatenate(lines[:-1], axis=0), jnp.concatenate(lines[1:], axis=0)], axis=1
        )
        window = jnp.concatenate(split_high_low(window), axis=0)
        product = jnp.dot(window, band, preferred_element_type=jnp.float32)
        product = product[:rows] + product[rows:]
        product = product[:, :lanes] + product[:, lanes:]
        if len(out_refs) == 1:
            out_refs[0][z] = product
            return carry
        lines_ref[z] = product
        quarter = rows // 4
        for out_ref, first_line in zip(out_refs, first_lines):
            for core in range(2):
                out_ref[z, core * quarter:(core + 1) * quarter, :] = lines_ref[
                    z, pl.ds(first_line + core, quarter, stride=4), :
                ]
        return carry

    for b in range(blocks):
        large[b].wait()
        lax.fori_loop(b * per_block, (b + 1) * per_block, one_plane, 0, unroll=True)


def shear_x(volume, x_offsets, x_fracs, classes, parts):
    plane_count, rows, lanes = volume.shape
    blocks = 2 if plane_count % 2 == 0 else 1
    return pl.pallas_call(
        functools.partial(shear_x_kernel, classes),
        out_shape=[
            jax.ShapeDtypeStruct((plane_count, rows // parts, lanes), jnp.float32)
        ] * parts,
        in_specs=[pl.BlockSpec(memory_space=pltpu.HBM)] * 3,
        out_specs=[VMEM_SPEC] * parts,
        scratch_shapes=[
            pltpu.VMEM(volume.shape, jnp.float32),
            pltpu.VMEM((plane_count, rows + 16, lanes), jnp.float32),
            pltpu.VMEM((plane_count, lanes), jnp.float32),
            pltpu.VMEM(volume.shape, jnp.float32),
            pltpu.SMEM(x_offsets.shape, jnp.int32),
            pltpu.SMEM(x_fracs.shape, jnp.float32),
            pltpu.SemaphoreType.DMA((2,)),
            pltpu.SemaphoreType.DMA((blocks,)),
        ],
        compiler_params=pltpu.CompilerParams(vmem_limit_bytes=VMEM_LIMIT),
        name="shear_x",
    )(
        *(pltpu.with_memory_space_constraint(v, pltpu.HBM) for v in (x_offsets, x_fracs, volume)),
    )


def weights_kernel(
    plane_count, depth, ny, shares, shift_ref, frac_ref, slopes_ref, shifts_ref, fracs_ref,
    mixing_ref, taps_ref, chosen_ref,
):
    reach = plane_count + 2 * depth
    place = lax.axis_index("gz")
    even = place % 2 == 0
    target = lax.broadcasted_iota(jnp.int32, (plane_count, reach), 0)
    column = lax.broadcasted_iota(jnp.int32, (plane_count, reach), 1)
    pair_start = jnp.where(even, plane_count, -depth)
    other_start = jnp.where(even, -depth, plane_count)
    source = jnp.where(
        column < depth,
        column + pair_start,
        jnp.where(
            column < depth + plane_count,
            column - depth,
            column - (depth + plane_count) + other_start,
        ),
    )
    mixing_ref[...] = tap_weight_in_kernel(source - target - shift_ref[0], frac_ref[0])
    lanes = taps_ref.shape[1]
    distance = lax.broadcasted_iota(jnp.int32, (2 * ny, lanes), 0) - (ny - 1)
    for tile in range(shifts_ref.shape[1] // lanes):
        part = slice(tile * lanes, (tile + 1) * lanes)
        taps_ref[tile * 2 * ny:(tile + 1) * 2 * ny, :] = tap_weight_in_kernel(
            distance - shifts_ref[:, part], fracs_ref[:, part]
        )
    total_planes = plane_count * shares
    tilts = slopes_ref.shape[0]
    span = ny // 4
    entry = lax.broadcasted_iota(jnp.int32, chosen_ref.shape, 0)
    plane = lax.broadcasted_iota(jnp.int32, chosen_ref.shape, 1) + place * plane_count
    lift = entry // tilts - span
    tilt = entry - (lift + span) * tilts
    slope = jnp.zeros_like(tilt)
    for t in range(tilts):
        slope = jnp.where(tilt == t, slopes_ref[t], slope)
    numerator = slope * (2 * plane - total_planes) * ny
    floor_at = lift * (16 * total_planes)
    chosen = (numerator >= floor_at) & (numerator < floor_at + 16 * total_planes)
    chosen_ref[...] = jnp.where(chosen, 1.0, 0.0)


def weights(
    z_offsets, z_fracs, slopes, y_offsets, y_fracs, plane_count, depth, ny, shares
):
    width = y_offsets.shape[0]
    lifts = 2 * (ny // 4) + 1
    return pl.pallas_call(
        functools.partial(weights_kernel, plane_count, depth, ny, shares),
        out_shape=(
            jax.ShapeDtypeStruct((plane_count, plane_count + 2 * depth), jnp.float32),
            jax.ShapeDtypeStruct((width // LANES * 2 * ny, LANES), jnp.float32),
            jax.ShapeDtypeStruct((lifts * slopes.shape[0], plane_count), jnp.float32),
        ),
        in_specs=[SMEM_SPEC] * 3 + [VMEM_SPEC] * 2,
        out_specs=(VMEM_SPEC, VMEM_SPEC, VMEM_SPEC),
        compiler_params=pltpu.CompilerParams(vmem_limit_bytes=VMEM_LIMIT),
        name="weights",
    )(
        z_offsets, z_fracs, slopes,
        y_offsets.reshape(1, width), y_fracs.reshape(1, width),
    )


def shear_z_kernel(
    plane_count, depth, chips, mixing_ref, pair_ref, own_ref, other_ref, *outs
):
    lanes = own_ref.shape[1]
    rows = own_ref.shape[0] // plane_count
    half = chips // 2
    tiles = rows // chips
    pair = 2 if tiles % 2 == 0 else 1
    high, low = split_high_low(mixing_ref[...])
    mixing = jnp.concatenate(
        [jnp.concatenate([high, high], axis=1), jnp.concatenate([low, low], axis=1)], axis=0
    )
    own_row = lax.axis_index("gy")
    core, chip_pair = own_row % 2, own_row // 4
    for index, out_ref in enumerate(outs):
        first = (core ^ (index % 2)) * (rows // 2) + (chip_pair ^ (index // 2))
        for tile in range(0, tiles, pair):
            columns = []
            for i in range(tile, tile + pair):
                row = first + i * half
                columns.append(
                    jnp.concatenate(
                        [
                            pair_ref[pl.ds(row, depth, stride=rows), :],
                            own_ref[pl.ds(row, plane_count, stride=rows), :],
                            other_ref[pl.ds(row, depth, stride=rows), :],
                        ],
                        axis=0,
                    )
                )
            stack = jnp.concatenate(columns, axis=1)
            stack = jnp.concatenate(split_high_low(stack), axis=0)
            product = jnp.dot(mixing, stack, preferred_element_type=jnp.float32)
            out_ref[:, tile * lanes:(tile + pair) * lanes] = (
                product[:plane_count] + product[plane_count:]
            )


def shear_z(mixing, pair, own, other, chips):
    plane_count, rows, lanes = own.shape
    depth = pair.shape[0]
    width = rows * lanes // chips
    return pl.pallas_call(
        functools.partial(shear_z_kernel, plane_count, depth, chips),
        out_shape=[jax.ShapeDtypeStruct((plane_count, width), jnp.float32)] * chips,
        in_specs=[VMEM_SPEC] * 4,
        out_specs=[VMEM_SPEC] * chips,
        compiler_params=pltpu.CompilerParams(vmem_limit_bytes=VMEM_LIMIT),
        name="shear_z",
    )(mixing, *(value.reshape(-1, lanes) for value in (pair, own, other)))


def start_order(ny):
    return sorted(range(ny), key=lambda slot: (-(slot // 2 % 2), -(slot // 4), slot % 2, -slot))


def shear_y_kernel(ny, taps_ref, *refs):
    in_refs, out_refs = refs[:ny], refs[ny:]
    in_refs = [in_refs[start_order(ny).index(slot)] for slot in range(ny)]
    plane_count, width = in_refs[0].shape
    row = lax.axis_index("gy")
    for tile in range(width // LANES):
        lanes = slice(tile * LANES, (tile + 1) * LANES)
        first = tile * 2 * ny + ny - 1
        for target in range(ny):
            weight = [
                jnp.broadcast_to(
                    taps_ref[pl.ds(first + (row ^ source) - (row ^ target), 1), :], (8, LANES)
                )
                for source in range(ny)
            ]
            for block in range(plane_count // 8):
                planes = slice(block * 8, (block + 1) * 8)
                value = weight[0] * in_refs[0][planes, lanes]
                for source in range(1, ny):
                    value = value + weight[source] * in_refs[source][planes, lanes]
                if target < 2:
                    out_refs[target][planes, lanes] = value
                elif target < ny - 2:
                    out_refs[target // 2 + 1][target % 2, planes, lanes] = value
                else:
                    out_refs[target - ny][planes, lanes] = value


def shear_y(taps, columns):
    ny = len(columns)
    shape = columns[0].shape
    single = [jax.ShapeDtypeStruct(shape, jnp.float32)] * 2
    out_shape = single + [jax.ShapeDtypeStruct((2, *shape), jnp.float32)] * (ny // 2 - 2) + single
    return pl.pallas_call(
        functools.partial(shear_y_kernel, ny),
        out_shape=out_shape,
        in_specs=[VMEM_SPEC] * (1 + ny),
        out_specs=[VMEM_SPEC] * len(out_shape),
        compiler_params=pltpu.CompilerParams(vmem_limit_bytes=VMEM_LIMIT),
        name="shear_y",
    )(taps, *(columns[slot] for slot in start_order(ny)))


def collect_kernel(*refs):
    count = len(refs) // 2
    for source, target in zip(refs[:count], refs[count:]):
        target[...] = source[1]


def collect(landed):
    return pl.pallas_call(
        collect_kernel,
        out_shape=[jax.ShapeDtypeStruct(v.shape[1:], jnp.float32) for v in landed],
        in_specs=[VMEM_SPEC] * len(landed),
        out_specs=[VMEM_SPEC] * len(landed),
        compiler_params=pltpu.CompilerParams(vmem_limit_bytes=VMEM_LIMIT),
        name="collect",
    )(*landed)


def project_kernel(chips, tilts, chosen_ref, *refs):
    place, own_row = lax.axis_index("gz"), lax.axis_index("gy")
    in_refs, share_refs, totals_ref = refs[:chips + 2], refs[chips + 2:-1], refs[-1]
    ny, shares = 2 * chips, len(share_refs)
    plane_count, width = in_refs[0].shape
    total_planes = plane_count * shares
    span = ny // 4
    tiles = width // LANES
    lifts = 2 * span + 1
    chosen = chosen_ref[...].astype(jnp.bfloat16)
    chosen = jnp.concatenate([chosen, chosen], axis=1)

    per_tile = (ny + 2 * span) * tilts
    totals_ref[...] = jnp.zeros(totals_ref.shape, jnp.float32)
    for source in range(ny):
        if source < 2:
            value = in_refs[source][...]
        elif source < ny - 2:
            value = in_refs[source // 2 + 1][source % 2]
        else:
            value = in_refs[source - ny][...]
        sums = jnp.dot(
            chosen,
            jnp.concatenate(split_high_low(value), axis=0),
            preferred_element_type=jnp.float32,
        )
        row = own_row ^ source
        for l in range(lifts):
            for tile in range(tiles):
                start = pl.multiple_of(tile * per_tile + (row + 2 * span - l) * tilts, tilts)
                totals_ref[pl.ds(start, tilts), :] += sums[
                    l * tilts:(l + 1) * tilts, tile * LANES:(tile + 1) * LANES
                ]
    per_share = tilts // shares
    for step, share_ref in enumerate(share_refs):
        tilt = (place ^ step) * per_share
        for u in range(per_share):
            for tile in range(tiles):
                share_ref[u, :, tile * LANES:(tile + 1) * LANES] = (
                    totals_ref[
                        pl.ds(tile * per_tile + span * tilts + tilt + u, ny, stride=tilts), :
                    ]
                    * total_planes ** (-0.5)
                )


def project(chosen, rotated, shares):
    chips = len(rotated) - 2
    ny = 2 * chips
    tilts = chosen.shape[0] // (2 * (ny // 4) + 1)
    width = rotated[0].shape[1]
    share = jax.ShapeDtypeStruct((tilts // shares, ny, width), jnp.float32)
    totals = (width // LANES * (ny + 2 * (ny // 4)) * tilts, LANES)
    return pl.pallas_call(
        functools.partial(project_kernel, chips, tilts),
        out_shape=[share] * shares,
        in_specs=[VMEM_SPEC] * (1 + len(rotated)),
        out_specs=[VMEM_SPEC] * shares,
        scratch_shapes=[pltpu.VMEM(totals, jnp.float32)],
        compiler_params=pltpu.CompilerParams(vmem_limit_bytes=VMEM_LIMIT),
        name="project",
    )(chosen, *rotated)


def finish_kernel(slots, *refs):
    row = lax.axis_index("gy")
    rotated_ref, sources = refs[-1], refs[:len(slots)]
    rows = rotated_ref.shape[0] // sources[0].shape[-2]
    for ref, (slot, index) in zip(sources, slots):
        plane_count, width = ref.shape[-2:]
        per_group = width // LANES
        start = (row ^ slot) * per_group
        source = ref if index is None else ref.at[index]
        for tile in range(per_group):
            rotated_ref[pl.ds(start + tile, plane_count, stride=rows), :] = source[
                :, tile * LANES:(tile + 1) * LANES
            ]


def finish(own, early, landed, late, direct):
    chips = len(landed) + 2
    plane_count, width = own.shape
    slots = [(0, None), (1, None)]
    slots += [(2 * step, 0) for step in range(1, chips - 1)]
    slots += [(2 * step + 1, None) for step in range(1, chips - 1)]
    slots += [(2 * chips - 2, None), (2 * chips - 1, None)]
    return pl.pallas_call(
        functools.partial(finish_kernel, slots),
        out_shape=jax.ShapeDtypeStruct(
            (plane_count * 2 * chips * width // LANES, LANES), jnp.float32
        ),
        in_specs=[VMEM_SPEC] * len(slots),
        out_specs=VMEM_SPEC,
        compiler_params=pltpu.CompilerParams(vmem_limit_bytes=VMEM_LIMIT),
        name="finish",
    )(own, early, *landed, *late, *direct)


def add_kernel(*refs):
    total = refs[0][...]
    for ref in refs[1:-1]:
        total = total + ref[...]
    refs[-1][...] = total


def add(shares):
    return pl.pallas_call(
        add_kernel,
        out_shape=jax.ShapeDtypeStruct(shares[0].shape, jnp.float32),
        in_specs=[VMEM_SPEC] * len(shares),
        out_specs=VMEM_SPEC,
        compiler_params=pltpu.CompilerParams(vmem_limit_bytes=VMEM_LIMIT),
        name="add_shares",
    )(*shares)


def with_halo(value, sides, width):
    for axis, dim in sides:
        peers, length = (lax.axis_size(axis), value.shape[dim])
        up = [(i, (i + 1) % peers) for i in range(peers - 1)]
        down = [(j, i) for i, j in up]
        last = lax.slice_in_dim(value, length - width, length, axis=dim)
        first = lax.slice_in_dim(value, 0, width, axis=dim)
        before = lax.ppermute(last, axis, up)
        after = lax.ppermute(first, axis, down)
        value = jnp.concatenate([before, value, after], axis=dim)
    return value


def narrow_local(sheared_x, first_plane, z_offsets, z_fracs, y_offsets, y_fracs, slopes):
    depth = TAPS // 2 + OFFZ
    plane_count, row_local, width_all = sheared_x.shape
    groups = lax.axis_size("gy")
    col_local = width_all // groups
    extended = with_halo(sheared_x, (("gz", 0),), depth)
    plane_index = jnp.arange(plane_count, dtype=jnp.int32)[:, None]
    source_index = jnp.arange(plane_count + 2 * depth, dtype=jnp.int32)[None, :]
    mixing = tap_weight(
        (source_index - depth - plane_index)[None] - z_offsets[:, None, None],
        z_fracs[:, None, None],
    )
    blocked = extended.reshape(plane_count + 2 * depth, row_local, groups, col_local)
    outgoing = jnp.einsum("rzj,jrgc->grcz", mixing, blocked, precision=lax.Precision.HIGHEST)
    outgoing = outgoing.reshape(groups, 1, row_local * col_local * plane_count)
    arrived = lax.all_to_all(outgoing, "gy", split_axis=0, concat_axis=1, tiled=True)
    row_total = groups * row_local
    columns = arrived.reshape(row_total, col_local, plane_count)
    target_row = jnp.arange(row_total, dtype=jnp.int32)[:, None]
    source_row = jnp.arange(row_total, dtype=jnp.int32)[None, :]
    operator = tap_weight(
        (source_row - target_row)[None] - y_offsets[:, None, None], y_fracs[:, None, None]
    )
    rotated_cols = jnp.einsum("cij,jcz->zci", operator, columns, precision=lax.Precision.HIGHEST)
    span_pad = row_total // 4
    total_planes = plane_count * lax.axis_size("gz")
    global_planes = first_plane + jnp.arange(plane_count, dtype=jnp.int32)
    padded_cols = jnp.pad(rotated_cols, ((0, 0), (0, 0), (span_pad, span_pad)))
    per_tilt = []
    for tilt_index in range(slopes.shape[0]):
        lifts = (
            slopes[tilt_index]
            * (2 * global_planes - total_planes)
            * row_total
            // (16 * total_planes)
        )
        moved = jax.vmap(
            lambda one_plane, lift_one: lax.dynamic_slice_in_dim(
                one_plane, span_pad + lift_one, row_total, 1
            )
        )(padded_cols, lifts)
        per_tilt.append(jnp.sum(moved, axis=0))
    partial_terms = jnp.stack(per_tilt) * total_planes ** (-0.5)
    projections = lax.psum_scatter(partial_terms, "gz", scatter_dimension=0, tiled=True)
    returning = rotated_cols.reshape(plane_count, col_local, groups, row_local)
    returning = jnp.transpose(returning, (2, 3, 1, 0)).reshape(
        groups, 1, row_local * col_local * plane_count
    )
    landed = lax.all_to_all(returning, "gy", split_axis=0, concat_axis=1, tiled=True)
    landed = landed.reshape(groups, row_local, col_local, plane_count)
    rotated = jnp.transpose(landed, (3, 1, 0, 2)).reshape(
        plane_count, row_local, groups * col_local
    )
    return (rotated, projections)


def swap(value, axis, step):
    return lax.ppermute(value, axis, [(i, i ^ step) for i in range(lax.axis_size(axis))])


def local(volume, x_offsets, x_fracs, z_offsets, z_fracs, y_offsets, y_fracs, slopes):
    depth = TAPS // 2 + OFFZ
    plane_count, row_local, width_all = volume.shape
    groups, shares = lax.axis_size("gy"), lax.axis_size("gz")
    assert row_local == 1 and width_all % LANES == 0
    rows = width_all // LANES
    col_local = width_all // groups
    place = lax.axis_index("gz").astype(jnp.int32)
    first_plane = place * plane_count
    chips = groups // 2
    even = chips % 4 == 0 and groups & (groups - 1) == 0 and shares & (shares - 1) == 0
    wide = even and col_local % LANES == 0 and col_local > LANES and slopes.shape[0] % shares == 0
    sheared = shear_x(
        volume.reshape(plane_count, rows, LANES), x_offsets, x_fracs,
        col_local // LANES if wide else 1, 2 if wide else 1,
    )
    if not wide:
        return narrow_local(
            sheared[0].reshape(volume.shape), first_plane, z_offsets, z_fracs, y_offsets, y_fracs,
            slopes,
        )
    mixing, taps, chosen = weights(
        z_offsets, z_fracs, slopes, y_offsets, y_fracs, plane_count, depth, groups, shares
    )
    spare = plane_count - depth
    pair_first = jnp.where(place % 2 == 0, spare, 0)
    ends = [[], []]
    for i in range(shares - 1):
        ends[i % 2] += [(i, i + 1), (i + 1, i)]
    columns = [None] * groups
    for half, value in zip((1, 0), sheared):
        pair, other = (
            lax.ppermute(lax.dynamic_slice_in_dim(value, first, depth, 0), "gz", ends[parity])
            for parity, first in ((0, pair_first), (1, spare - pair_first))
        )
        mixed = shear_z(mixing, pair, value, other, chips)
        mixing, *mixed = lax.optimization_barrier((mixing, *mixed))
        for index in reversed(range(chips)):
            step = 2 * (2 * (index // 2) + half) + index % 2
            columns[step] = swap(mixed[index], "gy", step) if step else mixed[index]
    own, cross, *rotated = shear_y(taps, columns)
    pairs, direct = rotated[:-2], rotated[-2:]
    landed = [swap(value, "gy", 2 * step + 2) for step, value in enumerate(pairs)]
    direct = [swap(value, "gy", groups - 2 + core) for core, value in enumerate(direct)]
    early = swap(cross, "gy", 1)
    tilted = project(chosen, (own, cross, *rotated), shares)
    tilted = [swap(tilted[step], "gz", step) for step in range(shares - 1, 0, -1)] + [tilted[0]]
    late = [swap(value, "gy", 1) for value in collect(landed)]
    tilted, direct, late = lax.optimization_barrier((tilted, direct, late))
    rotated = finish(own, early, landed, late, direct)
    return (
        rotated.reshape(plane_count, row_local, width_all),
        jnp.swapaxes(add(tilted), 1, 2),
    )


def solution(mesh):
    return jax.shard_map(
        local,
        mesh=mesh,
        in_specs=(P("gz", "gy", None), P(), P(), P("gy"), P("gy"), P("gy"), P("gy"), P()),
        out_specs=(P("gz", "gy", None), P("gz", "gy", None)),
        check_vma=False,
    )
```

```python
import functools

import jax
import jax.numpy as jnp
from jax import lax
from jax.experimental import pallas as pl
from jax.experimental.pallas import tpu as pltpu
from jax.sharding import PartitionSpec as P

TAPS = 64
OFFX = 64
OFFZ = 4
LANES = 128
BELOW = TAPS // 2 - 1
VMEM_LIMIT = 32 * 1024 * 1024

SMEM_SPEC = pl.BlockSpec(memory_space=pltpu.SMEM)
VMEM_SPEC = pl.BlockSpec(memory_space=pltpu.VMEM)


def tap_weight(offset, fraction):
    moved = offset.astype(jnp.float32) - fraction
    inside = (offset >= 1 - TAPS // 2) & (offset <= TAPS // 2)
    value = jnp.sinc(moved) * (0.5 + 0.5 * jnp.cos(jnp.pi * moved / (TAPS // 2 + 1)))
    return jnp.where(inside, value, jnp.zeros_like(value))


def tap_weight_in_kernel(offset, fraction):
    moved = offset.astype(jnp.float32) - fraction
    inside = (offset >= 1 - TAPS // 2) & (offset <= TAPS // 2)
    angle = jnp.pi * moved
    at_zero = moved == 0.0
    sinc = jnp.where(at_zero, 1.0, jnp.sin(angle) / jnp.where(at_zero, 1.0, angle))
    window = 0.5 + 0.5 * jnp.cos(angle / (TAPS // 2 + 1))
    return jnp.where(inside, sinc * window, 0.0)


def split_high_low(value):
    high = value.astype(jnp.bfloat16)
    low = (value - high.astype(jnp.float32)).astype(jnp.bfloat16)
    return high, low


def shear_x_kernel(
    classes, shifts_hbm, fracs_hbm, planes_hbm, *rest
):
    out_refs = rest[:-8]
    planes_ref, margin_ref, base_ref, lines_ref, shifts_ref, fracs_ref, small_sem, plane_sem = (
        rest[-8:]
    )
    plane_count, rows, lanes = planes_ref.shape
    per_class = rows // classes
    before, after = 8, margin_ref.shape[1] - rows - 8
    blocks = plane_sem.shape[0]
    per_block = plane_count // blocks
    small = [
        pltpu.make_async_copy(shifts_hbm, shifts_ref, small_sem.at[0]),
        pltpu.make_async_copy(fracs_hbm, fracs_ref, small_sem.at[1]),
    ]
    large = [
        pltpu.make_async_copy(
            planes_hbm.at[b * per_block:(b + 1) * per_block],
            planes_ref.at[b * per_block:(b + 1) * per_block],
            plane_sem.at[b],
        )
        for b in range(blocks)
    ]
    for copy in small + large:
        copy.start()
    line = lax.broadcasted_iota(jnp.int32, (lanes, lanes), 0)
    lane = lax.broadcasted_iota(jnp.int32, (lanes, lanes), 1)
    own_side = lane <= line
    tap = (lanes - lax.broadcasted_iota(jnp.int32, (plane_count, lanes), 1)) % lanes
    lane_of_row = lax.broadcasted_iota(jnp.int32, (per_class, lanes), 1)
    zeros = jnp.zeros((8, lanes), jnp.float32)
    first = lax.axis_index("gz") * plane_count
    side = lax.axis_index("gy") // 2 % 2
    first_lines = (2 - 2 * side, 2 * side)
    for copy in small:
        copy.wait()
    for z in range(plane_count):
        base_ref[z:z + 1, :] = jnp.full((1, lanes), fracs_ref[first + z], jnp.float32)
    base_ref[...] = tap_weight_in_kernel(tap - BELOW, base_ref[...])

    def one_plane(z, carry):
        margin_ref[z, 0:before, :] = zeros
        margin_ref[z, before:before + rows, :] = planes_ref[z]
        margin_ref[z, before + rows:before + rows + after, :] = zeros
        spread = pltpu.roll(
            jnp.broadcast_to(base_ref[pl.ds(z, 1), :], (lanes, lanes)),
            0, 1, stride=1, stride_axis=0,
        )
        own = jnp.where(own_side, spread, 0.0)
        band = jnp.concatenate([own, spread - own], axis=0)
        band = jnp.concatenate(split_high_low(band), axis=1)
        start = shifts_ref[first + z] - BELOW + before * lanes
        top = start // lanes
        back = lanes - (start - top * lanes)
        keep = lane_of_row < back
        turned = [
            pltpu.roll(margin_ref[z, pl.ds(top + i, per_class, stride=classes), :], back, 1)
            for i in range(classes + 2)
        ]
        lines = [jnp.where(keep, turned[i], turned[i + 1]) for i in range(classes + 1)]
        window = jnp.concatenate(
            [jnp.concatenate(lines[:-1], axis=0), jnp.concatenate(lines[1:], axis=0)], axis=1
        )
        window = jnp.concatenate(split_high_low(window), axis=0)
        product = jnp.dot(window, band, preferred_element_type=jnp.float32)
        product = product[:rows] + product[rows:]
        product = product[:, :lanes] + product[:, lanes:]
        if len(out_refs) == 1:
            out_refs[0][z] = product
            return carry
        lines_ref[z] = product
        quarter = rows // 4
        for out_ref, first_line in zip(out_refs, first_lines):
            for core in range(2):
                out_ref[z, core * quarter:(core + 1) * quarter, :] = lines_ref[
                    z, pl.ds(first_line + core, quarter, stride=4), :
                ]
        return carry

    for b in range(blocks):
        large[b].wait()
        lax.fori_loop(b * per_block, (b + 1) * per_block, one_plane, 0, unroll=True)


def shear_x(volume, x_offsets, x_fracs, classes, parts):
    plane_count, rows, lanes = volume.shape
    blocks = 2 if plane_count % 2 == 0 else 1
    return pl.pallas_call(
        functools.partial(shear_x_kernel, classes),
        out_shape=[
            jax.ShapeDtypeStruct((plane_count, rows // parts, lanes), jnp.float32)
        ] * parts,
        in_specs=[pl.BlockSpec(memory_space=pltpu.HBM)] * 3,
        out_specs=[VMEM_SPEC] * parts,
        scratch_shapes=[
            pltpu.VMEM(volume.shape, jnp.float32),
            pltpu.VMEM((plane_count, rows + 16, lanes), jnp.float32),
            pltpu.VMEM((plane_count, lanes), jnp.float32),
            pltpu.VMEM(volume.shape, jnp.float32),
            pltpu.SMEM(x_offsets.shape, jnp.int32),
            pltpu.SMEM(x_fracs.shape, jnp.float32),
            pltpu.SemaphoreType.DMA((2,)),
            pltpu.SemaphoreType.DMA((blocks,)),
        ],
        compiler_params=pltpu.CompilerParams(vmem_limit_bytes=VMEM_LIMIT),
        name="shear_x",
    )(
        *(pltpu.with_memory_space_constraint(v, pltpu.HBM) for v in (x_offsets, x_fracs, volume)),
    )


def weights_kernel(
    plane_count, depth, ny, shares, shift_ref, frac_ref, slopes_ref, shifts_ref, fracs_ref,
    mixing_ref, taps_ref, chosen_ref,
):
    reach = plane_count + 2 * depth
    place = lax.axis_index("gz")
    even = place % 2 == 0
    target = lax.broadcasted_iota(jnp.int32, (plane_count, reach), 0)
    column = lax.broadcasted_iota(jnp.int32, (plane_count, reach), 1)
    pair_start = jnp.where(even, plane_count, -depth)
    other_start = jnp.where(even, -depth, plane_count)
    source = jnp.where(
        column < depth,
        column + pair_start,
        jnp.where(
            column < depth + plane_count,
            column - depth,
            column - (depth + plane_count) + other_start,
        ),
    )
    mixing_ref[...] = tap_weight_in_kernel(source - target - shift_ref[0], frac_ref[0])
    lanes = taps_ref.shape[1]
    distance = lax.broadcasted_iota(jnp.int32, (2 * ny, lanes), 0) - (ny - 1)
    for tile in range(shifts_ref.shape[1] // lanes):
        part = slice(tile * lanes, (tile + 1) * lanes)
        taps_ref[tile * 2 * ny:(tile + 1) * 2 * ny, :] = tap_weight_in_kernel(
            distance - shifts_ref[:, part], fracs_ref[:, part]
        )
    total_planes = plane_count * shares
    tilts = slopes_ref.shape[0]
    span = ny // 4
    entry = lax.broadcasted_iota(jnp.int32, chosen_ref.shape, 0)
    plane = lax.broadcasted_iota(jnp.int32, chosen_ref.shape, 1) + place * plane_count
    lift = entry // tilts - span
    tilt = entry - (lift + span) * tilts
    slope = jnp.zeros_like(tilt)
    for t in range(tilts):
        slope = jnp.where(tilt == t, slopes_ref[t], slope)
    numerator = slope * (2 * plane - total_planes) * ny
    floor_at = lift * (16 * total_planes)
    chosen = (numerator >= floor_at) & (numerator < floor_at + 16 * total_planes)
    chosen_ref[...] = jnp.where(chosen, 1.0, 0.0)


def weights(
    z_offsets, z_fracs, slopes, y_offsets, y_fracs, plane_count, depth, ny, shares
):
    width = y_offsets.shape[0]
    lifts = 2 * (ny // 4) + 1
    return pl.pallas_call(
        functools.partial(weights_kernel, plane_count, depth, ny, shares),
        out_shape=(
            jax.ShapeDtypeStruct((plane_count, plane_count + 2 * depth), jnp.float32),
            jax.ShapeDtypeStruct((width // LANES * 2 * ny, LANES), jnp.float32),
            jax.ShapeDtypeStruct((lifts * slopes.shape[0], plane_count), jnp.float32),
        ),
        in_specs=[SMEM_SPEC] * 3 + [VMEM_SPEC] * 2,
        out_specs=(VMEM_SPEC, VMEM_SPEC, VMEM_SPEC),
        compiler_params=pltpu.CompilerParams(vmem_limit_bytes=VMEM_LIMIT),
        name="weights",
    )(
        z_offsets, z_fracs, slopes,
        y_offsets.reshape(1, width), y_fracs.reshape(1, width),
    )


def shear_z_kernel(
    plane_count, depth, chips, mixing_ref, pair_ref, own_ref, other_ref, *outs
):
    lanes = own_ref.shape[1]
    rows = own_ref.shape[0] // plane_count
    half = chips // 2
    tiles = rows // chips
    pair = 2 if tiles % 2 == 0 else 1
    high, low = split_high_low(mixing_ref[...])
    mixing = jnp.concatenate(
        [jnp.concatenate([high, high], axis=1), jnp.concatenate([low, low], axis=1)], axis=0
    )
    own_row = lax.axis_index("gy")
    core, chip_pair = own_row % 2, own_row // 4
    for index, out_ref in enumerate(outs):
        first = (core ^ (index % 2)) * (rows // 2) + (chip_pair ^ (index // 2))
        for tile in range(0, tiles, pair):
            columns = []
            for i in range(tile, tile + pair):
                row = first + i * half
                columns.append(
                    jnp.concatenate(
                        [
                            pair_ref[pl.ds(row, depth, stride=rows), :],
                            own_ref[pl.ds(row, plane_count, stride=rows), :],
                            other_ref[pl.ds(row, depth, stride=rows), :],
                        ],
                        axis=0,
                    )
                )
            stack = jnp.concatenate(columns, axis=1)
            stack = jnp.concatenate(split_high_low(stack), axis=0)
            product = jnp.dot(mixing, stack, preferred_element_type=jnp.float32)
            out_ref[:, tile * lanes:(tile + pair) * lanes] = (
                product[:plane_count] + product[plane_count:]
            )


def shear_z(mixing, pair, own, other, chips):
    plane_count, rows, lanes = own.shape
    depth = pair.shape[0]
    width = rows * lanes // chips
    return pl.pallas_call(
        functools.partial(shear_z_kernel, plane_count, depth, chips),
        out_shape=[jax.ShapeDtypeStruct((plane_count, width), jnp.float32)] * chips,
        in_specs=[VMEM_SPEC] * 4,
        out_specs=[VMEM_SPEC] * chips,
        compiler_params=pltpu.CompilerParams(vmem_limit_bytes=VMEM_LIMIT),
        name="shear_z",
    )(mixing, *(value.reshape(-1, lanes) for value in (pair, own, other)))


def start_order(ny):
    return sorted(range(ny), key=lambda slot: (-(slot // 2 % 2), -(slot // 4), slot % 2, -slot))


def shear_y_kernel(ny, taps_ref, *refs):
    in_refs, out_refs = refs[:ny], refs[ny:]
    in_refs = [in_refs[start_order(ny).index(slot)] for slot in range(ny)]
    plane_count, width = in_refs[0].shape
    row = lax.axis_index("gy")
    tiles = width // LANES
    for tile in range(tiles):
        lanes = slice(tile * LANES, (tile + 1) * LANES)
        first = tile * 2 * ny + ny - 1
        for target in range(ny):
            weight = [
                jnp.broadcast_to(
                    taps_ref[pl.ds(first + (row ^ source) - (row ^ target), 1), :], (8, LANES)
                )
                for source in range(ny)
            ]
            for block in range(plane_count // 8):
                planes = slice(block * 8, (block + 1) * 8)
                value = weight[0] * in_refs[0][planes, lanes]
                for source in range(1, ny):
                    value = value + weight[source] * in_refs[source][planes, lanes]
                lines = pl.ds(block * 8 * tiles + tile, 8, stride=tiles)
                if target < 2:
                    out_refs[target][lines, :] = value
                elif target < ny - 2:
                    out_refs[target // 2 + 1][target % 2, lines, :] = value
                else:
                    out_refs[target - ny][lines, :] = value


def shear_y(taps, columns):
    ny = len(columns)
    plane_count, width = columns[0].shape
    shape = (plane_count * width // LANES, LANES)
    single = [jax.ShapeDtypeStruct(shape, jnp.float32)] * 2
    out_shape = single + [jax.ShapeDtypeStruct((2, *shape), jnp.float32)] * (ny // 2 - 2) + single
    return pl.pallas_call(
        functools.partial(shear_y_kernel, ny),
        out_shape=out_shape,
        in_specs=[VMEM_SPEC] * (1 + ny),
        out_specs=[VMEM_SPEC] * len(out_shape),
        compiler_params=pltpu.CompilerParams(vmem_limit_bytes=VMEM_LIMIT),
        name="shear_y",
    )(taps, *(columns[slot] for slot in start_order(ny)))


def collect_kernel(*refs):
    count = len(refs) // 2
    for source, target in zip(refs[:count], refs[count:]):
        target[...] = source[1]


def collect(landed):
    return pl.pallas_call(
        collect_kernel,
        out_shape=[jax.ShapeDtypeStruct(v.shape[1:], jnp.float32) for v in landed],
        in_specs=[VMEM_SPEC] * len(landed),
        out_specs=[VMEM_SPEC] * len(landed),
        compiler_params=pltpu.CompilerParams(vmem_limit_bytes=VMEM_LIMIT),
        name="collect",
    )(*landed)


def project_kernel(chips, tilts, chosen_ref, *refs):
    place, own_row = lax.axis_index("gz"), lax.axis_index("gy")
    in_refs, share_refs, totals_ref = refs[:chips + 2], refs[chips + 2:-1], refs[-1]
    ny, shares = 2 * chips, len(share_refs)
    plane_count = chosen_ref.shape[1]
    total_planes = plane_count * shares
    span = ny // 4
    tiles = in_refs[0].shape[0] // plane_count
    lifts = 2 * span + 1
    chosen = chosen_ref[...].astype(jnp.bfloat16)
    chosen = jnp.concatenate([chosen, chosen], axis=1)

    per_tile = (ny + 2 * span) * tilts
    totals_ref[...] = jnp.zeros(totals_ref.shape, jnp.float32)
    for source in range(ny):
        if source < 2:
            ref = in_refs[source]
        elif source < ny - 2:
            ref = in_refs[source // 2 + 1].at[source % 2]
        else:
            ref = in_refs[source - ny]
        value = jnp.concatenate(
            [ref[pl.ds(tile, plane_count, stride=tiles), :] for tile in range(tiles)], axis=1
        )
        sums = jnp.dot(
            chosen,
            jnp.concatenate(split_high_low(value), axis=0),
            preferred_element_type=jnp.float32,
        )
        row = own_row ^ source
        for l in range(lifts):
            for tile in range(tiles):
                start = pl.multiple_of(tile * per_tile + (row + 2 * span - l) * tilts, tilts)
                totals_ref[pl.ds(start, tilts), :] += sums[
                    l * tilts:(l + 1) * tilts, tile * LANES:(tile + 1) * LANES
                ]
    per_share = tilts // shares
    for step, share_ref in enumerate(share_refs):
        tilt = (place ^ step) * per_share
        for u in range(per_share):
            for tile in range(tiles):
                share_ref[u, :, tile * LANES:(tile + 1) * LANES] = (
                    totals_ref[
                        pl.ds(tile * per_tile + span * tilts + tilt + u, ny, stride=tilts), :
                    ]
                    * total_planes ** (-0.5)
                )


def project(chosen, rotated, shares):
    chips = len(rotated) - 2
    ny = 2 * chips
    tilts = chosen.shape[0] // (2 * (ny // 4) + 1)
    width = rotated[0].shape[0] // chosen.shape[1] * LANES
    share = jax.ShapeDtypeStruct((tilts // shares, ny, width), jnp.float32)
    totals = (width // LANES * (ny + 2 * (ny // 4)) * tilts, LANES)
    return pl.pallas_call(
        functools.partial(project_kernel, chips, tilts),
        out_shape=[share] * shares,
        in_specs=[VMEM_SPEC] * (1 + len(rotated)),
        out_specs=[VMEM_SPEC] * shares,
        scratch_shapes=[pltpu.VMEM(totals, jnp.float32)],
        compiler_params=pltpu.CompilerParams(vmem_limit_bytes=VMEM_LIMIT),
        name="project",
    )(chosen, *rotated)


def finish_kernel(slots, *refs):
    sources, share_refs = refs[:len(slots)], refs[len(slots):-3]
    rotated_ref, projections_ref, sems = refs[-3:]
    row = lax.axis_index("gy")
    copies = [
        pltpu.make_async_copy(
            ref if index is None else ref.at[index], rotated_ref.at[:, row ^ slot], sems.at[slot]
        )
        for ref, (slot, index) in zip(sources, slots)
    ]
    for copy in copies:
        copy.start()
    total = share_refs[0][...]
    for share_ref in share_refs[1:]:
        total = total + share_ref[...]
    projections_ref[...] = total
    for copy in copies:
        copy.wait()


def finish(own, early, landed, late, direct, shares, plane_count):
    chips = len(landed) + 2
    slots = [(0, None), (1, None)]
    slots += [(2 * step, 0) for step in range(1, chips - 1)]
    slots += [(2 * step + 1, None) for step in range(1, chips - 1)]
    slots += [(2 * chips - 2, None), (2 * chips - 1, None)]
    tiles = own.shape[0] // plane_count
    sources = [
        value.reshape(*value.shape[:-2], plane_count, tiles, LANES)
        for value in (own, early, *landed, *late, *direct)
    ]
    return pl.pallas_call(
        functools.partial(finish_kernel, slots),
        out_shape=(
            jax.ShapeDtypeStruct((plane_count, 2 * chips, tiles, LANES), jnp.float32),
            jax.ShapeDtypeStruct(shares[0].shape, jnp.float32),
        ),
        in_specs=[VMEM_SPEC] * (len(slots) + len(shares)),
        out_specs=(pl.BlockSpec(memory_space=pltpu.HBM), VMEM_SPEC),
        scratch_shapes=[pltpu.SemaphoreType.DMA((2 * chips,))],
        compiler_params=pltpu.CompilerParams(vmem_limit_bytes=VMEM_LIMIT),
        name="finish",
    )(*sources, *shares)


def with_halo(value, sides, width):
    for axis, dim in sides:
        peers, length = (lax.axis_size(axis), value.shape[dim])
        up = [(i, (i + 1) % peers) for i in range(peers - 1)]
        down = [(j, i) for i, j in up]
        last = lax.slice_in_dim(value, length - width, length, axis=dim)
        first = lax.slice_in_dim(value, 0, width, axis=dim)
        before = lax.ppermute(last, axis, up)
        after = lax.ppermute(first, axis, down)
        value = jnp.concatenate([before, value, after], axis=dim)
    return value


def narrow_local(sheared_x, first_plane, z_offsets, z_fracs, y_offsets, y_fracs, slopes):
    depth = TAPS // 2 + OFFZ
    plane_count, row_local, width_all = sheared_x.shape
    groups = lax.axis_size("gy")
    col_local = width_all // groups
    extended = with_halo(sheared_x, (("gz", 0),), depth)
    plane_index = jnp.arange(plane_count, dtype=jnp.int32)[:, None]
    source_index = jnp.arange(plane_count + 2 * depth, dtype=jnp.int32)[None, :]
    mixing = tap_weight(
        (source_index - depth - plane_index)[None] - z_offsets[:, None, None],
        z_fracs[:, None, None],
    )
    blocked = extended.reshape(plane_count + 2 * depth, row_local, groups, col_local)
    outgoing = jnp.einsum("rzj,jrgc->grcz", mixing, blocked, precision=lax.Precision.HIGHEST)
    outgoing = outgoing.reshape(groups, 1, row_local * col_local * plane_count)
    arrived = lax.all_to_all(outgoing, "gy", split_axis=0, concat_axis=1, tiled=True)
    row_total = groups * row_local
    columns = arrived.reshape(row_total, col_local, plane_count)
    target_row = jnp.arange(row_total, dtype=jnp.int32)[:, None]
    source_row = jnp.arange(row_total, dtype=jnp.int32)[None, :]
    operator = tap_weight(
        (source_row - target_row)[None] - y_offsets[:, None, None], y_fracs[:, None, None]
    )
    rotated_cols = jnp.einsum("cij,jcz->zci", operator, columns, precision=lax.Precision.HIGHEST)
    span_pad = row_total // 4
    total_planes = plane_count * lax.axis_size("gz")
    global_planes = first_plane + jnp.arange(plane_count, dtype=jnp.int32)
    padded_cols = jnp.pad(rotated_cols, ((0, 0), (0, 0), (span_pad, span_pad)))
    per_tilt = []
    for tilt_index in range(slopes.shape[0]):
        lifts = (
            slopes[tilt_index]
            * (2 * global_planes - total_planes)
            * row_total
            // (16 * total_planes)
        )
        moved = jax.vmap(
            lambda one_plane, lift_one: lax.dynamic_slice_in_dim(
                one_plane, span_pad + lift_one, row_total, 1
            )
        )(padded_cols, lifts)
        per_tilt.append(jnp.sum(moved, axis=0))
    partial_terms = jnp.stack(per_tilt) * total_planes ** (-0.5)
    projections = lax.psum_scatter(partial_terms, "gz", scatter_dimension=0, tiled=True)
    returning = rotated_cols.reshape(plane_count, col_local, groups, row_local)
    returning = jnp.transpose(returning, (2, 3, 1, 0)).reshape(
        groups, 1, row_local * col_local * plane_count
    )
    landed = lax.all_to_all(returning, "gy", split_axis=0, concat_axis=1, tiled=True)
    landed = landed.reshape(groups, row_local, col_local, plane_count)
    rotated = jnp.transpose(landed, (3, 1, 0, 2)).reshape(
        plane_count, row_local, groups * col_local
    )
    return (rotated, projections)


def swap(value, axis, step):
    return lax.ppermute(value, axis, [(i, i ^ step) for i in range(lax.axis_size(axis))])


def local(volume, x_offsets, x_fracs, z_offsets, z_fracs, y_offsets, y_fracs, slopes):
    depth = TAPS // 2 + OFFZ
    plane_count, row_local, width_all = volume.shape
    groups, shares = lax.axis_size("gy"), lax.axis_size("gz")
    assert row_local == 1 and width_all % LANES == 0
    rows = width_all // LANES
    col_local = width_all // groups
    place = lax.axis_index("gz").astype(jnp.int32)
    first_plane = place * plane_count
    chips = groups // 2
    even = chips % 4 == 0 and groups & (groups - 1) == 0 and shares & (shares - 1) == 0
    wide = even and col_local % LANES == 0 and col_local > LANES and slopes.shape[0] % shares == 0
    sheared = shear_x(
        volume.reshape(plane_count, rows, LANES), x_offsets, x_fracs,
        col_local // LANES if wide else 1, 2 if wide else 1,
    )
    if not wide:
        return narrow_local(
            sheared[0].reshape(volume.shape), first_plane, z_offsets, z_fracs, y_offsets, y_fracs,
            slopes,
        )
    mixing, taps, chosen = weights(
        z_offsets, z_fracs, slopes, y_offsets, y_fracs, plane_count, depth, groups, shares
    )
    spare = plane_count - depth
    pair_first = jnp.where(place % 2 == 0, spare, 0)
    ends = [[], []]
    for i in range(shares - 1):
        ends[i % 2] += [(i, i + 1), (i + 1, i)]
    columns = [None] * groups
    for half, value in zip((1, 0), sheared):
        pair, other = (
            lax.ppermute(lax.dynamic_slice_in_dim(value, first, depth, 0), "gz", ends[parity])
            for parity, first in ((0, pair_first), (1, spare - pair_first))
        )
        mixed = shear_z(mixing, pair, value, other, chips)
        mixing, *mixed = lax.optimization_barrier((mixing, *mixed))
        for index in reversed(range(chips)):
            step = 2 * (2 * (index // 2) + half) + index % 2
            columns[step] = swap(mixed[index], "gy", step) if step else mixed[index]
    own, cross, *rotated = shear_y(taps, columns)
    pairs, direct = rotated[:-2], rotated[-2:]
    landed = [swap(value, "gy", 2 * step + 2) for step, value in enumerate(pairs)]
    direct = [swap(value, "gy", groups - 2 + core) for core, value in enumerate(direct)]
    early = swap(cross, "gy", 1)
    tilted = project(chosen, (own, cross, *rotated), shares)
    tilted = [swap(tilted[step], "gz", step) for step in range(shares - 1, 0, -1)] + [tilted[0]]
    late = [swap(value, "gy", 1) for value in collect(landed)]
    tilted, direct, late = lax.optimization_barrier((tilted, direct, late))
    rotated, projections = finish(own, early, landed, late, direct, tilted, plane_count)
    return (
        rotated.reshape(plane_count, row_local, width_all),
        jnp.swapaxes(projections, 1, 2),
    )


def solution(mesh):
    return jax.shard_map(
        local,
        mesh=mesh,
        in_specs=(P("gz", "gy", None), P(), P(), P("gy"), P("gy"), P("gy"), P("gy"), P()),
        out_specs=(P("gz", "gy", None), P("gz", "gy", None)),
        check_vma=False,
    )
```

```python
import functools

import jax
import jax.numpy as jnp
from jax import lax
from jax.experimental import pallas as pl
from jax.experimental.pallas import tpu as pltpu
from jax.sharding import PartitionSpec as P

TAPS = 64
OFFX = 64
OFFZ = 4
LANES = 128
BELOW = TAPS // 2 - 1
VMEM_LIMIT = 32 * 1024 * 1024

SMEM_SPEC = pl.BlockSpec(memory_space=pltpu.SMEM)
VMEM_SPEC = pl.BlockSpec(memory_space=pltpu.VMEM)


def tap_weight(offset, fraction):
    moved = offset.astype(jnp.float32) - fraction
    inside = (offset >= 1 - TAPS // 2) & (offset <= TAPS // 2)
    value = jnp.sinc(moved) * (0.5 + 0.5 * jnp.cos(jnp.pi * moved / (TAPS // 2 + 1)))
    return jnp.where(inside, value, jnp.zeros_like(value))


def tap_weight_in_kernel(offset, fraction):
    moved = offset.astype(jnp.float32) - fraction
    inside = (offset >= 1 - TAPS // 2) & (offset <= TAPS // 2)
    angle = jnp.pi * moved
    at_zero = moved == 0.0
    sinc = jnp.where(at_zero, 1.0, jnp.sin(angle) / jnp.where(at_zero, 1.0, angle))
    window = 0.5 + 0.5 * jnp.cos(angle / (TAPS // 2 + 1))
    return jnp.where(inside, sinc * window, 0.0)


def split_high_low(value):
    high = value.astype(jnp.bfloat16)
    low = (value - high.astype(jnp.float32)).astype(jnp.bfloat16)
    return high, low


def shear_x_kernel(
    classes, shifts_hbm, fracs_hbm, planes_hbm, *rest
):
    out_refs = rest[:-8]
    planes_ref, margin_ref, base_ref, lines_ref, shifts_ref, fracs_ref, small_sem, plane_sem = (
        rest[-8:]
    )
    plane_count, rows, lanes = planes_ref.shape
    per_class = rows // classes
    before, after = 8, margin_ref.shape[1] - rows - 8
    blocks = plane_sem.shape[0]
    per_block = plane_count // blocks
    small = [
        pltpu.make_async_copy(shifts_hbm, shifts_ref, small_sem.at[0]),
        pltpu.make_async_copy(fracs_hbm, fracs_ref, small_sem.at[1]),
    ]
    large = [
        pltpu.make_async_copy(
            planes_hbm.at[b * per_block:(b + 1) * per_block],
            planes_ref.at[b * per_block:(b + 1) * per_block],
            plane_sem.at[b],
        )
        for b in range(blocks)
    ]
    for copy in small + large:
        copy.start()
    line = lax.broadcasted_iota(jnp.int32, (lanes, lanes), 0)
    lane = lax.broadcasted_iota(jnp.int32, (lanes, lanes), 1)
    own_side = lane <= line
    tap = (lanes - lax.broadcasted_iota(jnp.int32, (plane_count, lanes), 1)) % lanes
    lane_of_row = lax.broadcasted_iota(jnp.int32, (per_class, lanes), 1)
    zeros = jnp.zeros((8, lanes), jnp.float32)
    first = lax.axis_index("gz") * plane_count
    side = lax.axis_index("gy") // 2 % 2
    first_lines = (2 - 2 * side, 2 * side)
    for copy in small:
        copy.wait()
    for z in range(plane_count):
        base_ref[z:z + 1, :] = jnp.full((1, lanes), fracs_ref[first + z], jnp.float32)
    base_ref[...] = tap_weight_in_kernel(tap - BELOW, base_ref[...])

    def one_plane(z, carry):
        margin_ref[z, 0:before, :] = zeros
        margin_ref[z, before:before + rows, :] = planes_ref[z]
        margin_ref[z, before + rows:before + rows + after, :] = zeros
        spread = pltpu.roll(
            jnp.broadcast_to(base_ref[pl.ds(z, 1), :], (lanes, lanes)),
            0, 1, stride=1, stride_axis=0,
        )
        own = jnp.where(own_side, spread, 0.0)
        band = jnp.concatenate([own, spread - own], axis=0)
        band = jnp.concatenate(split_high_low(band), axis=1)
        start = shifts_ref[first + z] - BELOW + before * lanes
        top = start // lanes
        back = lanes - (start - top * lanes)
        keep = lane_of_row < back
        turned = [
            pltpu.roll(margin_ref[z, pl.ds(top + i, per_class, stride=classes), :], back, 1)
            for i in range(classes + 2)
        ]
        lines = [jnp.where(keep, turned[i], turned[i + 1]) for i in range(classes + 1)]
        window = jnp.concatenate(
            [jnp.concatenate(lines[:-1], axis=0), jnp.concatenate(lines[1:], axis=0)], axis=1
        )
        window = jnp.concatenate(split_high_low(window), axis=0)
        product = jnp.dot(window, band, preferred_element_type=jnp.float32)
        product = product[:rows] + product[rows:]
        product = product[:, :lanes] + product[:, lanes:]
        if len(out_refs) == 1:
            out_refs[0][z] = product
            return carry
        lines_ref[z] = product
        quarter = rows // 4
        for out_ref, first_line in zip(out_refs, first_lines):
            for core in range(2):
                out_ref[z, core * quarter:(core + 1) * quarter, :] = lines_ref[
                    z, pl.ds(first_line + core, quarter, stride=4), :
                ]
        return carry

    for b in range(blocks):
        large[b].wait()
        lax.fori_loop(b * per_block, (b + 1) * per_block, one_plane, 0, unroll=True)


def shear_x(volume, x_offsets, x_fracs, classes, parts):
    plane_count, rows, lanes = volume.shape
    blocks = 2 if plane_count % 2 == 0 else 1
    return pl.pallas_call(
        functools.partial(shear_x_kernel, classes),
        out_shape=[
            jax.ShapeDtypeStruct((plane_count, rows // parts, lanes), jnp.float32)
        ] * parts,
        in_specs=[pl.BlockSpec(memory_space=pltpu.HBM)] * 3,
        out_specs=[VMEM_SPEC] * parts,
        scratch_shapes=[
            pltpu.VMEM(volume.shape, jnp.float32),
            pltpu.VMEM((plane_count, rows + 16, lanes), jnp.float32),
            pltpu.VMEM((plane_count, lanes), jnp.float32),
            pltpu.VMEM(volume.shape, jnp.float32),
            pltpu.SMEM(x_offsets.shape, jnp.int32),
            pltpu.SMEM(x_fracs.shape, jnp.float32),
            pltpu.SemaphoreType.DMA((2,)),
            pltpu.SemaphoreType.DMA((blocks,)),
        ],
        compiler_params=pltpu.CompilerParams(vmem_limit_bytes=VMEM_LIMIT),
        name="shear_x",
    )(
        *(pltpu.with_memory_space_constraint(v, pltpu.HBM) for v in (x_offsets, x_fracs, volume)),
    )


def weights_kernel(
    plane_count, depth, ny, shares, shift_ref, frac_ref, slopes_ref, shifts_ref, fracs_ref,
    mixing_ref, taps_ref, chosen_ref,
):
    reach = plane_count + 2 * depth
    place = lax.axis_index("gz")
    even = place % 2 == 0
    target = lax.broadcasted_iota(jnp.int32, (plane_count, reach), 0)
    column = lax.broadcasted_iota(jnp.int32, (plane_count, reach), 1)
    pair_start = jnp.where(even, plane_count, -depth)
    other_start = jnp.where(even, -depth, plane_count)
    source = jnp.where(
        column < depth,
        column + pair_start,
        jnp.where(
            column < depth + plane_count,
            column - depth,
            column - (depth + plane_count) + other_start,
        ),
    )
    mixing_ref[...] = tap_weight_in_kernel(source - target - shift_ref[0], frac_ref[0])
    lanes = taps_ref.shape[1]
    distance = lax.broadcasted_iota(jnp.int32, (2 * ny, lanes), 0) - (ny - 1)
    for tile in range(shifts_ref.shape[1] // lanes):
        part = slice(tile * lanes, (tile + 1) * lanes)
        taps_ref[tile * 2 * ny:(tile + 1) * 2 * ny, :] = tap_weight_in_kernel(
            distance - shifts_ref[:, part], fracs_ref[:, part]
        )
    total_planes = plane_count * shares
    tilts = slopes_ref.shape[0]
    span = ny // 4
    entry = lax.broadcasted_iota(jnp.int32, chosen_ref.shape, 0)
    plane = lax.broadcasted_iota(jnp.int32, chosen_ref.shape, 1) + place * plane_count
    lift = entry // tilts - span
    tilt = entry - (lift + span) * tilts
    slope = jnp.zeros_like(tilt)
    for t in range(tilts):
        slope = jnp.where(tilt == t, slopes_ref[t], slope)
    numerator = slope * (2 * plane - total_planes) * ny
    floor_at = lift * (16 * total_planes)
    chosen = (numerator >= floor_at) & (numerator < floor_at + 16 * total_planes)
    chosen_ref[...] = jnp.where(chosen, 1.0, 0.0)


def weights(
    z_offsets, z_fracs, slopes, y_offsets, y_fracs, plane_count, depth, ny, shares
):
    width = y_offsets.shape[0]
    lifts = 2 * (ny // 4) + 1
    return pl.pallas_call(
        functools.partial(weights_kernel, plane_count, depth, ny, shares),
        out_shape=(
            jax.ShapeDtypeStruct((plane_count, plane_count + 2 * depth), jnp.float32),
            jax.ShapeDtypeStruct((width // LANES * 2 * ny, LANES), jnp.float32),
            jax.ShapeDtypeStruct((lifts * slopes.shape[0], plane_count), jnp.float32),
        ),
        in_specs=[SMEM_SPEC] * 3 + [VMEM_SPEC] * 2,
        out_specs=(VMEM_SPEC, VMEM_SPEC, VMEM_SPEC),
        compiler_params=pltpu.CompilerParams(vmem_limit_bytes=VMEM_LIMIT),
        name="weights",
    )(
        z_offsets, z_fracs, slopes,
        y_offsets.reshape(1, width), y_fracs.reshape(1, width),
    )


def shear_z_kernel(
    plane_count, depth, chips, mixing_ref, pair_ref, own_ref, other_ref, *outs
):
    lanes = own_ref.shape[1]
    rows = own_ref.shape[0] // plane_count
    half = chips // 2
    tiles = rows // chips
    pair = 2 if tiles % 2 == 0 else 1
    high, low = split_high_low(mixing_ref[...])
    mixing = jnp.concatenate(
        [jnp.concatenate([high, high], axis=1), jnp.concatenate([low, low], axis=1)], axis=0
    )
    own_row = lax.axis_index("gy")
    core, chip_pair = own_row % 2, own_row // 4
    for index, out_ref in enumerate(outs):
        first = (core ^ (index % 2)) * (rows // 2) + (chip_pair ^ (index // 2))
        for tile in range(0, tiles, pair):
            columns = []
            for i in range(tile, tile + pair):
                row = first + i * half
                columns.append(
                    jnp.concatenate(
                        [
                            pair_ref[pl.ds(row, depth, stride=rows), :],
                            own_ref[pl.ds(row, plane_count, stride=rows), :],
                            other_ref[pl.ds(row, depth, stride=rows), :],
                        ],
                        axis=0,
                    )
                )
            stack = jnp.concatenate(columns, axis=1)
            stack = jnp.concatenate(split_high_low(stack), axis=0)
            product = jnp.dot(mixing, stack, preferred_element_type=jnp.float32)
            out_ref[:, tile * lanes:(tile + pair) * lanes] = (
                product[:plane_count] + product[plane_count:]
            )


def shear_z(mixing, pair, own, other, chips):
    plane_count, rows, lanes = own.shape
    depth = pair.shape[0]
    width = rows * lanes // chips
    return pl.pallas_call(
        functools.partial(shear_z_kernel, plane_count, depth, chips),
        out_shape=[jax.ShapeDtypeStruct((plane_count, width), jnp.float32)] * chips,
        in_specs=[VMEM_SPEC] * 4,
        out_specs=[VMEM_SPEC] * chips,
        compiler_params=pltpu.CompilerParams(vmem_limit_bytes=VMEM_LIMIT),
        name="shear_z",
    )(mixing, *(value.reshape(-1, lanes) for value in (pair, own, other)))


def start_order(ny):
    return sorted(range(ny), key=lambda slot: (-(slot // 2 % 2), -(slot // 4), slot % 2, -slot))


def shear_y_kernel(ny, taps_ref, *refs):
    in_refs, out_refs = refs[:ny], refs[ny:]
    in_refs = [in_refs[start_order(ny).index(slot)] for slot in range(ny)]
    plane_count, width = in_refs[0].shape
    row = lax.axis_index("gy")
    tiles = width // LANES
    for tile in range(tiles):
        lanes = slice(tile * LANES, (tile + 1) * LANES)
        first = tile * 2 * ny + ny - 1
        for target in range(ny):
            weight = [
                jnp.broadcast_to(
                    taps_ref[pl.ds(first + (row ^ source) - (row ^ target), 1), :], (8, LANES)
                )
                for source in range(ny)
            ]
            for block in range(plane_count // 8):
                planes = slice(block * 8, (block + 1) * 8)
                value = weight[0] * in_refs[0][planes, lanes]
                for source in range(1, ny):
                    value = value + weight[source] * in_refs[source][planes, lanes]
                lines = pl.ds(block * 8 * tiles + tile, 8, stride=tiles)
                if target < 4:
                    out_refs[target][lines, :] = value
                else:
                    out_refs[target // 2 + 2][target % 2, lines, :] = value


def shear_y(taps, columns):
    ny = len(columns)
    plane_count, width = columns[0].shape
    shape = (plane_count * width // LANES, LANES)
    out_shape = [jax.ShapeDtypeStruct(shape, jnp.float32)] * 4
    out_shape += [jax.ShapeDtypeStruct((2, *shape), jnp.float32)] * (ny // 2 - 2)
    return pl.pallas_call(
        functools.partial(shear_y_kernel, ny),
        out_shape=out_shape,
        in_specs=[VMEM_SPEC] * (1 + ny),
        out_specs=[VMEM_SPEC] * len(out_shape),
        compiler_params=pltpu.CompilerParams(vmem_limit_bytes=VMEM_LIMIT),
        name="shear_y",
    )(taps, *(columns[slot] for slot in start_order(ny)))


def collect_kernel(*refs):
    count = len(refs) // 2
    for source, target in zip(refs[:count], refs[count:]):
        target[...] = source[1]


def collect(landed):
    return pl.pallas_call(
        collect_kernel,
        out_shape=[jax.ShapeDtypeStruct(v.shape[1:], jnp.float32) for v in landed],
        in_specs=[VMEM_SPEC] * len(landed),
        out_specs=[VMEM_SPEC] * len(landed),
        compiler_params=pltpu.CompilerParams(vmem_limit_bytes=VMEM_LIMIT),
        name="collect",
    )(*landed)


def project_kernel(chips, tilts, shares, chosen_ref, *refs):
    place, own_row = lax.axis_index("gz"), lax.axis_index("gy")
    in_refs, share_ref, totals_ref = refs[:chips + 2], refs[-2], refs[-1]
    ny = 2 * chips
    plane_count = chosen_ref.shape[1]
    total_planes = plane_count * shares
    span = ny // 4
    tiles = in_refs[0].shape[0] // plane_count
    lifts = 2 * span + 1
    chosen = chosen_ref[...].astype(jnp.bfloat16)
    chosen = jnp.concatenate([chosen, chosen], axis=1)

    per_tile = (ny + 2 * span) * tilts
    totals_ref[...] = jnp.zeros(totals_ref.shape, jnp.float32)
    for source in range(ny):
        if source < 4:
            ref = in_refs[source]
        else:
            ref = in_refs[source // 2 + 2].at[source % 2]
        value = jnp.concatenate(
            [ref[pl.ds(tile, plane_count, stride=tiles), :] for tile in range(tiles)], axis=1
        )
        sums = jnp.dot(
            chosen,
            jnp.concatenate(split_high_low(value), axis=0),
            preferred_element_type=jnp.float32,
        )
        row = own_row ^ source
        for l in range(lifts):
            for tile in range(tiles):
                start = pl.multiple_of(tile * per_tile + (row + 2 * span - l) * tilts, tilts)
                totals_ref[pl.ds(start, tilts), :] += sums[
                    l * tilts:(l + 1) * tilts, tile * LANES:(tile + 1) * LANES
                ]
    per_share = tilts // shares
    for step in range(shares):
        tilt = step * per_share
        for u in range(per_share):
            for tile in range(tiles):
                share_ref[step, u, :, tile * LANES:(tile + 1) * LANES] = (
                    totals_ref[
                        pl.ds(tile * per_tile + span * tilts + tilt + u, ny, stride=tilts), :
                    ]
                    * total_planes ** (-0.5)
                )


def project(chosen, rotated, shares):
    chips = len(rotated) - 2
    ny = 2 * chips
    tilts = chosen.shape[0] // (2 * (ny // 4) + 1)
    width = rotated[0].shape[0] // chosen.shape[1] * LANES
    share = jax.ShapeDtypeStruct((shares, tilts // shares, ny, width), jnp.float32)
    totals = (width // LANES * (ny + 2 * (ny // 4)) * tilts, LANES)
    return pl.pallas_call(
        functools.partial(project_kernel, chips, tilts, shares),
        out_shape=share,
        in_specs=[VMEM_SPEC] * (1 + len(rotated)),
        out_specs=VMEM_SPEC,
        scratch_shapes=[pltpu.VMEM(totals, jnp.float32)],
        compiler_params=pltpu.CompilerParams(vmem_limit_bytes=VMEM_LIMIT),
        name="project",
    )(chosen, *rotated)


def finish_kernel(slots, *refs):
    sources, share_refs = refs[:len(slots)], refs[len(slots):-3]
    rotated_ref, projections_ref, sems = refs[-3:]
    row = lax.axis_index("gy")
    copies = [
        pltpu.make_async_copy(
            ref if index is None else ref.at[index], rotated_ref.at[:, row ^ slot], sems.at[slot]
        )
        for ref, (slot, index) in zip(sources, slots)
    ]
    for copy in copies:
        copy.start()
    total = share_refs[0][0]
    for share in range(1, share_refs[0].shape[0]):
        total = total + share_refs[0][share]
    projections_ref[...] = total
    for copy in copies:
        copy.wait()


def finish(own, early, landed, late, direct, shares, plane_count):
    chips = len(landed) + 2
    slots = [(slot, None) for slot in range(4)]
    slots += [(2 * step, 0) for step in range(2, chips)]
    slots += [(2 * step + 1, None) for step in range(2, chips)]
    tiles = own.shape[0] // plane_count
    sources = [
        value.reshape(*value.shape[:-2], plane_count, tiles, LANES)
        for value in (own, early, *direct, *landed, *late)
    ]
    return pl.pallas_call(
        functools.partial(finish_kernel, slots),
        out_shape=(
            jax.ShapeDtypeStruct((plane_count, 2 * chips, tiles, LANES), jnp.float32),
            jax.ShapeDtypeStruct(shares[0].shape[1:], jnp.float32),
        ),
        in_specs=[VMEM_SPEC] * (len(slots) + len(shares)),
        out_specs=(pl.BlockSpec(memory_space=pltpu.HBM), VMEM_SPEC),
        scratch_shapes=[pltpu.SemaphoreType.DMA((2 * chips,))],
        compiler_params=pltpu.CompilerParams(vmem_limit_bytes=VMEM_LIMIT),
        name="finish",
    )(*sources, *shares)


def with_halo(value, sides, width):
    for axis, dim in sides:
        peers, length = (lax.axis_size(axis), value.shape[dim])
        up = [(i, (i + 1) % peers) for i in range(peers - 1)]
        down = [(j, i) for i, j in up]
        last = lax.slice_in_dim(value, length - width, length, axis=dim)
        first = lax.slice_in_dim(value, 0, width, axis=dim)
        before = lax.ppermute(last, axis, up)
        after = lax.ppermute(first, axis, down)
        value = jnp.concatenate([before, value, after], axis=dim)
    return value


def narrow_local(sheared_x, first_plane, z_offsets, z_fracs, y_offsets, y_fracs, slopes):
    depth = TAPS // 2 + OFFZ
    plane_count, row_local, width_all = sheared_x.shape
    groups = lax.axis_size("gy")
    col_local = width_all // groups
    extended = with_halo(sheared_x, (("gz", 0),), depth)
    plane_index = jnp.arange(plane_count, dtype=jnp.int32)[:, None]
    source_index = jnp.arange(plane_count + 2 * depth, dtype=jnp.int32)[None, :]
    mixing = tap_weight(
        (source_index - depth - plane_index)[None] - z_offsets[:, None, None],
        z_fracs[:, None, None],
    )
    blocked = extended.reshape(plane_count + 2 * depth, row_local, groups, col_local)
    outgoing = jnp.einsum("rzj,jrgc->grcz", mixing, blocked, precision=lax.Precision.HIGHEST)
    outgoing = outgoing.reshape(groups, 1, row_local * col_local * plane_count)
    arrived = lax.all_to_all(outgoing, "gy", split_axis=0, concat_axis=1, tiled=True)
    row_total = groups * row_local
    columns = arrived.reshape(row_total, col_local, plane_count)
    target_row = jnp.arange(row_total, dtype=jnp.int32)[:, None]
    source_row = jnp.arange(row_total, dtype=jnp.int32)[None, :]
    operator = tap_weight(
        (source_row - target_row)[None] - y_offsets[:, None, None], y_fracs[:, None, None]
    )
    rotated_cols = jnp.einsum("cij,jcz->zci", operator, columns, precision=lax.Precision.HIGHEST)
    span_pad = row_total // 4
    total_planes = plane_count * lax.axis_size("gz")
    global_planes = first_plane + jnp.arange(plane_count, dtype=jnp.int32)
    padded_cols = jnp.pad(rotated_cols, ((0, 0), (0, 0), (span_pad, span_pad)))
    per_tilt = []
    for tilt_index in range(slopes.shape[0]):
        lifts = (
            slopes[tilt_index]
            * (2 * global_planes - total_planes)
            * row_total
            // (16 * total_planes)
        )
        moved = jax.vmap(
            lambda one_plane, lift_one: lax.dynamic_slice_in_dim(
                one_plane, span_pad + lift_one, row_total, 1
            )
        )(padded_cols, lifts)
        per_tilt.append(jnp.sum(moved, axis=0))
    partial_terms = jnp.stack(per_tilt) * total_planes ** (-0.5)
    projections = lax.psum_scatter(partial_terms, "gz", scatter_dimension=0, tiled=True)
    returning = rotated_cols.reshape(plane_count, col_local, groups, row_local)
    returning = jnp.transpose(returning, (2, 3, 1, 0)).reshape(
        groups, 1, row_local * col_local * plane_count
    )
    landed = lax.all_to_all(returning, "gy", split_axis=0, concat_axis=1, tiled=True)
    landed = landed.reshape(groups, row_local, col_local, plane_count)
    rotated = jnp.transpose(landed, (3, 1, 0, 2)).reshape(
        plane_count, row_local, groups * col_local
    )
    return (rotated, projections)


def swap(value, axis, step):
    return lax.ppermute(value, axis, [(i, i ^ step) for i in range(lax.axis_size(axis))])


def local(volume, x_offsets, x_fracs, z_offsets, z_fracs, y_offsets, y_fracs, slopes):
    depth = TAPS // 2 + OFFZ
    plane_count, row_local, width_all = volume.shape
    groups, shares = lax.axis_size("gy"), lax.axis_size("gz")
    assert row_local == 1 and width_all % LANES == 0
    rows = width_all // LANES
    col_local = width_all // groups
    place = lax.axis_index("gz").astype(jnp.int32)
    first_plane = place * plane_count
    chips = groups // 2
    even = chips % 4 == 0 and groups & (groups - 1) == 0 and shares & (shares - 1) == 0
    wide = even and col_local % LANES == 0 and col_local > LANES and slopes.shape[0] % shares == 0
    sheared = shear_x(
        volume.reshape(plane_count, rows, LANES), x_offsets, x_fracs,
        col_local // LANES if wide else 1, 2 if wide else 1,
    )
    if not wide:
        return narrow_local(
            sheared[0].reshape(volume.shape), first_plane, z_offsets, z_fracs, y_offsets, y_fracs,
            slopes,
        )
    mixing, taps, chosen = weights(
        z_offsets, z_fracs, slopes, y_offsets, y_fracs, plane_count, depth, groups, shares
    )
    spare = plane_count - depth
    pair_first = jnp.where(place % 2 == 0, spare, 0)
    ends = [[], []]
    for i in range(shares - 1):
        ends[i % 2] += [(i, i + 1), (i + 1, i)]
    columns = [None] * groups
    for half, value in zip((1, 0), sheared):
        pair, other = (
            lax.ppermute(lax.dynamic_slice_in_dim(value, first, depth, 0), "gz", ends[parity])
            for parity, first in ((0, pair_first), (1, spare - pair_first))
        )
        mixed = shear_z(mixing, pair, value, other, chips)
        mixing, *mixed = lax.optimization_barrier((mixing, *mixed))
        for index in reversed(range(chips)):
            step = 2 * (2 * (index // 2) + half) + index % 2
            columns[step] = swap(mixed[index], "gy", step) if step else mixed[index]
    own, cross, *rotated = shear_y(taps, columns)
    direct, pairs = rotated[:2], rotated[2:]
    landed = [swap(value, "gy", 2 * step + 4) for step, value in enumerate(pairs)]
    direct = [swap(value, "gy", 2 + core) for core, value in enumerate(direct)]
    early = swap(cross, "gy", 1)
    tilted = project(chosen, (own, cross, *rotated), shares)
    tilted = [lax.all_to_all(tilted, "gz", split_axis=0, concat_axis=0, tiled=True)]
    late = [swap(value, "gy", 1) for value in collect(landed)]
    tilted, late, direct = lax.optimization_barrier((tilted, late, direct))
    rotated, projections = finish(own, early, landed, late, direct, tilted, plane_count)
    return (
        rotated.reshape(plane_count, row_local, width_all),
        jnp.swapaxes(projections, 1, 2),
    )


def solution(mesh):
    return jax.shard_map(
        local,
        mesh=mesh,
        in_specs=(P("gz", "gy", None), P(), P(), P("gy"), P("gy"), P("gy"), P("gy"), P()),
        out_specs=(P("gz", "gy", None), P("gz", "gy", None)),
        check_vma=False,
    )
```

```python
import functools

import jax
import jax.numpy as jnp
from jax import lax
from jax.experimental import pallas as pl
from jax.experimental.pallas import tpu as pltpu
from jax.sharding import PartitionSpec as P

TAPS = 64
OFFX = 64
OFFZ = 4
LANES = 128
BELOW = TAPS // 2 - 1
VMEM_LIMIT = 32 * 1024 * 1024

SMEM_SPEC = pl.BlockSpec(memory_space=pltpu.SMEM)
VMEM_SPEC = pl.BlockSpec(memory_space=pltpu.VMEM)


def tap_weight(offset, fraction):
    moved = offset.astype(jnp.float32) - fraction
    inside = (offset >= 1 - TAPS // 2) & (offset <= TAPS // 2)
    value = jnp.sinc(moved) * (0.5 + 0.5 * jnp.cos(jnp.pi * moved / (TAPS // 2 + 1)))
    return jnp.where(inside, value, jnp.zeros_like(value))


def tap_weight_in_kernel(offset, fraction):
    moved = offset.astype(jnp.float32) - fraction
    inside = (offset >= 1 - TAPS // 2) & (offset <= TAPS // 2)
    angle = jnp.pi * moved
    at_zero = moved == 0.0
    sinc = jnp.where(at_zero, 1.0, jnp.sin(angle) / jnp.where(at_zero, 1.0, angle))
    window = 0.5 + 0.5 * jnp.cos(angle / (TAPS // 2 + 1))
    return jnp.where(inside, sinc * window, 0.0)


def split_high_low(value):
    high = value.astype(jnp.bfloat16)
    low = (value - high.astype(jnp.float32)).astype(jnp.bfloat16)
    return high, low


def shear_x_kernel(
    classes, shifts_hbm, fracs_hbm, planes_hbm, *rest
):
    out_refs = rest[:-7]
    margin_ref, base_ref, lines_ref, shifts_ref, fracs_ref, small_sem, plane_sem = rest[-7:]
    plane_count, rows, lanes = lines_ref.shape
    per_class = rows // classes
    before, after = 8, margin_ref.shape[1] - rows - 8
    small = [
        pltpu.make_async_copy(shifts_hbm, shifts_ref, small_sem.at[0]),
        pltpu.make_async_copy(fracs_hbm, fracs_ref, small_sem.at[1]),
    ]
    large = pltpu.make_async_copy(
        planes_hbm, margin_ref.at[:, before:before + rows, :], plane_sem.at[0]
    )
    for copy in small:
        copy.start()
    large.start()
    line = lax.broadcasted_iota(jnp.int32, (lanes, lanes), 0)
    lane = lax.broadcasted_iota(jnp.int32, (lanes, lanes), 1)
    own_side = lane <= line
    tap = (lanes - lax.broadcasted_iota(jnp.int32, (plane_count, lanes), 1)) % lanes
    lane_of_row = lax.broadcasted_iota(jnp.int32, (per_class, lanes), 1)
    first = lax.axis_index("gz") * plane_count
    margin_ref[:, 0:before, :] = jnp.zeros((plane_count, before, lanes), jnp.float32)
    margin_ref[:, before + rows:, :] = jnp.zeros((plane_count, after, lanes), jnp.float32)
    side = lax.axis_index("gy") // 2 % 2
    first_lines = (2 - 2 * side, 2 * side)
    for copy in small:
        copy.wait()
    for z in range(plane_count):
        base_ref[z:z + 1, :] = jnp.full((1, lanes), fracs_ref[first + z], jnp.float32)
    base_ref[...] = tap_weight_in_kernel(tap - BELOW, base_ref[...])

    def one_plane(z, carry):
        spread = pltpu.roll(
            jnp.broadcast_to(base_ref[pl.ds(z, 1), :], (lanes, lanes)),
            0, 1, stride=1, stride_axis=0,
        )
        own = jnp.where(own_side, spread, 0.0)
        band = jnp.concatenate([own, spread - own], axis=0)
        band = jnp.concatenate(split_high_low(band), axis=1)
        start = shifts_ref[first + z] - BELOW + before * lanes
        top = start // lanes
        back = lanes - (start - top * lanes)
        keep = lane_of_row < back
        turned = [
            pltpu.roll(margin_ref[z, pl.ds(top + i, per_class, stride=classes), :], back, 1)
            for i in range(classes + 2)
        ]
        lines = [jnp.where(keep, turned[i], turned[i + 1]) for i in range(classes + 1)]
        window = jnp.concatenate(
            [jnp.concatenate(lines[:-1], axis=0), jnp.concatenate(lines[1:], axis=0)], axis=1
        )
        window = jnp.concatenate(split_high_low(window), axis=0)
        product = jnp.dot(window, band, preferred_element_type=jnp.float32)
        product = product[:rows] + product[rows:]
        product = product[:, :lanes] + product[:, lanes:]
        if len(out_refs) == 1:
            out_refs[0][z] = product
            return carry
        lines_ref[z] = product
        quarter = rows // 4
        for out_ref, first_line in zip(out_refs, first_lines):
            for core in range(2):
                out_ref[z, core * quarter:(core + 1) * quarter, :] = lines_ref[
                    z, pl.ds(first_line + core, quarter, stride=4), :
                ]
        return carry

    large.wait()
    lax.fori_loop(0, plane_count, one_plane, 0, unroll=True)


def shear_x(volume, x_offsets, x_fracs, classes, parts):
    plane_count, rows, lanes = volume.shape
    return pl.pallas_call(
        functools.partial(shear_x_kernel, classes),
        out_shape=[
            jax.ShapeDtypeStruct((plane_count, rows // parts, lanes), jnp.float32)
        ] * parts,
        in_specs=[pl.BlockSpec(memory_space=pltpu.HBM)] * 3,
        out_specs=[VMEM_SPEC] * parts,
        scratch_shapes=[
            pltpu.VMEM((plane_count, rows + 16, lanes), jnp.float32),
            pltpu.VMEM((plane_count, lanes), jnp.float32),
            pltpu.VMEM(volume.shape, jnp.float32),
            pltpu.SMEM(x_offsets.shape, jnp.int32),
            pltpu.SMEM(x_fracs.shape, jnp.float32),
            pltpu.SemaphoreType.DMA((2,)),
            pltpu.SemaphoreType.DMA((1,)),
        ],
        compiler_params=pltpu.CompilerParams(vmem_limit_bytes=VMEM_LIMIT),
        name="shear_x",
    )(
        *(pltpu.with_memory_space_constraint(v, pltpu.HBM) for v in (x_offsets, x_fracs, volume)),
    )


def weights_kernel(
    plane_count, depth, ny, shares, shift_ref, frac_ref, slopes_ref, shifts_ref, fracs_ref,
    mixing_ref, taps_ref, chosen_ref,
):
    reach = plane_count + 2 * depth
    place = lax.axis_index("gz")
    even = place % 2 == 0
    target = lax.broadcasted_iota(jnp.int32, (plane_count, reach), 0)
    column = lax.broadcasted_iota(jnp.int32, (plane_count, reach), 1)
    pair_start = jnp.where(even, plane_count, -depth)
    other_start = jnp.where(even, -depth, plane_count)
    source = jnp.where(
        column < depth,
        column + pair_start,
        jnp.where(
            column < depth + plane_count,
            column - depth,
            column - (depth + plane_count) + other_start,
        ),
    )
    mixing_ref[...] = tap_weight_in_kernel(source - target - shift_ref[0], frac_ref[0])
    lanes = taps_ref.shape[1]
    distance = lax.broadcasted_iota(jnp.int32, (2 * ny, lanes), 0) - (ny - 1)
    for tile in range(shifts_ref.shape[1] // lanes):
        part = slice(tile * lanes, (tile + 1) * lanes)
        taps_ref[tile * 2 * ny:(tile + 1) * 2 * ny, :] = tap_weight_in_kernel(
            distance - shifts_ref[:, part], fracs_ref[:, part]
        )
    total_planes = plane_count * shares
    tilts = slopes_ref.shape[0]
    span = ny // 4
    entry = lax.broadcasted_iota(jnp.int32, chosen_ref.shape, 0)
    plane = lax.broadcasted_iota(jnp.int32, chosen_ref.shape, 1) + place * plane_count
    lift = entry // tilts - span
    tilt = entry - (lift + span) * tilts
    slope = jnp.zeros_like(tilt)
    for t in range(tilts):
        slope = jnp.where(tilt == t, slopes_ref[t], slope)
    numerator = slope * (2 * plane - total_planes) * ny
    floor_at = lift * (16 * total_planes)
    chosen = (numerator >= floor_at) & (numerator < floor_at + 16 * total_planes)
    chosen_ref[...] = jnp.where(chosen, 1.0, 0.0)


def weights(
    z_offsets, z_fracs, slopes, y_offsets, y_fracs, plane_count, depth, ny, shares
):
    width = y_offsets.shape[0]
    lifts = 2 * (ny // 4) + 1
    return pl.pallas_call(
        functools.partial(weights_kernel, plane_count, depth, ny, shares),
        out_shape=(
            jax.ShapeDtypeStruct((plane_count, plane_count + 2 * depth), jnp.float32),
            jax.ShapeDtypeStruct((width // LANES * 2 * ny, LANES), jnp.float32),
            jax.ShapeDtypeStruct((lifts * slopes.shape[0], plane_count), jnp.float32),
        ),
        in_specs=[SMEM_SPEC] * 3 + [VMEM_SPEC] * 2,
        out_specs=(VMEM_SPEC, VMEM_SPEC, VMEM_SPEC),
        compiler_params=pltpu.CompilerParams(vmem_limit_bytes=VMEM_LIMIT),
        name="weights",
    )(
        z_offsets, z_fracs, slopes,
        y_offsets.reshape(1, width), y_fracs.reshape(1, width),
    )


def shear_z_kernel(
    plane_count, depth, chips, mixing_ref, pair_ref, own_ref, other_ref, *outs
):
    lanes = own_ref.shape[1]
    rows = own_ref.shape[0] // plane_count
    half = chips // 2
    tiles = rows // chips
    pair = 2 if tiles % 2 == 0 else 1
    high, low = split_high_low(mixing_ref[...])
    mixing = jnp.concatenate(
        [jnp.concatenate([high, high], axis=1), jnp.concatenate([low, low], axis=1)], axis=0
    )
    own_row = lax.axis_index("gy")
    core, chip_pair = own_row % 2, own_row // 4
    for index, out_ref in enumerate(outs):
        first = (core ^ (index % 2)) * (rows // 2) + (chip_pair ^ (index // 2))
        for tile in range(0, tiles, pair):
            columns = []
            for i in range(tile, tile + pair):
                row = first + i * half
                columns.append(
                    jnp.concatenate(
                        [
                            pair_ref[pl.ds(row, depth, stride=rows), :],
                            own_ref[pl.ds(row, plane_count, stride=rows), :],
                            other_ref[pl.ds(row, depth, stride=rows), :],
                        ],
                        axis=0,
                    )
                )
            stack = jnp.concatenate(columns, axis=1)
            stack = jnp.concatenate(split_high_low(stack), axis=0)
            product = jnp.dot(mixing, stack, preferred_element_type=jnp.float32)
            out_ref[:, tile * lanes:(tile + pair) * lanes] = (
                product[:plane_count] + product[plane_count:]
            )


def shear_z(mixing, pair, own, other, chips):
    plane_count, rows, lanes = own.shape
    depth = pair.shape[0]
    width = rows * lanes // chips
    return pl.pallas_call(
        functools.partial(shear_z_kernel, plane_count, depth, chips),
        out_shape=[jax.ShapeDtypeStruct((plane_count, width), jnp.float32)] * chips,
        in_specs=[VMEM_SPEC] * 4,
        out_specs=[VMEM_SPEC] * chips,
        compiler_params=pltpu.CompilerParams(vmem_limit_bytes=VMEM_LIMIT),
        name="shear_z",
    )(mixing, *(value.reshape(-1, lanes) for value in (pair, own, other)))


def start_order(ny):
    return sorted(range(ny), key=lambda slot: (-(slot // 2 % 2), -(slot // 4), slot % 2, -slot))


def shear_y_kernel(ny, taps_ref, *refs):
    in_refs, out_refs = refs[:ny], refs[ny:]
    in_refs = [in_refs[start_order(ny).index(slot)] for slot in range(ny)]
    plane_count, width = in_refs[0].shape
    row = lax.axis_index("gy")
    tiles = width // LANES
    for tile in range(tiles):
        lanes = slice(tile * LANES, (tile + 1) * LANES)
        first = tile * 2 * ny + ny - 1
        for target in range(ny):
            weight = [
                jnp.broadcast_to(
                    taps_ref[pl.ds(first + (row ^ source) - (row ^ target), 1), :], (8, LANES)
                )
                for source in range(ny)
            ]
            for block in range(plane_count // 8):
                planes = slice(block * 8, (block + 1) * 8)
                value = weight[0] * in_refs[0][planes, lanes]
                for source in range(1, ny):
                    value = value + weight[source] * in_refs[source][planes, lanes]
                lines = pl.ds(block * 8 * tiles + tile, 8, stride=tiles)
                if target < 4:
                    out_refs[target][lines, :] = value
                else:
                    out_refs[target // 2 + 2][target % 2, lines, :] = value


def shear_y(taps, columns):
    ny = len(columns)
    plane_count, width = columns[0].shape
    shape = (plane_count * width // LANES, LANES)
    out_shape = [jax.ShapeDtypeStruct(shape, jnp.float32)] * 4
    out_shape += [jax.ShapeDtypeStruct((2, *shape), jnp.float32)] * (ny // 2 - 2)
    return pl.pallas_call(
        functools.partial(shear_y_kernel, ny),
        out_shape=out_shape,
        in_specs=[VMEM_SPEC] * (1 + ny),
        out_specs=[VMEM_SPEC] * len(out_shape),
        compiler_params=pltpu.CompilerParams(vmem_limit_bytes=VMEM_LIMIT),
        name="shear_y",
    )(taps, *(columns[slot] for slot in start_order(ny)))


def collect_kernel(*refs):
    count = len(refs) // 2
    for source, target in zip(refs[:count], refs[count:]):
        target[...] = source[1]


def collect(landed):
    return pl.pallas_call(
        collect_kernel,
        out_shape=[jax.ShapeDtypeStruct(v.shape[1:], jnp.float32) for v in landed],
        in_specs=[VMEM_SPEC] * len(landed),
        out_specs=[VMEM_SPEC] * len(landed),
        compiler_params=pltpu.CompilerParams(vmem_limit_bytes=VMEM_LIMIT),
        name="collect",
    )(*landed)


def project_kernel(chips, tilts, shares, chosen_ref, *refs):
    place, own_row = lax.axis_index("gz"), lax.axis_index("gy")
    in_refs, share_ref, totals_ref = refs[:chips + 2], refs[-2], refs[-1]
    ny = 2 * chips
    plane_count = chosen_ref.shape[1]
    total_planes = plane_count * shares
    span = ny // 4
    tiles = in_refs[0].shape[0] // plane_count
    lifts = 2 * span + 1
    chosen = chosen_ref[...].astype(jnp.bfloat16)
    chosen = jnp.concatenate([chosen, chosen], axis=1)

    per_tile = (ny + 2 * span) * tilts
    totals_ref[...] = jnp.zeros(totals_ref.shape, jnp.float32)
    for source in range(ny):
        if source < 4:
            ref = in_refs[source]
        else:
            ref = in_refs[source // 2 + 2].at[source % 2]
        value = jnp.concatenate(
            [ref[pl.ds(tile, plane_count, stride=tiles), :] for tile in range(tiles)], axis=1
        )
        sums = jnp.dot(
            chosen,
            jnp.concatenate(split_high_low(value), axis=0),
            preferred_element_type=jnp.float32,
        )
        row = own_row ^ source
        for l in range(lifts):
            for tile in range(tiles):
                start = pl.multiple_of(tile * per_tile + (row + 2 * span - l) * tilts, tilts)
                totals_ref[pl.ds(start, tilts), :] += sums[
                    l * tilts:(l + 1) * tilts, tile * LANES:(tile + 1) * LANES
                ]
    per_share = tilts // shares
    for step in range(shares):
        tilt = step * per_share
        for u in range(per_share):
            for tile in range(tiles):
                share_ref[step, u, :, tile * LANES:(tile + 1) * LANES] = (
                    totals_ref[
                        pl.ds(tile * per_tile + span * tilts + tilt + u, ny, stride=tilts), :
                    ]
                    * total_planes ** (-0.5)
                )


def project(chosen, rotated, shares):
    chips = len(rotated) - 2
    ny = 2 * chips
    tilts = chosen.shape[0] // (2 * (ny // 4) + 1)
    width = rotated[0].shape[0] // chosen.shape[1] * LANES
    share = jax.ShapeDtypeStruct((shares, tilts // shares, ny, width), jnp.float32)
    totals = (width // LANES * (ny + 2 * (ny // 4)) * tilts, LANES)
    return pl.pallas_call(
        functools.partial(project_kernel, chips, tilts, shares),
        out_shape=share,
        in_specs=[VMEM_SPEC] * (1 + len(rotated)),
        out_specs=VMEM_SPEC,
        scratch_shapes=[pltpu.VMEM(totals, jnp.float32)],
        compiler_params=pltpu.CompilerParams(vmem_limit_bytes=VMEM_LIMIT),
        name="project",
    )(chosen, *rotated)


def place_kernel(slots, *refs):
    rotated_ref, sems = refs[-2:]
    row = lax.axis_index("gy")
    copies = [
        pltpu.make_async_copy(
            ref if index is None else ref.at[index], rotated_ref.at[:, row ^ slot], sems.at[place]
        )
        for place, (ref, (slot, index)) in enumerate(zip(refs, slots))
    ]
    for copy in copies:
        copy.start()
    for copy in copies:
        copy.wait()


def in_columns(value, plane_count):
    return value.reshape(
        *value.shape[:-2], plane_count, value.shape[-2] // plane_count, value.shape[-1]
    )


def place_first(own, landed, plane_count):
    chips = len(landed) + 2
    slots = [(0, None)] + [(2 * step, 0) for step in range(2, chips)]
    sources = [in_columns(value, plane_count) for value in (own, *landed)]
    return pl.pallas_call(
        functools.partial(place_kernel, slots),
        out_shape=jax.ShapeDtypeStruct(
            (plane_count, 2 * chips, *sources[0].shape[-2:]), jnp.float32
        ),
        in_specs=[VMEM_SPEC] * len(slots),
        out_specs=pl.BlockSpec(memory_space=pltpu.HBM),
        scratch_shapes=[pltpu.SemaphoreType.DMA((len(slots),))],
        compiler_params=pltpu.CompilerParams(vmem_limit_bytes=VMEM_LIMIT),
        name="place_first",
    )(*sources)


def finish_kernel(slots, *refs):
    share_ref = refs[len(slots)]
    rotated_ref, projections_ref, total_ref, sems = refs[-4:]
    row = lax.axis_index("gy")
    copies = [
        pltpu.make_async_copy(ref, rotated_ref.at[:, row ^ slot], sems.at[place])
        for place, (ref, slot) in enumerate(zip(refs, slots))
    ]
    for copy in copies:
        copy.start()
    total = share_ref[0]
    for share in range(1, share_ref.shape[0]):
        total = total + share_ref[share]
    total_ref[...] = total
    copies.append(pltpu.make_async_copy(total_ref, projections_ref, sems.at[len(slots)]))
    copies[-1].start()
    for copy in copies:
        copy.wait()


def finish(placed, early, late, direct, shares, plane_count):
    chips = len(late) + 2
    slots = [1, 2, 3] + [2 * step + 1 for step in range(2, chips)]
    sources = [in_columns(value, plane_count) for value in (early, *direct, *late)]
    return pl.pallas_call(
        functools.partial(finish_kernel, slots),
        out_shape=(
            jax.ShapeDtypeStruct(placed.shape, jnp.float32),
            jax.ShapeDtypeStruct(shares.shape[1:], jnp.float32),
        ),
        in_specs=[VMEM_SPEC] * (len(slots) + 1) + [pl.BlockSpec(memory_space=pltpu.HBM)],
        out_specs=[pl.BlockSpec(memory_space=pltpu.HBM)] * 2,
        scratch_shapes=[
            pltpu.VMEM(shares.shape[1:], jnp.float32),
            pltpu.SemaphoreType.DMA((len(slots) + 1,)),
        ],
        input_output_aliases={len(slots) + 1: 0},
        compiler_params=pltpu.CompilerParams(vmem_limit_bytes=VMEM_LIMIT),
        name="finish",
    )(*sources, shares, placed)


def with_halo(value, sides, width):
    for axis, dim in sides:
        peers, length = (lax.axis_size(axis), value.shape[dim])
        up = [(i, (i + 1) % peers) for i in range(peers - 1)]
        down = [(j, i) for i, j in up]
        last = lax.slice_in_dim(value, length - width, length, axis=dim)
        first = lax.slice_in_dim(value, 0, width, axis=dim)
        before = lax.ppermute(last, axis, up)
        after = lax.ppermute(first, axis, down)
        value = jnp.concatenate([before, value, after], axis=dim)
    return value


def narrow_local(sheared_x, first_plane, z_offsets, z_fracs, y_offsets, y_fracs, slopes):
    depth = TAPS // 2 + OFFZ
    plane_count, row_local, width_all = sheared_x.shape
    groups = lax.axis_size("gy")
    col_local = width_all // groups
    extended = with_halo(sheared_x, (("gz", 0),), depth)
    plane_index = jnp.arange(plane_count, dtype=jnp.int32)[:, None]
    source_index = jnp.arange(plane_count + 2 * depth, dtype=jnp.int32)[None, :]
    mixing = tap_weight(
        (source_index - depth - plane_index)[None] - z_offsets[:, None, None],
        z_fracs[:, None, None],
    )
    blocked = extended.reshape(plane_count + 2 * depth, row_local, groups, col_local)
    outgoing = jnp.einsum("rzj,jrgc->grcz", mixing, blocked, precision=lax.Precision.HIGHEST)
    outgoing = outgoing.reshape(groups, 1, row_local * col_local * plane_count)
    arrived = lax.all_to_all(outgoing, "gy", split_axis=0, concat_axis=1, tiled=True)
    row_total = groups * row_local
    columns = arrived.reshape(row_total, col_local, plane_count)
    target_row = jnp.arange(row_total, dtype=jnp.int32)[:, None]
    source_row = jnp.arange(row_total, dtype=jnp.int32)[None, :]
    operator = tap_weight(
        (source_row - target_row)[None] - y_offsets[:, None, None], y_fracs[:, None, None]
    )
    rotated_cols = jnp.einsum("cij,jcz->zci", operator, columns, precision=lax.Precision.HIGHEST)
    span_pad = row_total // 4
    total_planes = plane_count * lax.axis_size("gz")
    global_planes = first_plane + jnp.arange(plane_count, dtype=jnp.int32)
    padded_cols = jnp.pad(rotated_cols, ((0, 0), (0, 0), (span_pad, span_pad)))
    per_tilt = []
    for tilt_index in range(slopes.shape[0]):
        lifts = (
            slopes[tilt_index]
            * (2 * global_planes - total_planes)
            * row_total
            // (16 * total_planes)
        )
        moved = jax.vmap(
            lambda one_plane, lift_one: lax.dynamic_slice_in_dim(
                one_plane, span_pad + lift_one, row_total, 1
            )
        )(padded_cols, lifts)
        per_tilt.append(jnp.sum(moved, axis=0))
    partial_terms = jnp.stack(per_tilt) * total_planes ** (-0.5)
    projections = lax.psum_scatter(partial_terms, "gz", scatter_dimension=0, tiled=True)
    returning = rotated_cols.reshape(plane_count, col_local, groups, row_local)
    returning = jnp.transpose(returning, (2, 3, 1, 0)).reshape(
        groups, 1, row_local * col_local * plane_count
    )
    landed = lax.all_to_all(returning, "gy", split_axis=0, concat_axis=1, tiled=True)
    landed = landed.reshape(groups, row_local, col_local, plane_count)
    rotated = jnp.transpose(landed, (3, 1, 0, 2)).reshape(
        plane_count, row_local, groups * col_local
    )
    return (rotated, projections)


def swap(value, axis, step):
    return lax.ppermute(value, axis, [(i, i ^ step) for i in range(lax.axis_size(axis))])


def local(volume, x_offsets, x_fracs, z_offsets, z_fracs, y_offsets, y_fracs, slopes):
    depth = TAPS // 2 + OFFZ
    plane_count, row_local, width_all = volume.shape
    groups, shares = lax.axis_size("gy"), lax.axis_size("gz")
    assert row_local == 1 and width_all % LANES == 0
    rows = width_all // LANES
    col_local = width_all // groups
    place = lax.axis_index("gz").astype(jnp.int32)
    first_plane = place * plane_count
    chips = groups // 2
    even = chips % 4 == 0 and groups & (groups - 1) == 0 and shares & (shares - 1) == 0
    wide = even and col_local % LANES == 0 and col_local > LANES and slopes.shape[0] % shares == 0
    sheared = shear_x(
        volume.reshape(plane_count, rows, LANES), x_offsets, x_fracs,
        col_local // LANES if wide else 1, 2 if wide else 1,
    )
    if not wide:
        return narrow_local(
            sheared[0].reshape(volume.shape), first_plane, z_offsets, z_fracs, y_offsets, y_fracs,
            slopes,
        )
    mixing, taps, chosen = weights(
        z_offsets, z_fracs, slopes, y_offsets, y_fracs, plane_count, depth, groups, shares
    )
    spare = plane_count - depth
    pair_first = jnp.where(place % 2 == 0, spare, 0)
    ends = [[], []]
    for i in range(shares - 1):
        ends[i % 2] += [(i, i + 1), (i + 1, i)]
    columns = [None] * groups
    for half, value in zip((1, 0), sheared):
        pair, other = (
            lax.ppermute(lax.dynamic_slice_in_dim(value, first, depth, 0), "gz", ends[parity])
            for parity, first in ((0, pair_first), (1, spare - pair_first))
        )
        mixed = shear_z(mixing, pair, value, other, chips)
        mixing, *mixed = lax.optimization_barrier((mixing, *mixed))
        for index in reversed(range(chips)):
            step = 2 * (2 * (index // 2) + half) + index % 2
            columns[step] = swap(mixed[index], "gy", step) if step else mixed[index]
    own, cross, *rotated = shear_y(taps, columns)
    direct, pairs = rotated[:2], rotated[2:]
    landed = [swap(value, "gy", 2 * step + 4) for step, value in enumerate(pairs)]
    direct = [swap(value, "gy", 2 + core) for core, value in enumerate(direct)]
    early = swap(cross, "gy", 1)
    tilted = project(chosen, (own, cross, *rotated), shares)
    tilted = [lax.all_to_all(tilted, "gz", split_axis=0, concat_axis=0, tiled=True)]
    late = [swap(value, "gy", 1) for value in collect(landed[::-1])][::-1]
    tilted, late, direct = lax.optimization_barrier((tilted, late, direct))
    placed = place_first(own, landed, plane_count)
    rotated, projections = finish(placed, early, late, direct, tilted[0], plane_count)
    return (
        rotated.reshape(plane_count, row_local, width_all),
        jnp.swapaxes(projections, 1, 2),
    )


def solution(mesh):
    return jax.shard_map(
        local,
        mesh=mesh,
        in_specs=(P("gz", "gy", None), P(), P(), P("gy"), P("gy"), P("gy"), P("gy"), P()),
        out_specs=(P("gz", "gy", None), P("gz", "gy", None)),
        check_vma=False,
    )
```

```python
import functools

import jax
import jax.numpy as jnp
from jax import lax
from jax.experimental import pallas as pl
from jax.experimental.pallas import tpu as pltpu
from jax.sharding import PartitionSpec as P

TAPS = 64
OFFX = 64
OFFZ = 4
LANES = 128
BELOW = TAPS // 2 - 1
VMEM_LIMIT = 32 * 1024 * 1024

SMEM_SPEC = pl.BlockSpec(memory_space=pltpu.SMEM)
VMEM_SPEC = pl.BlockSpec(memory_space=pltpu.VMEM)


def tap_weight(offset, fraction):
    moved = offset.astype(jnp.float32) - fraction
    inside = (offset >= 1 - TAPS // 2) & (offset <= TAPS // 2)
    value = jnp.sinc(moved) * (0.5 + 0.5 * jnp.cos(jnp.pi * moved / (TAPS // 2 + 1)))
    return jnp.where(inside, value, jnp.zeros_like(value))


def tap_weight_in_kernel(offset, fraction):
    moved = offset.astype(jnp.float32) - fraction
    inside = (offset >= 1 - TAPS // 2) & (offset <= TAPS // 2)
    angle = jnp.pi * moved
    at_zero = moved == 0.0
    sinc = jnp.where(at_zero, 1.0, jnp.sin(angle) / jnp.where(at_zero, 1.0, angle))
    window = 0.5 + 0.5 * jnp.cos(angle / (TAPS // 2 + 1))
    return jnp.where(inside, sinc * window, 0.0)


def split_high_low(value):
    high = value.astype(jnp.bfloat16)
    low = (value - high.astype(jnp.float32)).astype(jnp.bfloat16)
    return high, low


def shear_x_kernel(
    classes, shifts_hbm, fracs_hbm, planes_hbm, *rest
):
    out_refs = rest[:-7]
    margin_ref, base_ref, lines_ref, shifts_ref, fracs_ref, small_sem, plane_sem = rest[-7:]
    plane_count, rows, lanes = lines_ref.shape
    per_class = rows // classes
    before, after = 8, margin_ref.shape[1] - rows - 8
    small = [
        pltpu.make_async_copy(shifts_hbm, shifts_ref, small_sem.at[0]),
        pltpu.make_async_copy(fracs_hbm, fracs_ref, small_sem.at[1]),
    ]
    large = pltpu.make_async_copy(
        planes_hbm, margin_ref.at[:, before:before + rows, :], plane_sem.at[0]
    )
    for copy in small:
        copy.start()
    large.start()
    line = lax.broadcasted_iota(jnp.int32, (lanes, lanes), 0)
    lane = lax.broadcasted_iota(jnp.int32, (lanes, lanes), 1)
    own_side = lane <= line
    tap = (lanes - lax.broadcasted_iota(jnp.int32, (plane_count, lanes), 1)) % lanes
    lane_of_row = lax.broadcasted_iota(jnp.int32, (per_class, lanes), 1)
    first = lax.axis_index("gz") * plane_count
    margin_ref[:, 0:before, :] = jnp.zeros((plane_count, before, lanes), jnp.float32)
    margin_ref[:, before + rows:, :] = jnp.zeros((plane_count, after, lanes), jnp.float32)
    side = lax.axis_index("gy") // 2 % 2
    first_lines = (2 - 2 * side, 2 * side)
    for copy in small:
        copy.wait()
    for z in range(plane_count):
        base_ref[z:z + 1, :] = jnp.full((1, lanes), fracs_ref[first + z], jnp.float32)
    base_ref[...] = tap_weight_in_kernel(tap - BELOW, base_ref[...])

    def one_plane(z, carry):
        spread = pltpu.roll(
            jnp.broadcast_to(base_ref[pl.ds(z, 1), :], (lanes, lanes)),
            0, 1, stride=1, stride_axis=0,
        )
        own = jnp.where(own_side, spread, 0.0)
        band = jnp.concatenate([own, spread - own], axis=0)
        band = jnp.concatenate(split_high_low(band), axis=1)
        start = shifts_ref[first + z] - BELOW + before * lanes
        top = start // lanes
        back = lanes - (start - top * lanes)
        keep = lane_of_row < back
        turned = [
            pltpu.roll(margin_ref[z, pl.ds(top + i, per_class, stride=classes), :], back, 1)
            for i in range(classes + 2)
        ]
        lines = [jnp.where(keep, turned[i], turned[i + 1]) for i in range(classes + 1)]
        window = jnp.concatenate(
            [jnp.concatenate(lines[:-1], axis=0), jnp.concatenate(lines[1:], axis=0)], axis=1
        )
        window = jnp.concatenate(split_high_low(window), axis=0)
        product = jnp.dot(window, band, preferred_element_type=jnp.float32)
        product = product[:rows] + product[rows:]
        product = product[:, :lanes] + product[:, lanes:]
        if len(out_refs) == 1:
            out_refs[0][z] = product
            return carry
        lines_ref[z] = product
        quarter = rows // 4
        for out_ref, first_line in zip(out_refs, first_lines):
            for core in range(2):
                out_ref[z, core * quarter:(core + 1) * quarter, :] = lines_ref[
                    z, pl.ds(first_line + core, quarter, stride=4), :
                ]
        return carry

    large.wait()
    lax.fori_loop(0, plane_count, one_plane, 0, unroll=True)


def shear_x(volume, x_offsets, x_fracs, classes, parts):
    plane_count, rows, lanes = volume.shape
    return pl.pallas_call(
        functools.partial(shear_x_kernel, classes),
        out_shape=[
            jax.ShapeDtypeStruct((plane_count, rows // parts, lanes), jnp.float32)
        ] * parts,
        in_specs=[pl.BlockSpec(memory_space=pltpu.HBM)] * 3,
        out_specs=[VMEM_SPEC] * parts,
        scratch_shapes=[
            pltpu.VMEM((plane_count, rows + 16, lanes), jnp.float32),
            pltpu.VMEM((plane_count, lanes), jnp.float32),
            pltpu.VMEM(volume.shape, jnp.float32),
            pltpu.SMEM(x_offsets.shape, jnp.int32),
            pltpu.SMEM(x_fracs.shape, jnp.float32),
            pltpu.SemaphoreType.DMA((2,)),
            pltpu.SemaphoreType.DMA((1,)),
        ],
        compiler_params=pltpu.CompilerParams(vmem_limit_bytes=VMEM_LIMIT),
        name="shear_x",
    )(
        *(pltpu.with_memory_space_constraint(v, pltpu.HBM) for v in (x_offsets, x_fracs, volume)),
    )


def weights_kernel(
    plane_count, depth, ny, shares, shift_ref, frac_ref, slopes_ref, shifts_ref, fracs_ref,
    mixing_ref, taps_ref, chosen_ref,
):
    reach = plane_count + 2 * depth
    place = lax.axis_index("gz")
    even = place % 2 == 0
    target = lax.broadcasted_iota(jnp.int32, (plane_count, reach), 0)
    column = lax.broadcasted_iota(jnp.int32, (plane_count, reach), 1)
    pair_start = jnp.where(even, plane_count, -depth)
    other_start = jnp.where(even, -depth, plane_count)
    source = jnp.where(
        column < depth,
        column + pair_start,
        jnp.where(
            column < depth + plane_count,
            column - depth,
            column - (depth + plane_count) + other_start,
        ),
    )
    mixing_ref[...] = tap_weight_in_kernel(source - target - shift_ref[0], frac_ref[0])
    lanes = taps_ref.shape[1]
    distance = lax.broadcasted_iota(jnp.int32, (2 * ny, lanes), 0) - (ny - 1)
    for tile in range(shifts_ref.shape[1] // lanes):
        part = slice(tile * lanes, (tile + 1) * lanes)
        taps_ref[tile * 2 * ny:(tile + 1) * 2 * ny, :] = tap_weight_in_kernel(
            distance - shifts_ref[:, part], fracs_ref[:, part]
        )
    total_planes = plane_count * shares
    tilts = slopes_ref.shape[0]
    span = ny // 4
    entry = lax.broadcasted_iota(jnp.int32, chosen_ref.shape, 0)
    plane = lax.broadcasted_iota(jnp.int32, chosen_ref.shape, 1) + place * plane_count
    lift = entry // tilts - span
    tilt = entry - (lift + span) * tilts
    slope = jnp.zeros_like(tilt)
    for t in range(tilts):
        slope = jnp.where(tilt == t, slopes_ref[t], slope)
    numerator = slope * (2 * plane - total_planes) * ny
    floor_at = lift * (16 * total_planes)
    chosen = (numerator >= floor_at) & (numerator < floor_at + 16 * total_planes)
    chosen_ref[...] = jnp.where(chosen, 1.0, 0.0)


def weights(
    z_offsets, z_fracs, slopes, y_offsets, y_fracs, plane_count, depth, ny, shares
):
    width = y_offsets.shape[0]
    lifts = 2 * (ny // 4) + 1
    return pl.pallas_call(
        functools.partial(weights_kernel, plane_count, depth, ny, shares),
        out_shape=(
            jax.ShapeDtypeStruct((plane_count, plane_count + 2 * depth), jnp.float32),
            jax.ShapeDtypeStruct((width // LANES * 2 * ny, LANES), jnp.float32),
            jax.ShapeDtypeStruct((lifts * slopes.shape[0], plane_count), jnp.float32),
        ),
        in_specs=[SMEM_SPEC] * 3 + [VMEM_SPEC] * 2,
        out_specs=(VMEM_SPEC, VMEM_SPEC, VMEM_SPEC),
        compiler_params=pltpu.CompilerParams(vmem_limit_bytes=VMEM_LIMIT),
        name="weights",
    )(
        z_offsets, z_fracs, slopes,
        y_offsets.reshape(1, width), y_fracs.reshape(1, width),
    )


def shear_z_kernel(
    plane_count, depth, chips, mixing_ref, pair_ref, own_ref, other_ref, *outs
):
    lanes = own_ref.shape[1]
    rows = own_ref.shape[0] // plane_count
    half = chips // 2
    tiles = rows // chips
    pair = 2 if tiles % 2 == 0 else 1
    high, low = split_high_low(mixing_ref[...])
    mixing = jnp.concatenate(
        [jnp.concatenate([high, high], axis=1), jnp.concatenate([low, low], axis=1)], axis=0
    )
    own_row = lax.axis_index("gy")
    core, chip_pair = own_row % 2, own_row // 4
    for index, out_ref in enumerate(outs):
        first = (core ^ (index % 2)) * (rows // 2) + (chip_pair ^ (index // 2))
        for tile in range(0, tiles, pair):
            columns = []
            for i in range(tile, tile + pair):
                row = first + i * half
                columns.append(
                    jnp.concatenate(
                        [
                            pair_ref[pl.ds(row, depth, stride=rows), :],
                            own_ref[pl.ds(row, plane_count, stride=rows), :],
                            other_ref[pl.ds(row, depth, stride=rows), :],
                        ],
                        axis=0,
                    )
                )
            stack = jnp.concatenate(columns, axis=1)
            stack = jnp.concatenate(split_high_low(stack), axis=0)
            product = jnp.dot(mixing, stack, preferred_element_type=jnp.float32)
            out_ref[:, tile * lanes:(tile + pair) * lanes] = (
                product[:plane_count] + product[plane_count:]
            )


def shear_z(mixing, pair, own, other, chips):
    plane_count, rows, lanes = own.shape
    depth = pair.shape[0]
    width = rows * lanes // chips
    return pl.pallas_call(
        functools.partial(shear_z_kernel, plane_count, depth, chips),
        out_shape=[jax.ShapeDtypeStruct((plane_count, width), jnp.float32)] * chips,
        in_specs=[VMEM_SPEC] * 4,
        out_specs=[VMEM_SPEC] * chips,
        compiler_params=pltpu.CompilerParams(vmem_limit_bytes=VMEM_LIMIT),
        name="shear_z",
    )(mixing, *(value.reshape(-1, lanes) for value in (pair, own, other)))


def start_order(ny):
    return sorted(range(ny), key=lambda slot: (-(slot // 2 % 2), -(slot // 4), slot % 2, -slot))


def shear_y_kernel(ny, taps_ref, *refs):
    in_refs, out_refs = refs[:ny], refs[ny:]
    in_refs = [in_refs[start_order(ny).index(slot)] for slot in range(ny)]
    plane_count, width = in_refs[0].shape
    row = lax.axis_index("gy")
    tiles = width // LANES
    for tile in range(tiles):
        lanes = slice(tile * LANES, (tile + 1) * LANES)
        first = tile * 2 * ny + ny - 1
        for target in range(ny):
            weight = [
                jnp.broadcast_to(
                    taps_ref[pl.ds(first + (row ^ source) - (row ^ target), 1), :], (8, LANES)
                )
                for source in range(ny)
            ]
            for block in range(plane_count // 8):
                planes = slice(block * 8, (block + 1) * 8)
                value = weight[0] * in_refs[0][planes, lanes]
                for source in range(1, ny):
                    value = value + weight[source] * in_refs[source][planes, lanes]
                lines = pl.ds(block * 8 * tiles + tile, 8, stride=tiles)
                if target < 4:
                    out_refs[target][lines, :] = value
                else:
                    out_refs[target // 2 + 2][target % 2, lines, :] = value


def shear_y(taps, columns):
    ny = len(columns)
    plane_count, width = columns[0].shape
    shape = (plane_count * width // LANES, LANES)
    out_shape = [jax.ShapeDtypeStruct(shape, jnp.float32)] * 4
    out_shape += [jax.ShapeDtypeStruct((2, *shape), jnp.float32)] * (ny // 2 - 2)
    return pl.pallas_call(
        functools.partial(shear_y_kernel, ny),
        out_shape=out_shape,
        in_specs=[VMEM_SPEC] * (1 + ny),
        out_specs=[VMEM_SPEC] * len(out_shape),
        compiler_params=pltpu.CompilerParams(vmem_limit_bytes=VMEM_LIMIT),
        name="shear_y",
    )(taps, *(columns[slot] for slot in start_order(ny)))


def collect_kernel(*refs):
    count = len(refs) // 2
    for source, target in zip(refs[:count], refs[count:]):
        target[...] = source[1]


def collect(landed):
    return pl.pallas_call(
        collect_kernel,
        out_shape=[jax.ShapeDtypeStruct(v.shape[1:], jnp.float32) for v in landed],
        in_specs=[VMEM_SPEC] * len(landed),
        out_specs=[VMEM_SPEC] * len(landed),
        compiler_params=pltpu.CompilerParams(vmem_limit_bytes=VMEM_LIMIT),
        name="collect",
    )(*landed)


def project_kernel(chips, tilts, shares, chosen_ref, *refs):
    place, own_row = lax.axis_index("gz"), lax.axis_index("gy")
    in_refs, share_ref, totals_ref = refs[:chips + 2], refs[-2], refs[-1]
    ny = 2 * chips
    plane_count = chosen_ref.shape[1]
    total_planes = plane_count * shares
    span = ny // 4
    tiles = in_refs[0].shape[0] // plane_count
    lifts = 2 * span + 1
    chosen = chosen_ref[...].astype(jnp.bfloat16)
    chosen = jnp.concatenate([chosen, chosen], axis=1)

    per_tile = (ny + 2 * span) * tilts
    totals_ref[...] = jnp.zeros(totals_ref.shape, jnp.float32)
    for source in range(ny):
        if source < 4:
            ref = in_refs[source]
        else:
            ref = in_refs[source // 2 + 2].at[source % 2]
        value = jnp.concatenate(
            [ref[pl.ds(tile, plane_count, stride=tiles), :] for tile in range(tiles)], axis=1
        )
        sums = jnp.dot(
            chosen,
            jnp.concatenate(split_high_low(value), axis=0),
            preferred_element_type=jnp.float32,
        )
        row = own_row ^ source
        for l in range(lifts):
            for tile in range(tiles):
                start = pl.multiple_of(tile * per_tile + (row + 2 * span - l) * tilts, tilts)
                totals_ref[pl.ds(start, tilts), :] += sums[
                    l * tilts:(l + 1) * tilts, tile * LANES:(tile + 1) * LANES
                ]
    per_share = tilts // shares
    for step in range(shares):
        tilt = step * per_share
        for u in range(per_share):
            for tile in range(tiles):
                share_ref[step, u, :, tile * LANES:(tile + 1) * LANES] = (
                    totals_ref[
                        pl.ds(tile * per_tile + span * tilts + tilt + u, ny, stride=tilts), :
                    ]
                    * total_planes ** (-0.5)
                )


def project(chosen, rotated, shares):
    chips = len(rotated) - 2
    ny = 2 * chips
    tilts = chosen.shape[0] // (2 * (ny // 4) + 1)
    width = rotated[0].shape[0] // chosen.shape[1] * LANES
    share = jax.ShapeDtypeStruct((shares, tilts // shares, ny, width), jnp.float32)
    totals = (width // LANES * (ny + 2 * (ny // 4)) * tilts, LANES)
    return pl.pallas_call(
        functools.partial(project_kernel, chips, tilts, shares),
        out_shape=share,
        in_specs=[VMEM_SPEC] * (1 + len(rotated)),
        out_specs=VMEM_SPEC,
        scratch_shapes=[pltpu.VMEM(totals, jnp.float32)],
        compiler_params=pltpu.CompilerParams(vmem_limit_bytes=VMEM_LIMIT),
        name="project",
    )(chosen, *rotated)


def place_kernel(slots, *refs):
    rotated_ref, sems = refs[-2:]
    row = lax.axis_index("gy")
    copies = [
        pltpu.make_async_copy(
            ref if index is None else ref.at[index], rotated_ref.at[:, row ^ slot], sems.at[place]
        )
        for place, (ref, (slot, index)) in enumerate(zip(refs, slots))
    ]
    for copy in copies:
        copy.start()
    for copy in copies:
        copy.wait()


def in_columns(value, plane_count):
    return value.reshape(
        *value.shape[:-2], plane_count, value.shape[-2] // plane_count, value.shape[-1]
    )


def place_first(own, landed, plane_count):
    chips = len(landed) + 2
    slots = [(0, None)] + [(2 * step, 0) for step in range(2, chips)]
    sources = [in_columns(value, plane_count) for value in (own, *landed)]
    return pl.pallas_call(
        functools.partial(place_kernel, slots),
        out_shape=jax.ShapeDtypeStruct(
            (plane_count, 2 * chips, *sources[0].shape[-2:]), jnp.float32
        ),
        in_specs=[VMEM_SPEC] * len(slots),
        out_specs=pl.BlockSpec(memory_space=pltpu.HBM),
        scratch_shapes=[pltpu.SemaphoreType.DMA((len(slots),))],
        compiler_params=pltpu.CompilerParams(vmem_limit_bytes=VMEM_LIMIT),
        name="place_first",
    )(*sources)


def finish_kernel(slots, *refs):
    share_ref = refs[len(slots)]
    rotated_ref, projections_ref, total_ref, sems = refs[-4:]
    row = lax.axis_index("gy")
    copies = [
        pltpu.make_async_copy(ref, rotated_ref.at[:, row ^ slot], sems.at[place])
        for place, (ref, slot) in enumerate(zip(refs, slots))
    ]
    for copy in copies:
        copy.start()
    total = share_ref[0]
    for share in range(1, share_ref.shape[0]):
        total = total + share_ref[share]
    total_ref[...] = total
    copies.append(pltpu.make_async_copy(total_ref, projections_ref, sems.at[len(slots)]))
    copies[-1].start()
    for copy in copies:
        copy.wait()


def finish(placed, early, late, direct, shares, plane_count):
    chips = len(late) + 2
    slots = [1, 2, 3] + [2 * step + 1 for step in range(2, chips)]
    sources = [in_columns(value, plane_count) for value in (early, *direct, *late)]
    return pl.pallas_call(
        functools.partial(finish_kernel, slots),
        out_shape=(
            jax.ShapeDtypeStruct(placed.shape, jnp.float32),
            jax.ShapeDtypeStruct(shares.shape[1:], jnp.float32),
        ),
        in_specs=[VMEM_SPEC] * (len(slots) + 1) + [pl.BlockSpec(memory_space=pltpu.HBM)],
        out_specs=[pl.BlockSpec(memory_space=pltpu.HBM)] * 2,
        scratch_shapes=[
            pltpu.VMEM(shares.shape[1:], jnp.float32),
            pltpu.SemaphoreType.DMA((len(slots) + 1,)),
        ],
        input_output_aliases={len(slots) + 1: 0},
        compiler_params=pltpu.CompilerParams(vmem_limit_bytes=VMEM_LIMIT),
        name="finish",
    )(*sources, shares, placed)


def with_halo(value, sides, width):
    for axis, dim in sides:
        peers, length = (lax.axis_size(axis), value.shape[dim])
        up = [(i, (i + 1) % peers) for i in range(peers - 1)]
        down = [(j, i) for i, j in up]
        last = lax.slice_in_dim(value, length - width, length, axis=dim)
        first = lax.slice_in_dim(value, 0, width, axis=dim)
        before = lax.ppermute(last, axis, up)
        after = lax.ppermute(first, axis, down)
        value = jnp.concatenate([before, value, after], axis=dim)
    return value


def narrow_local(sheared_x, first_plane, z_offsets, z_fracs, y_offsets, y_fracs, slopes):
    depth = TAPS // 2 + OFFZ
    plane_count, row_local, width_all = sheared_x.shape
    groups = lax.axis_size("gy")
    col_local = width_all // groups
    extended = with_halo(sheared_x, (("gz", 0),), depth)
    plane_index = jnp.arange(plane_count, dtype=jnp.int32)[:, None]
    source_index = jnp.arange(plane_count + 2 * depth, dtype=jnp.int32)[None, :]
    mixing = tap_weight(
        (source_index - depth - plane_index)[None] - z_offsets[:, None, None],
        z_fracs[:, None, None],
    )
    blocked = extended.reshape(plane_count + 2 * depth, row_local, groups, col_local)
    outgoing = jnp.einsum("rzj,jrgc->grcz", mixing, blocked, precision=lax.Precision.HIGHEST)
    outgoing = outgoing.reshape(groups, 1, row_local * col_local * plane_count)
    arrived = lax.all_to_all(outgoing, "gy", split_axis=0, concat_axis=1, tiled=True)
    row_total = groups * row_local
    columns = arrived.reshape(row_total, col_local, plane_count)
    target_row = jnp.arange(row_total, dtype=jnp.int32)[:, None]
    source_row = jnp.arange(row_total, dtype=jnp.int32)[None, :]
    operator = tap_weight(
        (source_row - target_row)[None] - y_offsets[:, None, None], y_fracs[:, None, None]
    )
    rotated_cols = jnp.einsum("cij,jcz->zci", operator, columns, precision=lax.Precision.HIGHEST)
    span_pad = row_total // 4
    total_planes = plane_count * lax.axis_size("gz")
    global_planes = first_plane + jnp.arange(plane_count, dtype=jnp.int32)
    padded_cols = jnp.pad(rotated_cols, ((0, 0), (0, 0), (span_pad, span_pad)))
    per_tilt = []
    for tilt_index in range(slopes.shape[0]):
        lifts = (
            slopes[tilt_index]
            * (2 * global_planes - total_planes)
            * row_total
            // (16 * total_planes)
        )
        moved = jax.vmap(
            lambda one_plane, lift_one: lax.dynamic_slice_in_dim(
                one_plane, span_pad + lift_one, row_total, 1
            )
        )(padded_cols, lifts)
        per_tilt.append(jnp.sum(moved, axis=0))
    partial_terms = jnp.stack(per_tilt) * total_planes ** (-0.5)
    projections = lax.psum_scatter(partial_terms, "gz", scatter_dimension=0, tiled=True)
    returning = rotated_cols.reshape(plane_count, col_local, groups, row_local)
    returning = jnp.transpose(returning, (2, 3, 1, 0)).reshape(
        groups, 1, row_local * col_local * plane_count
    )
    landed = lax.all_to_all(returning, "gy", split_axis=0, concat_axis=1, tiled=True)
    landed = landed.reshape(groups, row_local, col_local, plane_count)
    rotated = jnp.transpose(landed, (3, 1, 0, 2)).reshape(
        plane_count, row_local, groups * col_local
    )
    return (rotated, projections)


def swap(value, axis, step):
    return lax.ppermute(value, axis, [(i, i ^ step) for i in range(lax.axis_size(axis))])


def local(volume, x_offsets, x_fracs, z_offsets, z_fracs, y_offsets, y_fracs, slopes):
    depth = TAPS // 2 + OFFZ
    plane_count, row_local, width_all = volume.shape
    groups, shares = lax.axis_size("gy"), lax.axis_size("gz")
    assert row_local == 1 and width_all % LANES == 0
    rows = width_all // LANES
    col_local = width_all // groups
    place = lax.axis_index("gz").astype(jnp.int32)
    first_plane = place * plane_count
    chips = groups // 2
    even = chips % 4 == 0 and groups & (groups - 1) == 0 and shares & (shares - 1) == 0
    wide = even and col_local % LANES == 0 and col_local > LANES and slopes.shape[0] % shares == 0
    sheared = shear_x(
        volume.reshape(plane_count, rows, LANES), x_offsets, x_fracs,
        col_local // LANES if wide else 1, 2 if wide else 1,
    )
    if not wide:
        return narrow_local(
            sheared[0].reshape(volume.shape), first_plane, z_offsets, z_fracs, y_offsets, y_fracs,
            slopes,
        )
    mixing, taps, chosen = weights(
        z_offsets, z_fracs, slopes, y_offsets, y_fracs, plane_count, depth, groups, shares
    )
    spare = plane_count - depth
    pair_first = jnp.where(place % 2 == 0, spare, 0)
    ends = [[], []]
    for i in range(shares - 1):
        ends[i % 2] += [(i, i + 1), (i + 1, i)]
    columns = [None] * groups
    for half, value in zip((1, 0), sheared):
        pair, other = (
            lax.ppermute(lax.dynamic_slice_in_dim(value, first, depth, 0), "gz", ends[parity])
            for parity, first in ((0, pair_first), (1, spare - pair_first))
        )
        mixed = shear_z(mixing, pair, value, other, chips)
        mixing, *mixed = lax.optimization_barrier((mixing, *mixed))
        for index in reversed(range(chips)):
            step = 2 * (2 * (index // 2) + half) + index % 2
            columns[step] = swap(mixed[index], "gy", step) if step else mixed[index]
    own, cross, *rotated = shear_y(taps, columns)
    direct, pairs = rotated[:2], rotated[2:]
    landed = [swap(value, "gy", 2 * step + 4) for step, value in enumerate(pairs)]
    direct = [swap(value, "gy", 2 + core) for core, value in enumerate(direct)]
    early = swap(cross, "gy", 1)
    tilted = project(chosen, (own, cross, *rotated), shares)
    tilted = [lax.all_to_all(tilted, "gz", split_axis=0, concat_axis=0, tiled=True)]
    late = [swap(value, "gy", 1) for value in collect(landed[::-1])][::-1]
    tilted, direct, late = lax.optimization_barrier((tilted, direct, late))
    placed = place_first(own, landed, plane_count)
    rotated, projections = finish(placed, early, late, direct, tilted[0], plane_count)
    return (
        rotated.reshape(plane_count, row_local, width_all),
        jnp.swapaxes(projections, 1, 2),
    )


def solution(mesh):
    return jax.shard_map(
        local,
        mesh=mesh,
        in_specs=(P("gz", "gy", None), P(), P(), P("gy"), P("gy"), P("gy"), P("gy"), P()),
        out_specs=(P("gz", "gy", None), P("gz", "gy", None)),
        check_vma=False,
    )
```
